256 devices in a mesh: tm: 64 (over y_hi, x, z), slab: 4 (over y_lo, core).
Axes of the slice: x: 4, y: 4 (y_hi: 2, y_lo: 2; y = y_hi * 2 + y_lo), z: 8, core: 2. Of those that a mesh axis runs over, the one named last changes fastest.
Arguments:
- adjoint_end: float32 [64, 32, 32, 512], P('tm', 'slab'), may hold values from -6 to 6
- forcing: float32 [64, 32, 32, 512], P('tm', 'slab'), may hold values from -0.5 to 0.5
- velocity: float32 [3, 32, 32, 512], P(None, 'slab'), may hold values from -0.1 to 0.1
- uptake: float32 [32, 32, 512], P('slab'), may hold values from 0.0005 to 0.04
Outputs:
- corrected: float32 [64, 32, 32, 512], P('tm', 'slab')
- coarse_new: float32 [64, 8, 8, 128], P('tm')
The draws below stay inside these ranges and needn't reach their ends.
All inputs are finite; a program needn't handle non-finite values.
Results may differ from the reference program's by a relative error of at most 0.00002.
Values sent between devices are 32-bit elements; how exact they have to be, the bound alone decides.
No kernel may reach another device: no remote copies, remote signals or barrier semaphores. Data moves between devices by JAX's collectives and lax.ppermute only.
A program may use at most 256 MiB of HBM per device.

```python
import math
import jax
import jax.numpy as jnp
from jax import lax

CY = 32
NX = 512
STEPS = 8
SLICES = 64
NZ = 32


def draw_forcing(key, part):
    key = jax.random.fold_in(key, 7)
    shape_all = (SLICES, NZ, CY, NX)
    rough = 0.1 * jax.random.normal(key, shape_all, jnp.float32)
    return jnp.clip(rough, -0.5, 0.5)


def level_of(key, dims, split, smallest, largest):
    loudness = 1.0
    for position, parts in split:
        heights = jax.random.uniform(jax.random.fold_in(jax.random.fold_in(key, 6), position), (parts,), jnp.float32, smallest / len(split), largest / len(split))
        loudness = loudness * jnp.repeat(jnp.exp(heights), dims[position] // parts).reshape((-1,) + (1,) * (len(dims) - 1 - position))
    return loudness


def gaussian(rng, shape, scale, bound, shards=(), held_as=jnp.bfloat16):
    drawn = jax.random.normal(rng, shape, jnp.float32) * scale
    if len(shards) > 0:
        drawn = level_of(rng, shape, shards, -0.22, 0.18) * drawn
    return jnp.clip(drawn, min=-bound, max=bound).astype(held_as)


def setup_inputs(seed: int = 0) -> dict:
    key_of = jax.random.split(jax.random.key(seed), 5)
    return {
        "adjoint_end": gaussian(key_of[0], (SLICES, NZ, CY, NX), 1.0, 6.0, ((0, 64), (1, 4)), jnp.float32),
        "forcing": draw_forcing(jax.random.fold_in(key_of[4], 71), 0),
        "velocity": jnp.clip(jax.random.uniform(key_of[2], (3, NZ, CY, NX), jnp.float32, -0.1, 0.1) * level_of(key_of[2], (3, NZ, CY, NX), ((1, 4),), -0.4, 0.0), -0.1, 0.1),
        "uptake": jnp.clip(jnp.exp(math.log(0.04) - 4.3820266 * jax.random.uniform(key_of[3], (NZ, CY, NX), jnp.float32) ** level_of(key_of[3], (NZ, CY, NX), ((0, 4),), -0.2, 0.2)), 0.0005, 0.04),
    }


diffusion_fine = 0.15
diffusion_coarse = 0.0375


def restrict(grid_field):
    shape_now = grid_field.shape
    blocked = grid_field.reshape(shape_now[0] // 4, 4, shape_now[1] // 4, 4, shape_now[2] // 4, 4)
    return jnp.mean(blocked, axis=(1, 3, 5))


def prolong(grid_field):
    return jnp.repeat(jnp.repeat(jnp.repeat(grid_field, 4, axis=0), 4, axis=1), 4, axis=2)


def fine_step(extended, velocity, uptake, source_slice):
    center = extended[1:-1]
    padded = jnp.pad(center, ((0, 0), (1, 1), (1, 1)))
    upper_z = extended[2:]
    lower_z = extended[:-2]
    upper_y = padded[:, 2:, 1:-1]
    lower_y = padded[:, :-2, 1:-1]
    upper_x = padded[:, 1:-1, 2:]
    lower_x = padded[:, 1:-1, :-2]
    spread = upper_z + lower_z + upper_y + lower_y + upper_x + lower_x - 6.0 * center
    carried = velocity[0] * (upper_z - lower_z) + velocity[1] * (upper_y - lower_y) + velocity[2] * (upper_x - lower_x)
    return center + diffusion_fine * spread + 0.5 * carried - uptake * center + source_slice


def coarse_half(coarse_field, coarse_velocity, coarse_uptake):
    padded = jnp.pad(coarse_field, 1)
    neighbours = ((padded[2:, 1:-1, 1:-1], padded[:-2, 1:-1, 1:-1]),
                  (padded[1:-1, 2:, 1:-1], padded[1:-1, :-2, 1:-1]),
                  (padded[1:-1, 1:-1, 2:], padded[1:-1, 1:-1, :-2]))
    spread = -6.0 * coarse_field
    carried = jnp.zeros_like(coarse_field)
    for axis_no in range(3):
        upper_side, lower_side = neighbours[axis_no]
        spread = spread + upper_side + lower_side
        advect = coarse_velocity[axis_no]
        carried = carried + jnp.maximum(advect, 0.0) * (upper_side - coarse_field) + jnp.minimum(advect, 0.0) * (coarse_field - lower_side)
    return coarse_field + diffusion_coarse * spread + carried - 4.0 * coarse_uptake * coarse_field


def coarse_step(coarse_field, coarse_velocity, coarse_uptake):
    halfway = coarse_half(coarse_field, coarse_velocity, coarse_uptake)
    return coarse_half(halfway, coarse_velocity, coarse_uptake)


def reference(adjoint_end, forcing, velocity, uptake):
    coarse_velocity = jnp.stack([restrict(velocity[component]) for component in range(3)])
    coarse_uptake = restrict(uptake)

    def propagate(pair):
        adjoint, source_slice = pair
        for step_no in range(STEPS):
            extended = jnp.pad(adjoint, ((1, 1), (0, 0), (0, 0)))
            adjoint = fine_step(extended, velocity, uptake, source_slice)
        return adjoint

    propagated = lax.map(propagate, (adjoint_end, forcing))

    def step_one(coarse_field):
        return coarse_step(coarse_field, coarse_velocity, coarse_uptake)

    coarse_end = jax.vmap(restrict)(adjoint_end)
    stepped_end = jax.vmap(step_one)(coarse_end)
    jumps = jax.vmap(restrict)(propagated) - stepped_end

    def sweep(inbound, jump_now):
        advanced = step_one(inbound)
        return advanced + jump_now, advanced

    final_carry, advanced_all = lax.scan(sweep, coarse_end[-1], jumps, reverse=True)
    coarse_new = advanced_all + jumps
    corrected = propagated + jax.vmap(prolong)(advanced_all - stepped_end)
    return corrected, coarse_new
```

```python
import functools

import jax
import jax.numpy as jnp
from jax import lax
from jax.experimental import pallas as pl
from jax.experimental.pallas import tpu as pltpu
from jax.sharding import PartitionSpec as P

STEPS = 8
WIDE = 4
AXES = ("tm", "slab")
DIFFUSION_FINE = 0.15
DIFFUSION_COARSE = 0.0375
HIGH = lax.Precision.HIGHEST
ANY = pl.BlockSpec(memory_space=pl.ANY)
SMEM = pl.BlockSpec(memory_space=pltpu.SMEM)
VMEM = pl.BlockSpec(memory_space=pltpu.VMEM)
PARAMS = pltpu.CompilerParams(vmem_limit_bytes=48 * 2**20)


def f32(*shape):
    return jax.ShapeDtypeStruct(shape, jnp.float32)


def pack_kernel(slab_ref, adj, force, vel, upt, chip_out, near_out, vel_out, sem):
    depth = adj.shape[0]
    slab = slab_ref[0]
    top = depth - WIDE
    odd = lax.rem(slab, 2)
    chip_first = (1 - odd) * top
    chip_inner = (1 - odd) * (top + 1)
    near_first = odd * top
    near_inner = odd * (top + 1)
    thin = WIDE - 1
    copies = []

    def add(src, dst):
        copies.append(pltpu.make_async_copy(src, dst, sem.at[len(copies)]))

    add(adj.at[pl.ds(chip_first, WIDE)], chip_out.at[pl.ds(0, WIDE)])
    add(force.at[pl.ds(chip_inner, thin)], chip_out.at[pl.ds(WIDE, thin)])
    add(upt.at[pl.ds(chip_inner, thin)], chip_out.at[pl.ds(WIDE + thin, thin)])
    for part in range(3):
        add(
            vel.at[part, pl.ds(chip_inner, thin)],
            chip_out.at[pl.ds(WIDE + (2 + part) * thin, thin)],
        )
    add(adj.at[pl.ds(near_first, WIDE)], near_out.at[pl.ds(0, WIDE)])
    add(force.at[pl.ds(near_inner, thin)], near_out.at[pl.ds(WIDE, thin)])
    add(upt.at[pl.ds(near_inner, thin)], near_out.at[pl.ds(WIDE + thin, thin)])
    for part in range(3):
        add(vel.at[part, pl.ds(near_inner, thin)], vel_out.at[pl.ds(part * thin, thin)])
    for copy in copies:
        copy.start()
    for copy in copies:
        copy.wait()


def pack(slab, adj, force, vel, upt):
    _, rows, cols = adj.shape
    thin = WIDE - 1
    return pl.pallas_call(
        pack_kernel,
        out_shape=(
            f32(WIDE + 5 * thin, rows, cols),
            f32(WIDE + 2 * thin, rows, cols),
            f32(3 * thin, rows, cols),
        ),
        in_specs=[SMEM, ANY, ANY, ANY, ANY],
        out_specs=(ANY, ANY, ANY),
        scratch_shapes=[pltpu.SemaphoreType.DMA((12,))],
        compiler_params=PARAMS,
        name="pack",
    )(slab, adj, force, vel, upt)


def averaging(cols, scale):
    fine = lax.broadcasted_iota(jnp.int32, (cols, cols // 4), 0)
    coarse = lax.broadcasted_iota(jnp.int32, (cols, cols // 4), 1)
    return jnp.where(lax.shift_right_logical(fine, 2) == coarse, scale, 0.0)


def row_sums(rows):
    coarse = lax.broadcasted_iota(jnp.int32, (rows // 4, rows), 0)
    fine = lax.broadcasted_iota(jnp.int32, (rows // 4, rows), 1)
    return jnp.where(lax.shift_right_logical(fine, 2) == coarse, 1.0, 0.0)


def restrict_summed(summed):
    count, rows, cols = summed.shape
    flat = summed.reshape(count * rows, cols)
    across = jnp.dot(flat, averaging(cols, 1.0 / 64.0), precision=HIGH)
    down = jnp.dot(row_sums(count * rows), across, precision=HIGH)
    return down.reshape(count, rows // 4, cols // 4)


def layer_sums(read, depth):
    parts = []
    for z in range(0, depth, 4):
        parts.append((read(z) + read(z + 1)) + (read(z + 2) + read(z + 3)))
    return parts


def restrict_kernel(adj, vel, upt, out):
    depth = adj.shape[0]
    parts = layer_sums(lambda z: adj[z], depth)
    for part in range(3):
        parts += layer_sums(lambda z: vel[part, z], depth)
    parts += layer_sums(lambda z: upt[z], depth)
    out[...] = restrict_summed(jnp.stack(parts))


def restrict_inputs(adj, vel, upt):
    depth, rows, cols = adj.shape
    return pl.pallas_call(
        restrict_kernel,
        out_shape=f32(5 * depth // 4, rows // 4, cols // 4),
        in_specs=[VMEM] * 3,
        out_specs=VMEM,
        compiler_params=PARAMS,
        name="restrict",
    )(adj, vel, upt)


def fine_kernel(last, steps, slab_ref, adj, force, vel, upt, *refs):
    depth, rows, cols = adj.shape
    tiles = cols // 128
    thin = WIDE - 1
    extended = depth + 2 * WIDE
    if last:
        chip_adj, near_adj, chip, near, near_vel, out, coarse = refs[:7]
        refs = refs[7:]
    else:
        chip, near, near_vel, out, chip_out, near_out = refs[:6]
        chip_adj, near_adj = chip.at[pl.ds(0, WIDE)], near.at[pl.ds(0, WIDE)]
        refs = refs[6:]
    state, force_x, vel_x, upt_x, sem, halo_sem = refs
    slab = slab_ref[0]
    odd = lax.rem(slab, 2) == 1
    has_near = jnp.logical_and(slab > 0, slab < 3)

    own = []

    def add(src, dst):
        own.append(pltpu.make_async_copy(src, dst, sem.at[len(own)]))

    for tile in range(tiles):
        add(
            adj.at[:, :, pl.ds(tile * 128, 128)],
            state.at[0, pl.ds(WIDE, depth), tile, pl.ds(8, rows)],
        )
    add(force, force_x.at[pl.ds(WIDE, depth)])
    add(upt, upt_x.at[pl.ds(WIDE, depth)])
    for part in range(3):
        add(vel.at[part], vel_x.at[part, pl.ds(WIDE, depth)])

    def halo(first, inner, adj_src, rest, rest_vel, at):
        made = []

        def add_halo(src, dst):
            made.append(pltpu.make_async_copy(src, dst, halo_sem.at[at + len(made)]))

        for tile in range(tiles):
            add_halo(
                adj_src.at[:, :, pl.ds(tile * 128, 128)],
                state.at[0, pl.ds(first, WIDE), tile, pl.ds(8, rows)],
            )
        add_halo(rest.at[pl.ds(WIDE, thin)], force_x.at[pl.ds(inner, thin)])
        add_halo(rest.at[pl.ds(WIDE + thin, thin)], upt_x.at[pl.ds(inner, thin)])
        for part in range(3):
            add_halo(rest_vel(part), vel_x.at[part, pl.ds(inner, thin)])
        return made

    low = (0, 1)
    high = (depth + WIDE, depth + WIDE)
    per_side = tiles + 5

    def chip_vel(part):
        return chip.at[pl.ds(WIDE + (2 + part) * thin, thin)]

    def far_vel(part):
        return near_vel.at[pl.ds(part * thin, thin)]

    chip_low = halo(*low, chip_adj, chip, chip_vel, 0)
    chip_high = halo(*high, chip_adj, chip, chip_vel, 0)
    near_low = halo(*low, near_adj, near, far_vel, per_side)
    near_high = halo(*high, near_adj, near, far_vel, per_side)

    def zero_state(which, first, count):
        state[which, pl.ds(first, count)] = jnp.zeros((count,) + state.shape[2:], jnp.float32)

    for which in range(2):
        for edge in (0, rows + 8):
            state[which, :, :, pl.ds(edge, 8)] = jnp.zeros((extended, tiles, 8, 128), jnp.float32)

    @pl.when(slab == 0)
    def _():
        zero_state(0, WIDE - 1, 1)
        zero_state(1, WIDE - 1, 1)

    @pl.when(slab == 3)
    def _():
        zero_state(0, depth + WIDE, 1)
        zero_state(1, depth + WIDE, 1)

    for copy in own:
        copy.start()

    def each(copies, act):
        for copy in copies:
            act(copy)

    for act in (lambda c: c.start(), lambda c: c.wait()):

        @pl.when(odd)
        def _():
            each(chip_low, act)

        @pl.when(jnp.logical_not(odd))
        def _():
            each(chip_high, act)

        @pl.when(jnp.logical_and(has_near, odd))
        def _():
            each(near_high, act)

        @pl.when(jnp.logical_and(has_near, jnp.logical_not(odd)))
        def _():
            each(near_low, act)

    for copy in own:
        copy.wait()

    lane = lax.broadcasted_iota(jnp.int32, (8, 128), 1)
    first_lane = lane == 0
    last_lane = lane == 127

    def layer(z, now, put):
        for block in range(rows // 8):
            y = 8 + 8 * block
            mid = [state[now, z, t, pl.ds(y, 8)] for t in range(tiles)]
            ahead = [pltpu.roll(m, 127, 1) for m in mid]
            behind = [pltpu.roll(m, 1, 1) for m in mid]
            zero = jnp.zeros((8, 128), jnp.float32)
            for t in range(tiles):
                xp = jnp.where(last_lane, ahead[t + 1] if t + 1 < tiles else zero, ahead[t])
                xm = jnp.where(first_lane, behind[t - 1] if t else zero, behind[t])
                zp = state[now, z + 1, t, pl.ds(y, 8)]
                zm = state[now, z - 1, t, pl.ds(y, 8)]
                yp = state[now, z, t, pl.ds(y + 1, 8)]
                ym = state[now, z, t, pl.ds(y - 1, 8)]
                at = (z, pl.ds(8 * block, 8), pl.ds(128 * t, 128))
                spread = ((zp + zm) + (yp + ym)) + (xp + xm)
                carried = (
                    vel_x[(0,) + at] * (zp - zm)
                    + vel_x[(1,) + at] * (yp - ym)
                    + vel_x[(2,) + at] * (xp - xm)
                )
                kept = ((1.0 - 6.0 * DIFFUSION_FINE) - upt_x[at]) * mid[t]
                put(block, t, (DIFFUSION_FINE * spread + 0.5 * carried) + (kept + force_x[at]))

    for step in range(1, steps + 1):
        now, later = (step - 1) % 2, step % 2
        begin = jnp.where(slab == 0, WIDE, step)
        end = jnp.where(slab == 3, depth + WIDE, extended - step)
        if step < steps:

            def body(z, carry):
                def put(block, t, value):
                    state[later, z, t, pl.ds(8 + 8 * block, 8)] = value

                layer(z, now, put)
                return carry

            lax.fori_loop(begin, end, body, 0)
        else:

            def body(z, carry):
                def put(block, t, value):
                    out[z, pl.ds(8 * block, 8), pl.ds(128 * t, 128)] = value

                layer(z + WIDE, now, put)
                return carry

            lax.fori_loop(0, depth, body, 0)
    if last:
        coarse[...] = restrict_summed(jnp.stack(layer_sums(lambda z: out[z], depth)))
    else:

        @pl.when(odd)
        def _():
            chip_out[...] = out[pl.ds(0, WIDE)]
            near_out[...] = out[pl.ds(depth - WIDE, WIDE)]

        @pl.when(jnp.logical_not(odd))
        def _():
            chip_out[...] = out[pl.ds(depth - WIDE, WIDE)]
            near_out[...] = out[pl.ds(0, WIDE)]


def fine(slab, adj, force, vel, upt, halos, last, steps):
    depth, rows, cols = adj.shape
    extended = depth + 2 * WIDE
    tiles = cols // 128
    if last:
        out_shape = (f32(depth, rows, cols), f32(depth // 4, rows // 4, cols // 4))
    else:
        out_shape = (f32(depth, rows, cols), f32(WIDE, rows, cols), f32(WIDE, rows, cols))
    return pl.pallas_call(
        functools.partial(fine_kernel, last, steps),
        out_shape=out_shape,
        in_specs=[SMEM] + [ANY] * (4 + len(halos)),
        out_specs=(VMEM,) * len(out_shape),
        scratch_shapes=[
            pltpu.VMEM((2, extended, tiles, rows + 16, 128), jnp.float32),
            pltpu.VMEM((extended, rows, cols), jnp.float32),
            pltpu.VMEM((3, extended, rows, cols), jnp.float32),
            pltpu.VMEM((extended, rows, cols), jnp.float32),
            pltpu.SemaphoreType.DMA((tiles + 5,)),
            pltpu.SemaphoreType.DMA((2 * (tiles + 5),)),
        ],
        compiler_params=PARAMS,
        name="fine_last" if last else "fine_first",
    )(slab, adj, force, vel, upt, *halos)


def half_step(field, coef):
    depth = len(field)
    stepped = []
    ahead = [pltpu.roll(c, c.shape[1] - 1, 1) for c in field]
    behind = [pltpu.roll(c, 1, 1) for c in field]
    for z in range(depth):
        c = field[z]
        total = coef[0, z] * c
        if z + 1 < depth:
            total += coef[1, z] * field[z + 1]
        if z:
            total += coef[2, z] * field[z - 1]
        other = coef[3, z] * pltpu.roll(c, c.shape[0] - 1, 0) + coef[4, z] * pltpu.roll(c, 1, 0)
        total = (total + other) + (coef[5, z] * ahead[z] + coef[6, z] * behind[z])
        stepped.append(total)
    return stepped


def place(ref, slab, own, others):
    depth = own.shape[-3]
    for flip, part in enumerate((own,) + tuple(others)):
        ref[pl.ds(lax.bitwise_xor(slab, flip) * depth, depth)] = part


def prepare_kernel(slab_ref, own, one, two, three, coef, stepped, whole):
    slab = slab_ref[0]
    depth = own.shape[0] // 5
    for flip, ref in enumerate((own, one, two, three)):
        for part in range(5):
            first = lax.bitwise_xor(slab, flip) * depth
            whole[part, pl.ds(first, depth)] = ref[pl.ds(part * depth, depth)]
    full = whole.shape[1:]
    center = (1.0 - 6.0 * DIFFUSION_COARSE) - 4.0 * whole[4]
    for dim in range(3):
        v = whole[1 + dim]
        center -= jnp.abs(v)
        place_in = lax.broadcasted_iota(jnp.int32, full, dim)
        plus = DIFFUSION_COARSE + jnp.maximum(v, 0.0)
        minus = DIFFUSION_COARSE - jnp.minimum(v, 0.0)
        coef[1 + 2 * dim] = jnp.where(place_in == full[dim] - 1, 0.0, plus)
        coef[2 + 2 * dim] = jnp.where(place_in == 0, 0.0, minus)
    coef[0] = center
    field = [whole[0, z] for z in range(full[0])]
    field = half_step(half_step(field, coef), coef)
    for z in range(full[0]):
        stepped[z] = field[z]


def prepare(slab, parts):
    depth5, rows, cols = parts[0].shape
    full = (4 * depth5 // 5, rows, cols)
    return pl.pallas_call(
        prepare_kernel,
        out_shape=(f32(7, *full), f32(*full)),
        in_specs=[SMEM] + [VMEM] * 4,
        out_specs=(VMEM, VMEM),
        scratch_shapes=[pltpu.VMEM((5,) + full, jnp.float32)],
        compiler_params=PARAMS,
        name="prepare",
    )(slab, *parts)


def start_kernel(place_ref, own, one, two, three, stepped, begun, whole):
    place(whole, place_ref[0], own[...], (one[...], two[...], three[...]))
    kept = jnp.where(place_ref[1] == 1, 0.0, 1.0)
    begun[...] = whole[...] - kept * stepped[...]


def start_sweep(where, parts, stepped):
    return pl.pallas_call(
        start_kernel,
        out_shape=(f32(*stepped.shape), f32(*stepped.shape)),
        in_specs=[SMEM] + [VMEM] * 5,
        out_specs=(VMEM, VMEM),
        compiler_params=PARAMS,
        name="start_sweep",
    )(where, *parts, stepped)


def chain_kernel(distance, coef, *refs):
    *terms, out = refs
    depth = out.shape[0]
    field = [terms[0][z] for z in range(depth)]
    for term in terms[1:]:

        def body(_, c):
            return tuple(half_step(half_step(c, coef), coef))

        field = lax.fori_loop(0, distance, body, tuple(field))
        field = [field[z] + term[z] for z in range(depth)]
    for z in range(depth):
        out[z] = field[z]


def chain(distance, coef, terms):
    return pl.pallas_call(
        functools.partial(chain_kernel, distance),
        out_shape=f32(*terms[0].shape),
        in_specs=[VMEM] * (1 + len(terms)),
        out_specs=VMEM,
        compiler_params=PARAMS,
        name="chain",
    )(coef, *terms)


def correct_kernel(slab_ref, prop, coarse_new, coarse_prop, out):
    depth, rows, cols = prop.shape
    count = depth // 4
    first = slab_ref[0] * count
    part = coarse_new[pl.ds(first, count)] - coarse_prop[pl.ds(first, count)]
    flat = part.reshape(count * rows // 4, cols // 4)
    fine = lax.broadcasted_iota(jnp.int32, (cols // 4, cols), 1)
    coarse = lax.broadcasted_iota(jnp.int32, (cols // 4, cols), 0)
    spread = jnp.where(lax.shift_right_logical(fine, 2) == coarse, 1.0, 0.0)
    across = jnp.dot(flat, spread, precision=HIGH)
    fine = lax.broadcasted_iota(jnp.int32, (count * rows, count * rows // 4), 0)
    coarse = lax.broadcasted_iota(jnp.int32, (count * rows, count * rows // 4), 1)
    spread = jnp.where(lax.shift_right_logical(fine, 2) == coarse, 1.0, 0.0)
    down = jnp.dot(spread, across, precision=HIGH).reshape(count, rows, cols)
    for z in range(depth):
        out[z] = prop[z] + down[z // 4]


def correct(slab, prop, coarse_new, coarse_prop):
    return pl.pallas_call(
        correct_kernel,
        out_shape=f32(*prop.shape),
        in_specs=[SMEM, VMEM, VMEM, VMEM],
        out_specs=VMEM,
        compiler_params=PARAMS,
        name="correct",
    )(slab, prop, coarse_new, coarse_prop)


def per_device(adjoint_end, forcing, velocity, uptake):
    adj, force = adjoint_end[0], forcing[0]
    times, slabs = lax.axis_size("tm"), lax.axis_size("slab")
    slab_no, time_no = lax.axis_index("slab"), lax.axis_index("tm")
    slab = slab_no.astype(jnp.int32).reshape(1)

    def send(array, pairs):
        route = [(t0 * slabs + s0, t1 * slabs + s1) for (t0, s0), (t1, s1) in pairs]
        return lax.ppermute(array, AXES, route)

    def flipped(array, flip):
        return send(array, [((t, s ^ flip), (t, s)) for t in range(times) for s in range(slabs)])

    def to_next_chip(array, shift=0):
        pairs = [(1, 2), (2, 1)]
        return send(
            array, [((t, a), ((t + shift) % times, b)) for t in range(times) for a, b in pairs]
        )

    def gathered(array):
        return [array] + [flipped(array, flip) for flip in (1, 2, 3)]

    chip_pack, near_pack, vel_pack = pack(slab, adj, force, velocity, uptake)
    near = to_next_chip(near_pack)
    near_vel = to_next_chip(vel_pack, times // 2)
    chip = flipped(chip_pack, 1)
    restricted = restrict_inputs(adj, velocity, uptake)
    coef, stepped = prepare(slab, gathered(restricted))

    halves = STEPS // 2
    adj, chip_send, near_send = fine(
        slab, adj, force, velocity, uptake, (chip, near, near_vel), False, halves
    )
    near_adj = to_next_chip(near_send)
    chip_adj = flipped(chip_send, 1)
    prop, coarse_part = fine(
        slab,
        adj,
        force,
        velocity,
        uptake,
        (chip_adj, near_adj, chip, near, near_vel),
        True,
        STEPS - halves,
    )
    at_end = (time_no == times - 1).astype(jnp.int32).reshape(1)
    where = jnp.concatenate([slab, at_end])
    field, coarse_prop = start_sweep(where, gathered(coarse_part), stepped)

    distance = 1
    while distance < times:
        terms = [field]
        for hops in range(distance, min(4 * distance, times), distance):
            terms.insert(
                0,
                send(
                    field, [((t + hops, s), (t, s)) for t in range(times - hops) for s in range(slabs)]
                ),
            )
        field = chain(distance, coef, terms)
        distance *= 4
    corrected = correct(slab, prop, field, coarse_prop)
    return corrected[None], field[None]


def solution(mesh):
    in_specs = (
        P("tm", "slab", None, None),
        P("tm", "slab", None, None),
        P(None, "slab", None, None),
        P("slab", None, None),
    )
    out_specs = (P("tm", "slab", None, None), P("tm", None, None, None))
    return jax.shard_map(
        per_device, mesh=mesh, in_specs=in_specs, out_specs=out_specs, check_vma=False
    )
```

```python
import functools

import jax
import jax.numpy as jnp
from jax import lax
from jax.experimental import pallas as pl
from jax.experimental.pallas import tpu as pltpu
from jax.sharding import PartitionSpec as P

STEPS = 8
WIDE = 4
THIN = WIDE - 1
DEPTH = 8
AXES = ("tm", "slab")
DIFFUSION_FINE = 0.15
DIFFUSION_COARSE = 0.0375
HIGH = lax.Precision.HIGHEST
HBM = pl.BlockSpec(memory_space=pltpu.HBM)
SMEM = pl.BlockSpec(memory_space=pltpu.SMEM)
VMEM = pl.BlockSpec(memory_space=pltpu.VMEM)
PARAMS = pltpu.CompilerParams(vmem_limit_bytes=24 * 2**20)


def f32(*shape):
    return jax.ShapeDtypeStruct(shape, jnp.float32)


def call(kernel, name, outs, in_specs, args, scratch=(), out_specs=None):
    return pl.pallas_call(
        kernel,
        out_shape=outs,
        in_specs=in_specs,
        out_specs=out_specs or ((VMEM,) * len(outs) if isinstance(outs, tuple) else VMEM),
        scratch_shapes=list(scratch),
        compiler_params=PARAMS,
        name=name,
    )(*args)


def pack_kernel(where, adj, force, vel, upt, chip_out, near_out, vel_out, sem):
    odd = lax.rem(where[0], 2)
    copies = []

    def add(src, dst):
        copies.append(pltpu.make_async_copy(src, dst, sem.at[len(copies)]))

    def z(c):
        return jnp.where(odd == 1, c, DEPTH - 1 - c)

    for i in range(WIDE):
        add(adj.at[z(DEPTH - WIDE + i)], near_out.at[i])
    for i in range(THIN):
        c = z(DEPTH - THIN + i)
        add(force.at[c], near_out.at[WIDE + i])
        add(upt.at[c], near_out.at[WIDE + THIN + i])
        for part in range(3):
            add(vel.at[part, c], vel_out.at[part * THIN + i])
    for i in range(WIDE):
        add(adj.at[z(i)], chip_out.at[i])
    for i in range(THIN):
        c = z(i)
        add(force.at[c], chip_out.at[WIDE + i])
        add(upt.at[c], chip_out.at[WIDE + THIN + i])
        for part in range(3):
            add(vel.at[part, c], chip_out.at[WIDE + (2 + part) * THIN + i])
    for copy in copies:
        copy.start()
    for copy in copies:
        copy.wait()


def pack(where, adj, force, vel, upt):
    _, rows, cols = adj.shape
    return call(
        pack_kernel,
        "pack",
        (
            f32(WIDE + 5 * THIN, rows, cols),
            f32(WIDE + 2 * THIN, rows, cols),
            f32(3 * THIN, rows, cols),
        ),
        [SMEM] + [HBM] * 4,
        (where, adj, force, vel, upt),
        [pltpu.SemaphoreType.DMA((2 * (WIDE + 5 * THIN),))],
    )


def groups_of_four(rows, cols, value):
    i = lax.broadcasted_iota(jnp.int32, (rows, cols), 0)
    j = lax.broadcasted_iota(jnp.int32, (rows, cols), 1)
    if rows > cols:
        i = lax.shift_right_logical(i, 2)
    else:
        j = lax.shift_right_logical(j, 2)
    return jnp.where(i == j, value, 0.0)


def restrict_summed(summed):
    rows, cols = summed.shape
    down = jnp.dot(groups_of_four(rows // 4, rows, 1.0), summed, precision=HIGH)
    return jnp.dot(down, groups_of_four(cols, cols // 4, 1.0 / 64.0), precision=HIGH)


def restrict_kernel(adj, vel, upt, out):
    sums = []
    for read in (
        lambda z: adj[z],
        lambda z: vel[0, z],
        lambda z: vel[1, z],
        lambda z: vel[2, z],
        lambda z: upt[z],
    ):
        for z in range(0, DEPTH, 4):
            sums.append((read(z) + read(z + 1)) + (read(z + 2) + read(z + 3)))
    stacked = jnp.concatenate(sums, axis=0)
    out[...] = restrict_summed(stacked).reshape(out.shape)


def restrict_inputs(adj, vel, upt):
    depth, rows, cols = adj.shape
    return call(
        restrict_kernel,
        "restrict",
        f32(5 * depth // 4, rows // 4, cols // 4),
        [VMEM] * 3,
        (adj, vel, upt),
    )


def layer_step(state, now, i, coefs, sign, put):
    tiles, rows = state.shape[2], state.shape[3] - 16
    lane = lax.broadcasted_iota(jnp.int32, (8, 128), 1)
    first_lane, last_lane = lane == 0, lane == 127
    zero = jnp.zeros((8, 128), jnp.float32)
    for block in range(rows // 8):
        y = 8 + 8 * block
        mid = [state[now, i, t, pl.ds(y, 8)] for t in range(tiles)]
        ahead = [pltpu.roll(m, 127, 1) for m in mid]
        behind = [pltpu.roll(m, 1, 1) for m in mid]
        for t in range(tiles):
            xp = jnp.where(last_lane, ahead[t + 1] if t + 1 < tiles else zero, ahead[t])
            xm = jnp.where(first_lane, behind[t - 1] if t else zero, behind[t])
            zp = state[now, i + 1, t, pl.ds(y, 8)]
            zm = state[now, i - 1, t, pl.ds(y, 8)]
            yp = state[now, i, t, pl.ds(y + 1, 8)]
            ym = state[now, i, t, pl.ds(y - 1, 8)]
            at = (pl.ds(8 * block, 8), pl.ds(128 * t, 128))
            force, upt, vz, vy, vx = (ref[index + at] for ref, index in coefs)
            spread = ((zp + zm) + (yp + ym)) + (xp + xm)
            carried = vz * (sign * (zp - zm)) + vy * (yp - ym) + vx * (xp - xm)
            kept = ((1.0 - 6.0 * DIFFUSION_FINE) - upt) * mid[t]
            put(block, t, (DIFFUSION_FINE * spread + 0.5 * carried) + (kept + force))


def zero_pads(state):
    count, layers, tiles, rows, lanes = state.shape
    for edge in (0, rows - 8):
        state[:, :, :, pl.ds(edge, 8)] = jnp.zeros((count, layers, tiles, 8, lanes), jnp.float32)


def put_layer(state, which, i, value):
    rows = value.shape[0]
    for t in range(state.shape[2]):
        state[which, i, t, pl.ds(8, rows)] = value[:, 128 * t : 128 * (t + 1)]


def own_coefs(odd, force, vel, upt, c):
    z = jnp.where(odd == 1, c, DEPTH - 1 - c)
    return [(force, (z,)), (upt, (z,)), (vel, (0, z)), (vel, (1, z)), (vel, (2, z))]


def inner_kernel(last, where, force, vel, upt, chip_part, near_part, halo, chip, *refs):
    if last:
        edge, out, coarse, state = refs
    else:
        edge, out, state = refs
    odd = lax.rem(where[0], 2)
    sign = jnp.where(odd == 1, 1.0, -1.0)
    zero_pads(state)
    for h in range(1, WIDE + 1):
        put_layer(state, 0, WIDE - h, halo[h - 1])
    for c in range(DEPTH):
        value = chip_part[c] if c < WIDE else near_part[c - WIDE]
        put_layer(state, 0, WIDE + c, value)
        if c >= DEPTH - 2:
            edge[0, c - (DEPTH - 2)] = value
    for step in range(1, WIDE + 1):
        now, later = (step - 1) % 2, step % 2
        for c in range(step - WIDE, DEPTH - step):
            if c < 0:
                i = -c - 1
                coefs = [(chip, (WIDE + part * THIN + i,)) for part in range(5)]
            else:
                coefs = own_coefs(odd, force, vel, upt, c)

            def put(block, t, value, c=c, step=step, later=later):
                at = (pl.ds(8 * block, 8), pl.ds(128 * t, 128))
                if step == WIDE:
                    out[(c,) + at] = value
                    return
                state[later, WIDE + c, t, pl.ds(8 + 8 * block, 8)] = value
                if c >= DEPTH - 2 - step:
                    edge[(step, c - (DEPTH - 2 - step)) + at] = value

            layer_step(state, now, WIDE + c, coefs, sign, put)
    if last:
        coarse[...] = restrict_summed((out[0] + out[1]) + (out[2] + out[3]))


def inner(last, where, force, vel, upt, chip_part, near_part, halo, chip):
    _, rows, cols = force.shape
    outs = (f32(WIDE, 2, rows, cols), f32(WIDE, rows, cols))
    if last:
        outs += (f32(rows // 4, cols // 4),)
    return call(
        functools.partial(inner_kernel, last),
        "inner_last" if last else "inner_first",
        outs,
        [SMEM] + [VMEM] * 7,
        (where, force, vel, upt, chip_part, near_part, halo, chip),
        [pltpu.VMEM((2, DEPTH + WIDE, cols // 128, rows + 16, 128), jnp.float32)],
    )


def wedge_kernel(last, where, force, vel, upt, edge, halo, near, near_vel, *refs):
    if last:
        coarse_chip, stepped, out, begun, coarse, state = refs
    else:
        out, state = refs
    slab = where[0]
    odd = lax.rem(slab, 2)
    sign = jnp.where(odd == 1, 1.0, -1.0)
    alive = jnp.where(jnp.logical_or(slab == 1, slab == 2), 1.0, 0.0)
    zero_pads(state)
    for h in range(1, WIDE + 1):
        put_layer(state, 0, 1 + h, halo[WIDE - h])
    for step in range(1, WIDE + 1):
        now, later = (step - 1) % 2, step % 2
        for i in range(2):
            put_layer(state, now, i, edge[step - 1, i])
        for j in range(WIDE):
            c = DEPTH - step + j
            if c < DEPTH:
                coefs = own_coefs(odd, force, vel, upt, c)
            else:
                i = THIN - 1 - (c - DEPTH)
                coefs = [(near, (WIDE + i,)), (near, (WIDE + THIN + i,))]
                coefs += [(near_vel, (part * THIN + i,)) for part in range(3)]

            def put(block, t, value, c=c, j=j, step=step, later=later):
                if c >= DEPTH:
                    value = value * alive
                if step == WIDE:
                    out[j, pl.ds(8 * block, 8), pl.ds(128 * t, 128)] = value
                else:
                    state[later, 2 + j, t, pl.ds(8 + 8 * block, 8)] = value

            layer_step(state, now, 1 + j, coefs, sign, put)
    if last:
        near_coarse = restrict_summed((out[0] + out[1]) + (out[2] + out[3]))
        chip_coarse = coarse_chip[...]
        coarse[0] = jnp.where(odd == 1, chip_coarse, near_coarse)
        coarse[1] = jnp.where(odd == 1, near_coarse, chip_coarse)
        kept = jnp.where(where[1] == 1, 0.0, 1.0)
        part = coarse[...] - kept * stepped[pl.ds(2 * slab, 2)]
        for copy in range(begun.shape[0]):
            begun[copy] = part


def wedge(last, where, force, vel, upt, edge, halo, near, near_vel, more=(), copies=0):
    _, rows, cols = force.shape
    outs = (f32(WIDE, rows, cols),)
    if last:
        outs += (f32(copies, 2, rows // 4, cols // 4), f32(2, rows // 4, cols // 4))
    return call(
        functools.partial(wedge_kernel, last),
        "wedge_last" if last else "wedge_first",
        outs,
        [SMEM] + [VMEM] * (7 + len(more)),
        (where, force, vel, upt, edge, halo, near, near_vel) + more,
        [pltpu.VMEM((2, WIDE + 2, cols // 128, rows + 16, 128), jnp.float32)],
    )


NEIGHBOURS = ((0, 0, 0), (1, 0, 0), (-1, 0, 0), (0, 1, 0), (0, -1, 0), (0, 0, 1), (0, 0, -1))
STENCIL = sorted({tuple(a + b for a, b in zip(p, q)) for p in NEIGHBOURS for q in NEIGHBOURS})


def shifted(field, offset):
    dz, dy, dx = offset
    if dz:
        field = jnp.concatenate([field[dz:], field[:dz]], axis=0)
    for axis, by in ((1, dy), (2, dx)):
        if by:
            size = field.shape[axis]
            field = pltpu.roll(field, (size - by) % size, axis)
    return field


def coarse_step(field, coef):
    depth = len(field)
    rows, cols = field[0].shape
    moved = {0: field}
    for dy in (-2, -1, 1, 2):
        moved[dy] = [pltpu.roll(c, (rows - dy) % rows, 0) for c in field]

    def part(dx, z):
        total = None
        for k, offset in enumerate(STENCIL):
            if offset[2] != dx or not 0 <= z + offset[0] < depth:
                continue
            term = coef[k, z] * moved[offset[1]][z + offset[0]]
            total = term if total is None else total + term
        return total

    sides = []
    for z in range(depth):
        sides.append([pltpu.roll(part(dx, z), (cols - dx) % cols, 1) for dx in (-2, 2, -1, 1)])
    return [part(0, z) + ((s[0] + s[1]) + (s[2] + s[3])) for z, s in enumerate(sides)]


def steps(field, coef, count):
    def body(_, layers):
        return tuple(coarse_step(coarse_step(list(layers), coef), coef))

    if count >= 2:
        field = lax.fori_loop(0, count // 2, body, tuple(field))
    if count % 2:
        field = coarse_step(list(field), coef)
    return list(field)


def prepare_kernel(where, own, one, two, three, coef, stepped, whole):
    slab = where[0]
    depth = own.shape[0] // 5
    for flip, ref in enumerate((own, one, two, three)):
        first = lax.bitwise_xor(slab, flip) * depth
        for part in range(5):
            whole[part, pl.ds(first, depth)] = ref[pl.ds(part * depth, depth)]
    full = whole.shape[1:]
    half = {NEIGHBOURS[0]: (1.0 - 6.0 * DIFFUSION_COARSE) - 4.0 * whole[4]}
    for dim in range(3):
        v = whole[1 + dim]
        half[NEIGHBOURS[0]] -= jnp.abs(v)
        at = lax.broadcasted_iota(jnp.int32, full, dim)
        plus = DIFFUSION_COARSE + jnp.maximum(v, 0.0)
        minus = DIFFUSION_COARSE - jnp.minimum(v, 0.0)
        half[NEIGHBOURS[1 + 2 * dim]] = jnp.where(at == full[dim] - 1, 0.0, plus)
        half[NEIGHBOURS[2 + 2 * dim]] = jnp.where(at == 0, 0.0, minus)
    both = {}
    for p in NEIGHBOURS:
        for q in NEIGHBOURS:
            offset = tuple(a + b for a, b in zip(p, q))
            term = half[p] * shifted(half[q], p)
            both[offset] = both[offset] + term if offset in both else term
    for k, offset in enumerate(STENCIL):
        coef[k] = shifted(both[offset], (0, 0, -offset[2]))
    field = coarse_step([whole[0, z] for z in range(full[0])], coef)
    for z in range(full[0]):
        stepped[z] = field[z]


def prepare(where, parts):
    depth5, rows, cols = parts[0].shape
    full = (4 * depth5 // 5, rows, cols)
    return call(
        prepare_kernel,
        "prepare",
        (f32(len(STENCIL), *full), f32(*full)),
        [SMEM] + [VMEM] * 4,
        (where, *parts),
        [pltpu.VMEM((5,) + full, jnp.float32)],
    )


def outer_kernel(inner_count, where, coef, own, one, two, three, out, whole):
    slab, group, place = where[0], where[2], where[3]
    count, part_depth = own.shape[:2]
    depth = whole.shape[1]
    for flip, ref in enumerate((own, one, two, three)):
        first = lax.bitwise_xor(slab, flip) * part_depth
        for r in range(count):
            whole[r, pl.ds(first, part_depth)] = ref[r]

    def body(i, layers):
        r = count - 2 - i
        layers = steps(layers, coef, inner_count)
        return tuple(layers[z] + whole[r, z] for z in range(depth))

    later = jnp.where(group == count - 1, 0.0, 1.0)
    field = tuple(later * whole[count - 1, z] for z in range(depth))
    without = lax.fori_loop(0, count - 2 - group, body, field)
    stepped = steps(without, coef, inner_count)
    for z in range(depth):
        with_own = stepped[z] + whole[group, z]
        for target in range(out.shape[0]):
            out[target, z] = jnp.where(place >= target, with_own, without[z])


def outer(inner_count, where, coef, parts):
    full = coef.shape[1:]
    count = parts[0].shape[0]
    return call(
        functools.partial(outer_kernel, inner_count),
        "outer",
        f32(inner_count, *full),
        [SMEM] + [VMEM] * 5,
        (where, coef, *parts),
        [pltpu.VMEM((count,) + full, jnp.float32)],
    )


def finish_kernel(where, coef, terms, coarse, chip_part, near_part, corrected, coarse_new):
    slab, place = where[0], where[3]
    odd = lax.rem(slab, 2)
    count, depth = terms.shape[:2]

    def term(j):
        return terms.at[lax.rem(place + j, count)]

    field = [term(count - 1)[z] for z in range(depth)]

    def body(i, layers):
        stepped = coarse_step(list(layers), coef)
        added = term(count - 2 - i)
        return tuple(stepped[z] + added[z] for z in range(depth))

    field = lax.fori_loop(0, count - 1, body, tuple(field))
    for z in range(depth):
        coarse_new[z] = field[z]
    part = coarse_new[pl.ds(2 * slab, 2)] - coarse[...]
    rows, cols = chip_part.shape[1:]
    flat = part.reshape(rows // 2, cols // 4)
    down = jnp.dot(groups_of_four(2 * rows, rows // 2, 1.0), flat, precision=HIGH)
    fine = jnp.dot(down, groups_of_four(cols // 4, cols, 1.0), precision=HIGH)
    lower, upper = fine[:rows], fine[rows:]
    for i in range(WIDE):
        z = jnp.where(odd == 1, i, DEPTH - 1 - i)
        corrected[z] = chip_part[i] + jnp.where(odd == 1, lower, upper)
        z = jnp.where(odd == 1, WIDE + i, DEPTH - 1 - WIDE - i)
        corrected[z] = near_part[i] + jnp.where(odd == 1, upper, lower)


def finish(where, coef, terms, coarse, chip_part, near_part):
    _, rows, cols = chip_part.shape
    return call(
        finish_kernel,
        "finish",
        (f32(DEPTH, rows, cols), f32(*terms.shape[1:])),
        [SMEM] + [VMEM] * 5,
        (where, coef, terms, coarse, chip_part, near_part),
    )


def per_device(adjoint_end, forcing, velocity, uptake):
    adj, force = adjoint_end[0], forcing[0]
    times, slabs = lax.axis_size("tm"), lax.axis_size("slab")
    slab, time = lax.axis_index("slab"), lax.axis_index("tm")
    inner_count = 8 if times >= 16 else 2
    outer_count = times // inner_count
    where = jnp.stack([slab, time == times - 1, time // inner_count, time % inner_count])
    where = where.astype(jnp.int32)

    def send(array, pairs):
        route = [(t0 * slabs + s0, t1 * slabs + s1) for (t0, s0), (t1, s1) in pairs]
        return lax.ppermute(array, AXES, route)

    def flipped(array, flip):
        return send(array, [((t, s ^ flip), (t, s)) for t in range(times) for s in range(slabs)])

    def to_next_chip(array, shift=0):
        pairs = [(1, 2), (2, 1)]
        return send(
            array, [((t, a), ((t + shift) % times, b)) for t in range(times) for a, b in pairs]
        )

    def gathered(array):
        return [array] + [flipped(array, flip) for flip in (1, 2, 3)]

    own = (force, velocity, uptake)
    chip_pack, near_pack, vel_pack = pack(where, adj, force, velocity, uptake)
    near = to_next_chip(near_pack)
    near_vel = to_next_chip(vel_pack, times // 2)
    chip = flipped(chip_pack, 1)
    edge, chip_part = inner(False, where, *own, chip_pack, near_pack, chip, chip)
    chip_halo = flipped(chip_part, 1)
    restricted = restrict_inputs(adj, velocity, uptake)
    near, near_vel, restricted, edge = lax.optimization_barrier((near, near_vel, restricted, edge))
    (near_part,) = wedge(False, where, *own, edge, near, near, near_vel)
    near_halo = to_next_chip(near_part)
    edge, chip_part, coarse_chip = inner(True, where, *own, chip_part, near_part, chip_halo, chip)
    coef, stepped = prepare(where, gathered(restricted))
    near_halo, edge, coef, stepped = lax.optimization_barrier((near_halo, edge, coef, stepped))
    near_part, begun, coarse = wedge(
        True, where, *own, edge, near_halo, near, near_vel, (coarse_chip, stepped), outer_count
    )

    across = [[g * inner_count + i for g in range(outer_count)] for i in range(inner_count)]
    within = [[g * inner_count + i for i in range(inner_count)] for g in range(outer_count)]
    begun = lax.all_to_all(begun, "tm", 0, 0, axis_index_groups=across)
    terms = outer(inner_count, where, coef, gathered(begun))
    terms = lax.all_to_all(terms, "tm", 0, 0, axis_index_groups=within)
    corrected, coarse_new = finish(where, coef, terms, coarse, chip_part, near_part)
    return corrected[None], coarse_new[None]


def solution(mesh):
    in_specs = (
        P("tm", "slab", None, None),
        P("tm", "slab", None, None),
        P(None, "slab", None, None),
        P("slab", None, None),
    )
    out_specs = (P("tm", "slab", None, None), P("tm", None, None, None))
    return jax.shard_map(
        per_device, mesh=mesh, in_specs=in_specs, out_specs=out_specs, check_vma=False
    )
```

```python
import functools

import jax
import jax.numpy as jnp
from jax import lax
from jax.experimental import pallas as pl
from jax.experimental.pallas import tpu as pltpu
from jax.sharding import PartitionSpec as P

STEPS = 8
WIDE = 4
THIN = WIDE - 1
DEPTH = 8
AXES = ("tm", "slab")
DIFFUSION_FINE = 0.15
DIFFUSION_COARSE = 0.0375
HIGH = lax.Precision.HIGHEST
HBM = pl.BlockSpec(memory_space=pltpu.HBM)
SMEM = pl.BlockSpec(memory_space=pltpu.SMEM)
VMEM = pl.BlockSpec(memory_space=pltpu.VMEM)
PARAMS = pltpu.CompilerParams(vmem_limit_bytes=24 * 2**20)


def f32(*shape):
    return jax.ShapeDtypeStruct(shape, jnp.float32)


def call(kernel, name, outs, in_specs, args, scratch=(), out_specs=None):
    return pl.pallas_call(
        kernel,
        out_shape=outs,
        in_specs=in_specs,
        out_specs=out_specs or ((VMEM,) * len(outs) if isinstance(outs, tuple) else VMEM),
        scratch_shapes=list(scratch),
        compiler_params=PARAMS,
        name=name,
    )(*args)


def pack_kernel(first, counts, where, adj, force, vel, upt, *refs):
    *outs, sem = refs[-1 - len(counts) :]
    places = [out.at[i] for out, count in zip(outs, counts) for i in range(count)]
    odd = lax.rem(where[0], 2)
    copies = []

    def add(src):
        at = len(copies)
        copies.append(pltpu.make_async_copy(src, places[at], sem.at[at]))

    def z(c):
        return jnp.where(odd == 1, c, DEPTH - 1 - c)

    for i in range(WIDE):
        add(adj.at[z(first + i)])
    inner_first = first + 1 if first else 0
    layers = [z(inner_first + i) for i in range(THIN)]
    for c in layers:
        add(force.at[c])
    for c in layers:
        add(upt.at[c])
    for part in range(3):
        for c in layers:
            add(vel.at[part, c])
    for copy in copies:
        copy.start()
    for copy in copies:
        copy.wait()


def pack(first, counts, where, adj, force, vel, upt, after=()):
    _, rows, cols = adj.shape
    arrays = [pltpu.with_memory_space_constraint(x, pltpu.HBM) for x in (adj, force, vel, upt)]
    return call(
        functools.partial(pack_kernel, first, counts),
        "pack",
        tuple(f32(count, rows, cols) for count in counts),
        [SMEM] + [HBM] * (4 + len(after)),
        (where, *arrays, *after),
        [pltpu.SemaphoreType.DMA((WIDE + 5 * THIN,))],
    )


def groups_of_four(rows, cols, value):
    i = lax.broadcasted_iota(jnp.int32, (rows, cols), 0)
    j = lax.broadcasted_iota(jnp.int32, (rows, cols), 1)
    if rows > cols:
        i = lax.shift_right_logical(i, 2)
    else:
        j = lax.shift_right_logical(j, 2)
    return jnp.where(i == j, value, 0.0)


def restrict_summed(summed):
    rows, cols = summed.shape
    down = jnp.dot(groups_of_four(rows // 4, rows, 1.0), summed, precision=HIGH)
    return jnp.dot(down, groups_of_four(cols, cols // 4, 1.0 / 64.0), precision=HIGH)


def restrict_kernel(adj, vel, upt, out):
    sums = []
    for read in (
        lambda z: adj[z],
        lambda z: vel[0, z],
        lambda z: vel[1, z],
        lambda z: vel[2, z],
        lambda z: upt[z],
    ):
        for z in range(0, DEPTH, 4):
            sums.append((read(z) + read(z + 1)) + (read(z + 2) + read(z + 3)))
    stacked = jnp.concatenate(sums, axis=0)
    out[...] = restrict_summed(stacked).reshape(out.shape)


def restrict_inputs(adj, vel, upt):
    depth, rows, cols = adj.shape
    return call(
        restrict_kernel,
        "restrict",
        f32(5 * depth // 4, rows // 4, cols // 4),
        [VMEM] * 3,
        (adj, vel, upt),
    )


def layer_step(state, now, i, coefs, sign, put):
    tiles, rows = state.shape[2], state.shape[3] - 16
    lane = lax.broadcasted_iota(jnp.int32, (8, 128), 1)
    first_lane, last_lane = lane == 0, lane == 127
    zero = jnp.zeros((8, 128), jnp.float32)
    for block in range(rows // 8):
        y = 8 + 8 * block
        mid = [state[now, i, t, pl.ds(y, 8)] for t in range(tiles)]
        ahead = [pltpu.roll(m, 127, 1) for m in mid]
        behind = [pltpu.roll(m, 1, 1) for m in mid]
        for t in range(tiles):
            xp = jnp.where(last_lane, ahead[t + 1] if t + 1 < tiles else zero, ahead[t])
            xm = jnp.where(first_lane, behind[t - 1] if t else zero, behind[t])
            zp = state[now, i + 1, t, pl.ds(y, 8)]
            zm = state[now, i - 1, t, pl.ds(y, 8)]
            yp = state[now, i, t, pl.ds(y + 1, 8)]
            ym = state[now, i, t, pl.ds(y - 1, 8)]
            at = (pl.ds(8 * block, 8), pl.ds(128 * t, 128))
            force, upt, vz, vy, vx = (ref[index + at] for ref, index in coefs)
            spread = ((zp + zm) + (yp + ym)) + (xp + xm)
            carried = vz * (sign * (zp - zm)) + vy * (yp - ym) + vx * (xp - xm)
            kept = ((1.0 - 6.0 * DIFFUSION_FINE) - upt) * mid[t]
            put(block, t, (DIFFUSION_FINE * spread + 0.5 * carried) + (kept + force))


def zero_pads(state):
    count, layers, tiles, rows, lanes = state.shape
    for edge in (0, rows - 8):
        state[:, :, :, pl.ds(edge, 8)] = jnp.zeros((count, layers, tiles, 8, lanes), jnp.float32)


def put_layer(state, which, i, value):
    rows = value.shape[0]
    for t in range(state.shape[2]):
        state[which, i, t, pl.ds(8, rows)] = value[:, 128 * t : 128 * (t + 1)]


def own_coefs(odd, force, vel, upt, c):
    z = jnp.where(odd == 1, c, DEPTH - 1 - c)
    return [(force, (z,)), (upt, (z,)), (vel, (0, z)), (vel, (1, z)), (vel, (2, z))]


def inner_kernel(last, where, force, vel, upt, chip_part, near_part, halo, chip, *refs):
    if last:
        edge, out, coarse, state = refs
    else:
        edge, out, state = refs
    odd = lax.rem(where[0], 2)
    sign = jnp.where(odd == 1, 1.0, -1.0)
    zero_pads(state)
    for h in range(1, WIDE + 1):
        put_layer(state, 0, WIDE - h, halo[h - 1])
    for c in range(DEPTH):
        value = chip_part[c] if c < WIDE else near_part[c - WIDE]
        put_layer(state, 0, WIDE + c, value)
        if c >= DEPTH - 2:
            edge[0, c - (DEPTH - 2)] = value
    for step in range(1, WIDE + 1):
        now, later = (step - 1) % 2, step % 2
        for c in range(step - WIDE, DEPTH - step):
            if c < 0:
                i = -c - 1
                coefs = [(chip, (WIDE + part * THIN + i,)) for part in range(5)]
            else:
                coefs = own_coefs(odd, force, vel, upt, c)

            def put(block, t, value, c=c, step=step, later=later):
                at = (pl.ds(8 * block, 8), pl.ds(128 * t, 128))
                if step == WIDE:
                    out[(c,) + at] = value
                    return
                state[later, WIDE + c, t, pl.ds(8 + 8 * block, 8)] = value
                if c >= DEPTH - 2 - step:
                    edge[(step, c - (DEPTH - 2 - step)) + at] = value

            layer_step(state, now, WIDE + c, coefs, sign, put)
    if last:
        coarse[...] = restrict_summed((out[0] + out[1]) + (out[2] + out[3]))


def inner(last, where, force, vel, upt, chip_part, near_part, halo, chip):
    _, rows, cols = force.shape
    outs = (f32(WIDE, 2, rows, cols), f32(WIDE, rows, cols))
    if last:
        outs += (f32(rows // 4, cols // 4),)
    return call(
        functools.partial(inner_kernel, last),
        "inner_last" if last else "inner_first",
        outs,
        [SMEM] + [VMEM] * 7,
        (where, force, vel, upt, chip_part, near_part, halo, chip),
        [pltpu.VMEM((2, DEPTH + WIDE, cols // 128, rows + 16, 128), jnp.float32)],
    )


def wedge_kernel(last, where, force, vel, upt, edge, halo, near, near_vel, *refs):
    if last:
        coarse_chip, stepped, out, begun, coarse, state = refs
    else:
        out, state = refs
    slab = where[0]
    odd = lax.rem(slab, 2)
    sign = jnp.where(odd == 1, 1.0, -1.0)
    alive = jnp.where(jnp.logical_or(slab == 1, slab == 2), 1.0, 0.0)
    zero_pads(state)
    for h in range(1, WIDE + 1):
        put_layer(state, 0, 1 + h, halo[WIDE - h])
    for step in range(1, WIDE + 1):
        now, later = (step - 1) % 2, step % 2
        for i in range(2):
            put_layer(state, now, i, edge[step - 1, i])
        for j in range(WIDE):
            c = DEPTH - step + j
            if c < DEPTH:
                coefs = own_coefs(odd, force, vel, upt, c)
            else:
                i = THIN - 1 - (c - DEPTH)
                coefs = [(near, (WIDE + i,)), (near, (WIDE + THIN + i,))]
                coefs += [(near_vel, (part * THIN + i,)) for part in range(3)]

            def put(block, t, value, c=c, j=j, step=step, later=later):
                if c >= DEPTH:
                    value = value * alive
                if step == WIDE:
                    out[j, pl.ds(8 * block, 8), pl.ds(128 * t, 128)] = value
                else:
                    state[later, 2 + j, t, pl.ds(8 + 8 * block, 8)] = value

            layer_step(state, now, 1 + j, coefs, sign, put)
    if last:
        near_coarse = restrict_summed((out[0] + out[1]) + (out[2] + out[3]))
        chip_coarse = coarse_chip[...]
        coarse[0] = jnp.where(odd == 1, chip_coarse, near_coarse)
        coarse[1] = jnp.where(odd == 1, near_coarse, chip_coarse)
        kept = jnp.where(where[1] == 1, 0.0, 1.0)
        part = coarse[...] - kept * stepped[pl.ds(2 * slab, 2)]
        for copy in range(begun.shape[0]):
            begun[copy] = part


def wedge(last, where, force, vel, upt, edge, halo, near, near_vel, more=(), copies=0):
    _, rows, cols = force.shape
    outs = (f32(WIDE, rows, cols),)
    if last:
        outs += (f32(copies, 2, rows // 4, cols // 4), f32(2, rows // 4, cols // 4))
    return call(
        functools.partial(wedge_kernel, last),
        "wedge_last" if last else "wedge_first",
        outs,
        [SMEM] + [VMEM] * (7 + len(more)),
        (where, force, vel, upt, edge, halo, near, near_vel) + more,
        [pltpu.VMEM((2, WIDE + 2, cols // 128, rows + 16, 128), jnp.float32)],
    )


NEIGHBOURS = ((0, 0, 0), (1, 0, 0), (-1, 0, 0), (0, 1, 0), (0, -1, 0), (0, 0, 1), (0, 0, -1))
STENCIL = sorted({tuple(a + b for a, b in zip(p, q)) for p in NEIGHBOURS for q in NEIGHBOURS})


def shifted(field, offset):
    dz, dy, dx = offset
    if dz:
        field = jnp.concatenate([field[dz:], field[:dz]], axis=0)
    for axis, by in ((1, dy), (2, dx)):
        if by:
            size = field.shape[axis]
            field = pltpu.roll(field, (size - by) % size, axis)
    return field


def coarse_step(field, coef):
    depth = len(field)
    rows, cols = field[0].shape
    moved = {0: field}
    for dy in (-2, -1, 1, 2):
        moved[dy] = [pltpu.roll(c, (rows - dy) % rows, 0) for c in field]

    def part(dx, z):
        total = None
        for k, offset in enumerate(STENCIL):
            if offset[2] != dx or not 0 <= z + offset[0] < depth:
                continue
            term = coef[k, z] * moved[offset[1]][z + offset[0]]
            total = term if total is None else total + term
        return total

    sides = []
    for z in range(depth):
        sides.append([pltpu.roll(part(dx, z), (cols - dx) % cols, 1) for dx in (-2, 2, -1, 1)])
    return [part(0, z) + ((s[0] + s[1]) + (s[2] + s[3])) for z, s in enumerate(sides)]


def steps(field, coef, count):
    def body(_, layers):
        return tuple(coarse_step(coarse_step(list(layers), coef), coef))

    if count >= 2:
        field = lax.fori_loop(0, count // 2, body, tuple(field))
    if count % 2:
        field = coarse_step(list(field), coef)
    return list(field)


def prepare_kernel(where, own, one, pair, coef, stepped, whole):
    slab = where[0]
    size = own.shape[0]
    depth = size // 5
    parts = (own, one, pair.at[pl.ds(0, size)], pair.at[pl.ds(size, size)])
    for flip, ref in enumerate(parts):
        first = lax.bitwise_xor(slab, flip) * depth
        for part in range(5):
            whole[part, pl.ds(first, depth)] = ref[pl.ds(part * depth, depth)]
    full = whole.shape[1:]
    half = {NEIGHBOURS[0]: (1.0 - 6.0 * DIFFUSION_COARSE) - 4.0 * whole[4]}
    for dim in range(3):
        v = whole[1 + dim]
        half[NEIGHBOURS[0]] -= jnp.abs(v)
        at = lax.broadcasted_iota(jnp.int32, full, dim)
        plus = DIFFUSION_COARSE + jnp.maximum(v, 0.0)
        minus = DIFFUSION_COARSE - jnp.minimum(v, 0.0)
        half[NEIGHBOURS[1 + 2 * dim]] = jnp.where(at == full[dim] - 1, 0.0, plus)
        half[NEIGHBOURS[2 + 2 * dim]] = jnp.where(at == 0, 0.0, minus)
    both = {}
    for p in NEIGHBOURS:
        for q in NEIGHBOURS:
            offset = tuple(a + b for a, b in zip(p, q))
            term = half[p] * shifted(half[q], p)
            both[offset] = both[offset] + term if offset in both else term
    for k, offset in enumerate(STENCIL):
        coef[k] = shifted(both[offset], (0, 0, -offset[2]))
    field = coarse_step([whole[0, z] for z in range(full[0])], coef)
    for z in range(full[0]):
        stepped[z] = field[z]


def prepare(where, parts):
    depth5, rows, cols = parts[0].shape
    full = (4 * depth5 // 5, rows, cols)
    return call(
        prepare_kernel,
        "prepare",
        (f32(len(STENCIL), *full), f32(*full)),
        [SMEM] + [VMEM] * 3,
        (where, *parts),
        [pltpu.VMEM((5,) + full, jnp.float32)],
    )


def outer_kernel(inner_count, where, coef, own, one, pair, mine, *refs):
    *outs, whole = refs
    slab, group, place = where[0], where[2], where[3]
    count, part_depth = own.shape[:2]
    depth = whole.shape[1]
    parts = (own, one, pair.at[pl.ds(0, count)], pair.at[pl.ds(count, count)])
    for flip, ref in enumerate(parts):
        first = lax.bitwise_xor(slab, flip) * part_depth
        for r in range(count):
            whole[r, pl.ds(first, part_depth)] = ref[r]

    def body(i, layers):
        r = count - 2 - i
        layers = steps(layers, coef, inner_count)
        return tuple(layers[z] + whole[r, z] for z in range(depth))

    later = jnp.where(group == count - 1, 0.0, 1.0)
    field = tuple(later * whole[count - 1, z] for z in range(depth))
    without = lax.fori_loop(0, count - 2 - group, body, field)
    stepped = steps(without, coef, inner_count)
    core = lax.rem(slab, 2)
    for z in range(depth):
        with_own = stepped[z] + whole[group, z]
        mine[z] = with_own
        for out, hops in zip(outs, distances(inner_count)):
            before = jnp.where(core == 0, place >= hops, place + hops >= inner_count)
            out[z] = jnp.where(before, with_own, without[z])


def distances(count):
    return range(count // 2, 0, -1)


def outer(inner_count, where, coef, own, one, pair):
    full = coef.shape[1:]
    count = own.shape[0]
    return call(
        functools.partial(outer_kernel, inner_count),
        "outer",
        tuple(f32(*full) for _ in range(1 + inner_count // 2)),
        [SMEM] + [VMEM] * 4,
        (where, coef, own, one, pair),
        [pltpu.VMEM((count,) + full, jnp.float32)],
    )


def finish_kernel(inner_count, where, coef, mine, *refs):
    half = inner_count // 2
    here, there = refs[:half], refs[half : 2 * half]
    coarse, chip_part, near_part, corrected, coarse_new, terms = refs[2 * half :]
    slab = where[0]
    odd = lax.rem(slab, 2)
    depth = mine.shape[0]
    terms[0] = mine[...]
    for k, hops in enumerate(distances(inner_count)):
        mine_now, other_now = here[k][...], there[k][...]
        terms[hops] = jnp.where(odd == 0, mine_now, other_now)
        if hops < half:
            terms[inner_count - hops] = jnp.where(odd == 0, other_now, mine_now)

    def body(i, layers):
        stepped = coarse_step(list(layers), coef)
        return tuple(stepped[z] + terms[inner_count - 2 - i, z] for z in range(depth))

    field = tuple(terms[inner_count - 1, z] for z in range(depth))
    field = lax.fori_loop(0, inner_count - 1, body, field)
    for z in range(depth):
        coarse_new[z] = field[z]
    part = coarse_new[pl.ds(2 * slab, 2)] - coarse[...]
    rows, cols = chip_part.shape[1:]
    flat = part.reshape(rows // 2, cols // 4)
    down = jnp.dot(groups_of_four(2 * rows, rows // 2, 1.0), flat, precision=HIGH)
    fine = jnp.dot(down, groups_of_four(cols // 4, cols, 1.0), precision=HIGH)
    lower, upper = fine[:rows], fine[rows:]
    for i in range(WIDE):
        z = jnp.where(odd == 1, i, DEPTH - 1 - i)
        corrected[z] = chip_part[i] + jnp.where(odd == 1, lower, upper)
        z = jnp.where(odd == 1, WIDE + i, DEPTH - 1 - WIDE - i)
        corrected[z] = near_part[i] + jnp.where(odd == 1, upper, lower)


def finish(inner_count, where, coef, mine, here, there, coarse, chip_part, near_part):
    _, rows, cols = chip_part.shape
    args = (coef, mine, *here, *there, coarse, chip_part, near_part)
    return call(
        functools.partial(finish_kernel, inner_count),
        "finish",
        (f32(DEPTH, rows, cols), f32(*mine.shape)),
        [SMEM] + [VMEM] * len(args),
        (where, *args),
        [pltpu.VMEM((inner_count,) + mine.shape, jnp.float32)],
    )


def per_device(adjoint_end, forcing, velocity, uptake):
    adj, force = adjoint_end[0], forcing[0]
    times, slabs = lax.axis_size("tm"), lax.axis_size("slab")
    slab, time = lax.axis_index("slab"), lax.axis_index("tm")
    inner_count = 8 if times >= 16 else 2
    outer_count = times // inner_count
    where = jnp.stack([slab, time == times - 1, time // inner_count, time % inner_count])
    where = where.astype(jnp.int32)

    def send(array, pairs):
        route = [(t0 * slabs + s0, t1 * slabs + s1) for (t0, s0), (t1, s1) in pairs]
        return lax.ppermute(array, AXES, route)

    def flipped(array, flip):
        return send(array, [((t, s ^ flip), (t, s)) for t in range(times) for s in range(slabs)])

    def to_next_chip(array, shift=0):
        pairs = [(1, 2), (2, 1)]
        return send(
            array, [((t, a), ((t + shift) % times, b)) for t in range(times) for a, b in pairs]
        )

    def gathered(array):
        one = flipped(array, 1)
        return array, one, flipped(jnp.concatenate([array, one]), 2)

    def within_group(array, hops):
        pairs = []
        for t in range(times):
            group, place = divmod(t, inner_count)
            for s in range(slabs):
                if s % 2 and hops == inner_count // 2:
                    continue
                target = (place + hops if s % 2 else place - hops) % inner_count
                pairs.append(((t, s), (group * inner_count + target, s)))
        return send(array, pairs)

    own = (force, velocity, uptake)
    near_pack, vel_pack = pack(
        DEPTH - WIDE, (WIDE + 2 * THIN, 3 * THIN), where, adj, force, velocity, uptake
    )
    near = to_next_chip(near_pack)
    near_vel = to_next_chip(vel_pack, times // 2)
    (chip_pack,) = pack(
        0, (WIDE + 5 * THIN,), where, adj, force, velocity, uptake, (near_pack, vel_pack)
    )
    chip = flipped(chip_pack, 1)
    restricted = gathered(restrict_inputs(adj, velocity, uptake))
    edge, chip_part = inner(False, where, *own, chip_pack, near_pack, chip, chip)
    chip_halo = flipped(chip_part, 1)
    near, near_vel, restricted, edge = lax.optimization_barrier((near, near_vel, restricted, edge))
    (near_part,) = wedge(False, where, *own, edge, near, near, near_vel)
    near_halo = to_next_chip(near_part)
    edge, chip_part, coarse_chip = inner(True, where, *own, chip_part, near_part, chip_halo, chip)
    coef, stepped = prepare(where, restricted)
    near_halo, edge, coef, stepped = lax.optimization_barrier((near_halo, edge, coef, stepped))
    near_part, begun, coarse = wedge(
        True, where, *own, edge, near_halo, near, near_vel, (coarse_chip, stepped), outer_count
    )

    across = [[g * inner_count + i for g in range(outer_count)] for i in range(inner_count)]
    begun = lax.all_to_all(begun, "tm", 0, 0, axis_index_groups=across)
    mine, *messages = outer(inner_count, where, coef, *gathered(begun))
    here = [within_group(m, hops) for m, hops in zip(messages, distances(inner_count))]
    there = [flipped(h, 1) for h in here]
    corrected, coarse_new = finish(
        inner_count, where, coef, mine, here, there, coarse, chip_part, near_part
    )
    return corrected[None], coarse_new[None]


def solution(mesh):
    in_specs = (
        P("tm", "slab", None, None),
        P("tm", "slab", None, None),
        P(None, "slab", None, None),
        P("slab", None, None),
    )
    out_specs = (P("tm", "slab", None, None), P("tm", None, None, None))
    return jax.shard_map(
        per_device, mesh=mesh, in_specs=in_specs, out_specs=out_specs, check_vma=False
    )
```

```python
import functools

import jax
import jax.numpy as jnp
from jax import lax
from jax.experimental import pallas as pl
from jax.experimental.pallas import tpu as pltpu
from jax.sharding import PartitionSpec as P

STEPS = 8
WIDE = 4
THIN = WIDE - 1
DEPTH = 8
AXES = ("tm", "slab")
DIFFUSION_FINE = 0.15
DIFFUSION_COARSE = 0.0375
HIGH = lax.Precision.HIGHEST
HBM = pl.BlockSpec(memory_space=pltpu.HBM)
SMEM = pl.BlockSpec(memory_space=pltpu.SMEM)
VMEM = pl.BlockSpec(memory_space=pltpu.VMEM)
PARAMS = pltpu.CompilerParams(vmem_limit_bytes=24 * 2**20)


def f32(*shape):
    return jax.ShapeDtypeStruct(shape, jnp.float32)


def call(kernel, name, outs, in_specs, args, scratch=(), out_specs=None):
    return pl.pallas_call(
        kernel,
        out_shape=outs,
        in_specs=in_specs,
        out_specs=out_specs or ((VMEM,) * len(outs) if isinstance(outs, tuple) else VMEM),
        scratch_shapes=list(scratch),
        compiler_params=PARAMS,
        name=name,
    )(*args)


def pack_kernel(where, adj, force, vel, upt, near_out, vel_out, chip_out, sem):
    odd = lax.rem(where[0], 2)
    copies = []

    def add(src, dst):
        copies.append(pltpu.make_async_copy(src, dst, sem.at[len(copies)]))

    def z(c):
        return jnp.where(odd == 1, c, DEPTH - 1 - c)

    for i in range(WIDE):
        add(adj.at[z(DEPTH - WIDE + i)], near_out.at[i])
    for i in range(THIN):
        c = z(DEPTH - THIN + i)
        add(force.at[c], near_out.at[WIDE + i])
        add(upt.at[c], near_out.at[WIDE + THIN + i])
        for part in range(3):
            add(vel.at[part, c], vel_out.at[part * THIN + i])
    for i in range(WIDE):
        add(adj.at[z(i)], chip_out.at[i])
    for i in range(THIN):
        c = z(i)
        add(force.at[c], chip_out.at[WIDE + i])
        add(upt.at[c], chip_out.at[WIDE + THIN + i])
        for part in range(3):
            add(vel.at[part, c], chip_out.at[WIDE + (2 + part) * THIN + i])
    for copy in copies:
        copy.start()
    for copy in copies:
        copy.wait()


def pack(where, *arrays):
    _, rows, cols = arrays[0].shape
    arrays = [pltpu.with_memory_space_constraint(x, pltpu.HBM) for x in arrays]
    counts = (WIDE + 2 * THIN, 3 * THIN, WIDE + 5 * THIN)
    return call(
        pack_kernel,
        "pack",
        tuple(f32(count, rows, cols) for count in counts),
        [SMEM] + [HBM] * 4,
        (where, *arrays),
        [pltpu.SemaphoreType.DMA((sum(counts),))],
    )


def groups_of_four(rows, cols, value):
    i = lax.broadcasted_iota(jnp.int32, (rows, cols), 0)
    j = lax.broadcasted_iota(jnp.int32, (rows, cols), 1)
    if rows > cols:
        i = lax.shift_right_logical(i, 2)
    else:
        j = lax.shift_right_logical(j, 2)
    return jnp.where(i == j, value, 0.0)


def restrict_summed(summed):
    rows, cols = summed.shape
    down = jnp.dot(groups_of_four(rows // 4, rows, 1.0), summed, precision=HIGH)
    return jnp.dot(down, groups_of_four(cols, cols // 4, 1.0 / 64.0), precision=HIGH)


def restrict_kernel(adj, vel, upt, out):
    sums = []
    for read in (
        lambda z: adj[z],
        lambda z: vel[0, z],
        lambda z: vel[1, z],
        lambda z: vel[2, z],
        lambda z: upt[z],
    ):
        for z in range(0, DEPTH, 4):
            sums.append((read(z) + read(z + 1)) + (read(z + 2) + read(z + 3)))
    stacked = jnp.concatenate(sums, axis=0)
    out[...] = restrict_summed(stacked).reshape(out.shape)


def restrict_inputs(adj, vel, upt):
    depth, rows, cols = adj.shape
    return call(
        restrict_kernel,
        "restrict",
        f32(5 * depth // 4, rows // 4, cols // 4),
        [VMEM] * 3,
        (adj, vel, upt),
    )


def layer_step(state, now, i, coefs, sign, put):
    tiles, rows = state.shape[2], state.shape[3] - 16
    lane = lax.broadcasted_iota(jnp.int32, (8, 128), 1)
    first_lane, last_lane = lane == 0, lane == 127
    zero = jnp.zeros((8, 128), jnp.float32)
    for block in range(rows // 8):
        y = 8 + 8 * block
        mid = [state[now, i, t, pl.ds(y, 8)] for t in range(tiles)]
        ahead = [pltpu.roll(m, 127, 1) for m in mid]
        behind = [pltpu.roll(m, 1, 1) for m in mid]
        for t in range(tiles):
            xp = jnp.where(last_lane, ahead[t + 1] if t + 1 < tiles else zero, ahead[t])
            xm = jnp.where(first_lane, behind[t - 1] if t else zero, behind[t])
            zp = state[now, i + 1, t, pl.ds(y, 8)]
            zm = state[now, i - 1, t, pl.ds(y, 8)]
            yp = state[now, i, t, pl.ds(y + 1, 8)]
            ym = state[now, i, t, pl.ds(y - 1, 8)]
            at = (pl.ds(8 * block, 8), pl.ds(128 * t, 128))
            force, upt, vz, vy, vx = (ref[index + at] for ref, index in coefs)
            spread = ((zp + zm) + (yp + ym)) + (xp + xm)
            carried = vz * (sign * (zp - zm)) + vy * (yp - ym) + vx * (xp - xm)
            kept = ((1.0 - 6.0 * DIFFUSION_FINE) - upt) * mid[t]
            put(block, t, (DIFFUSION_FINE * spread + 0.5 * carried) + (kept + force))


def zero_pads(state):
    count, layers, tiles, rows, lanes = state.shape
    for edge in (0, rows - 8):
        state[:, :, :, pl.ds(edge, 8)] = jnp.zeros((count, layers, tiles, 8, lanes), jnp.float32)


def put_layer(state, which, i, value):
    rows = value.shape[0]
    for t in range(state.shape[2]):
        state[which, i, t, pl.ds(8, rows)] = value[:, 128 * t : 128 * (t + 1)]


def own_coefs(odd, force, vel, upt, c):
    z = jnp.where(odd == 1, c, DEPTH - 1 - c)
    return [(force, (z,)), (upt, (z,)), (vel, (0, z)), (vel, (1, z)), (vel, (2, z))]


def inner_kernel(last, where, force, vel, upt, chip_part, near_part, halo, chip, *refs):
    if last:
        edge, out, coarse, state = refs
    else:
        edge, out, state = refs
    odd = lax.rem(where[0], 2)
    sign = jnp.where(odd == 1, 1.0, -1.0)
    zero_pads(state)
    for h in range(1, WIDE + 1):
        put_layer(state, 0, WIDE - h, halo[h - 1])
    for c in range(DEPTH):
        value = chip_part[c] if c < WIDE else near_part[c - WIDE]
        put_layer(state, 0, WIDE + c, value)
        if c >= DEPTH - 2:
            edge[0, c - (DEPTH - 2)] = value
    for step in range(1, WIDE + 1):
        now, later = (step - 1) % 2, step % 2
        for c in range(step - WIDE, DEPTH - step):
            if c < 0:
                i = -c - 1
                coefs = [(chip, (WIDE + part * THIN + i,)) for part in range(5)]
            else:
                coefs = own_coefs(odd, force, vel, upt, c)

            def put(block, t, value, c=c, step=step, later=later):
                at = (pl.ds(8 * block, 8), pl.ds(128 * t, 128))
                if step == WIDE:
                    out[(c,) + at] = value
                    return
                state[later, WIDE + c, t, pl.ds(8 + 8 * block, 8)] = value
                if c >= DEPTH - 2 - step:
                    edge[(step, c - (DEPTH - 2 - step)) + at] = value

            layer_step(state, now, WIDE + c, coefs, sign, put)
    if last:
        coarse[...] = restrict_summed((out[0] + out[1]) + (out[2] + out[3]))


def inner(last, where, force, vel, upt, chip_part, near_part, halo, chip):
    _, rows, cols = force.shape
    outs = (f32(WIDE, 2, rows, cols), f32(WIDE, rows, cols))
    if last:
        outs += (f32(rows // 4, cols // 4),)
    return call(
        functools.partial(inner_kernel, last),
        "inner_last" if last else "inner_first",
        outs,
        [SMEM] + [VMEM] * 7,
        (where, force, vel, upt, chip_part, near_part, halo, chip),
        [pltpu.VMEM((2, DEPTH + WIDE, cols // 128, rows + 16, 128), jnp.float32)],
    )


def wedge_kernel(last, where, force, vel, upt, edge, halo, near, near_vel, *refs):
    if last:
        coarse_chip, stepped, out, begun, coarse, state = refs
    else:
        out, state = refs
    slab = where[0]
    odd = lax.rem(slab, 2)
    sign = jnp.where(odd == 1, 1.0, -1.0)
    alive = jnp.where(jnp.logical_or(slab == 1, slab == 2), 1.0, 0.0)
    zero_pads(state)
    for h in range(1, WIDE + 1):
        put_layer(state, 0, 1 + h, halo[WIDE - h])
    for step in range(1, WIDE + 1):
        now, later = (step - 1) % 2, step % 2
        for i in range(2):
            put_layer(state, now, i, edge[step - 1, i])
        for j in range(WIDE):
            c = DEPTH - step + j
            if c < DEPTH:
                coefs = own_coefs(odd, force, vel, upt, c)
            else:
                i = THIN - 1 - (c - DEPTH)
                coefs = [(near, (WIDE + i,)), (near, (WIDE + THIN + i,))]
                coefs += [(near_vel, (part * THIN + i,)) for part in range(3)]

            def put(block, t, value, c=c, j=j, step=step, later=later):
                if c >= DEPTH:
                    value = value * alive
                if step == WIDE:
                    out[j, pl.ds(8 * block, 8), pl.ds(128 * t, 128)] = value
                else:
                    state[later, 2 + j, t, pl.ds(8 + 8 * block, 8)] = value

            layer_step(state, now, 1 + j, coefs, sign, put)
    if last:
        near_coarse = restrict_summed((out[0] + out[1]) + (out[2] + out[3]))
        chip_coarse = coarse_chip[...]
        coarse[0] = jnp.where(odd == 1, chip_coarse, near_coarse)
        coarse[1] = jnp.where(odd == 1, near_coarse, chip_coarse)
        kept = jnp.where(where[1] == 1, 0.0, 1.0)
        part = coarse[...] - kept * stepped[pl.ds(2 * slab, 2)]
        for copy in range(begun.shape[0]):
            begun[copy] = part


def wedge(last, where, force, vel, upt, edge, halo, near, near_vel, more=(), copies=0):
    _, rows, cols = force.shape
    outs = (f32(WIDE, rows, cols),)
    if last:
        outs += (f32(copies, 2, rows // 4, cols // 4), f32(2, rows // 4, cols // 4))
    return call(
        functools.partial(wedge_kernel, last),
        "wedge_last" if last else "wedge_first",
        outs,
        [SMEM] + [VMEM] * (7 + len(more)),
        (where, force, vel, upt, edge, halo, near, near_vel) + more,
        [pltpu.VMEM((2, WIDE + 2, cols // 128, rows + 16, 128), jnp.float32)],
    )


NEIGHBOURS = ((0, 0, 0), (1, 0, 0), (-1, 0, 0), (0, 1, 0), (0, -1, 0), (0, 0, 1), (0, 0, -1))
STENCIL = sorted({tuple(a + b for a, b in zip(p, q)) for p in NEIGHBOURS for q in NEIGHBOURS})


def shifted(field, offset):
    dz, dy, dx = offset
    if dz:
        field = jnp.concatenate([field[dz:], field[:dz]], axis=0)
    for axis, by in ((1, dy), (2, dx)):
        if by:
            size = field.shape[axis]
            field = pltpu.roll(field, (size - by) % size, axis)
    return field


def coarse_step(field, coef):
    depth = len(field)
    rows, cols = field[0].shape
    moved = {0: field}
    for dy in (-2, -1, 1, 2):
        moved[dy] = [pltpu.roll(c, (rows - dy) % rows, 0) for c in field]

    def part(dx, z):
        total = None
        for k, offset in enumerate(STENCIL):
            if offset[2] != dx or not 0 <= z + offset[0] < depth:
                continue
            term = coef[k, z] * moved[offset[1]][z + offset[0]]
            total = term if total is None else total + term
        return total

    sides = []
    for z in range(depth):
        sides.append([pltpu.roll(part(dx, z), (cols - dx) % cols, 1) for dx in (-2, 2, -1, 1)])
    return [part(0, z) + ((s[0] + s[1]) + (s[2] + s[3])) for z, s in enumerate(sides)]


def steps(field, coef, count):
    def body(_, layers):
        return tuple(coarse_step(coarse_step(list(layers), coef), coef))

    if count >= 2:
        field = lax.fori_loop(0, count // 2, body, tuple(field))
    if count % 2:
        field = coarse_step(list(field), coef)
    return list(field)


def prepare_kernel(where, own, one, pair, coef, stepped, whole):
    slab = where[0]
    size = own.shape[0]
    depth = size // 5
    parts = (own, one, pair.at[pl.ds(0, size)], pair.at[pl.ds(size, size)])
    for flip, ref in enumerate(parts):
        first = lax.bitwise_xor(slab, flip) * depth
        for part in range(5):
            whole[part, pl.ds(first, depth)] = ref[pl.ds(part * depth, depth)]
    full = whole.shape[1:]
    half = {NEIGHBOURS[0]: (1.0 - 6.0 * DIFFUSION_COARSE) - 4.0 * whole[4]}
    for dim in range(3):
        v = whole[1 + dim]
        half[NEIGHBOURS[0]] -= jnp.abs(v)
        at = lax.broadcasted_iota(jnp.int32, full, dim)
        plus = DIFFUSION_COARSE + jnp.maximum(v, 0.0)
        minus = DIFFUSION_COARSE - jnp.minimum(v, 0.0)
        half[NEIGHBOURS[1 + 2 * dim]] = jnp.where(at == full[dim] - 1, 0.0, plus)
        half[NEIGHBOURS[2 + 2 * dim]] = jnp.where(at == 0, 0.0, minus)
    both = {}
    for p in NEIGHBOURS:
        for q in NEIGHBOURS:
            offset = tuple(a + b for a, b in zip(p, q))
            term = half[p] * shifted(half[q], p)
            both[offset] = both[offset] + term if offset in both else term
    for k, offset in enumerate(STENCIL):
        coef[k] = shifted(both[offset], (0, 0, -offset[2]))
    field = coarse_step([whole[0, z] for z in range(full[0])], coef)
    for z in range(full[0]):
        stepped[z] = field[z]


def prepare(where, parts):
    depth5, rows, cols = parts[0].shape
    full = (4 * depth5 // 5, rows, cols)
    return call(
        prepare_kernel,
        "prepare",
        (f32(len(STENCIL), *full), f32(*full)),
        [SMEM] + [VMEM] * 3,
        (where, *parts),
        [pltpu.VMEM((5,) + full, jnp.float32)],
    )


def within_kernel(where, coef, own, one, two, three, mine, total, whole):
    slab, place = where[0], where[3]
    count, part_depth = own.shape[:2]
    depth = whole.shape[1]
    for flip, ref in enumerate((own, one, two, three)):
        first = lax.bitwise_xor(slab, flip) * part_depth
        for t in range(count):
            whole[t, pl.ds(first, part_depth)] = ref[t]

    def keep(t, layers):
        @pl.when(t == place)
        def _():
            for z in range(depth):
                mine[z] = layers[z]

    def body(i, layers):
        t = count - 2 - i
        layers = coarse_step(list(layers), coef)
        layers = tuple(layers[z] + whole[t, z] for z in range(depth))
        keep(t, layers)
        return layers

    field = tuple(whole[count - 1, z] for z in range(depth))
    keep(count - 1, field)
    field = lax.fori_loop(0, count - 1, body, field)
    for copy in range(total.shape[0]):
        for z in range(depth):
            total[copy, z] = field[z]


def within(where, coef, parts, copies):
    full = coef.shape[1:]
    count = parts[0].shape[0]
    return call(
        within_kernel,
        "within",
        (f32(*full), f32(copies, *full)),
        [SMEM] + [VMEM] * 5,
        (where, coef, *parts),
        [pltpu.VMEM((count,) + full, jnp.float32)],
    )


def finish_kernel(inner_count, where, coef, mine, totals, coarse, chip_part, near_part, *outs):
    corrected, coarse_new = outs
    slab, group, place = where[0], where[2], where[3]
    odd = lax.rem(slab, 2)
    count, depth = totals.shape[:2]

    def body(i, layers):
        layers = steps(layers, coef, inner_count)
        return tuple(layers[z] + totals[count - 2 - i, z] for z in range(depth))

    later = jnp.where(group == count - 1, 0.0, 1.0)
    field = tuple(later * totals[count - 1, z] for z in range(depth))
    field = lax.fori_loop(0, count - 2 - group, body, field)
    field = lax.fori_loop(
        0, inner_count - place, lambda _, layers: tuple(coarse_step(list(layers), coef)), field
    )
    for z in range(depth):
        coarse_new[z] = field[z] + mine[z]
    part = coarse_new[pl.ds(2 * slab, 2)] - coarse[...]
    rows, cols = chip_part.shape[1:]
    flat = part.reshape(rows // 2, cols // 4)
    down = jnp.dot(groups_of_four(2 * rows, rows // 2, 1.0), flat, precision=HIGH)
    fine = jnp.dot(down, groups_of_four(cols // 4, cols, 1.0), precision=HIGH)
    lower, upper = fine[:rows], fine[rows:]
    for i in range(WIDE):
        z = jnp.where(odd == 1, i, DEPTH - 1 - i)
        corrected[z] = chip_part[i] + jnp.where(odd == 1, lower, upper)
        z = jnp.where(odd == 1, WIDE + i, DEPTH - 1 - WIDE - i)
        corrected[z] = near_part[i] + jnp.where(odd == 1, upper, lower)


def finish(inner_count, where, *args):
    _, rows, cols = args[-1].shape
    return call(
        functools.partial(finish_kernel, inner_count),
        "finish",
        (f32(DEPTH, rows, cols), f32(*args[1].shape)),
        [SMEM] + [VMEM] * len(args),
        (where, *args),
    )


def per_device(adjoint_end, forcing, velocity, uptake):
    adj, force = adjoint_end[0], forcing[0]
    times, slabs = lax.axis_size("tm"), lax.axis_size("slab")
    slab, time = lax.axis_index("slab"), lax.axis_index("tm")
    inner_count = 8 if times >= 16 else 2
    outer_count = times // inner_count
    where = jnp.stack([slab, time == times - 1, time // inner_count, time % inner_count])
    where = where.astype(jnp.int32)

    def send(array, pairs):
        route = [(t0 * slabs + s0, t1 * slabs + s1) for (t0, s0), (t1, s1) in pairs]
        return lax.ppermute(array, AXES, route)

    def flipped(array, flip):
        return send(array, [((t, s ^ flip), (t, s)) for t in range(times) for s in range(slabs)])

    def to_next_chip(array, shift=0):
        pairs = [(1, 2), (2, 1)]
        return send(
            array, [((t, a), ((t + shift) % times, b)) for t in range(times) for a, b in pairs]
        )

    own = (force, velocity, uptake)
    near_pack, vel_pack, chip_pack = pack(where, adj, *own)
    near = to_next_chip(near_pack)
    near_vel = to_next_chip(vel_pack, times // 2)
    chip = flipped(chip_pack, 1)
    restricted = restrict_inputs(adj, velocity, uptake)
    restricted_one = flipped(restricted, 1)
    pair = flipped(jnp.concatenate([restricted, restricted_one]), 2)
    edge, chip_part = inner(False, where, *own, chip_pack, near_pack, chip, chip)
    chip_halo = flipped(chip_part, 1)
    near, near_vel, pair, edge = lax.optimization_barrier((near, near_vel, pair, edge))
    (near_part,) = wedge(False, where, *own, edge, near, near, near_vel)
    near_halo = to_next_chip(near_part)
    edge, chip_part, coarse_chip = inner(True, where, *own, chip_part, near_part, chip_halo, chip)
    coef, stepped = prepare(where, (restricted, restricted_one, pair))
    near_halo, edge, coef, stepped = lax.optimization_barrier((near_halo, edge, coef, stepped))
    near_part, begun, coarse = wedge(
        True, where, *own, edge, near_halo, near, near_vel, (coarse_chip, stepped), inner_count
    )

    groups = [[g * inner_count + i for i in range(inner_count)] for g in range(outer_count)]
    begun = lax.all_to_all(begun, "tm", 0, 0, axis_index_groups=groups)
    parts = [begun] + [flipped(begun, flip) for flip in (1, 2, 3)]
    mine, total = within(where, coef, parts, outer_count)
    groups = [list(members) for members in zip(*groups)]
    totals = lax.all_to_all(total, "tm", 0, 0, axis_index_groups=groups)
    corrected, coarse_new = finish(
        inner_count, where, coef, mine, totals, coarse, chip_part, near_part
    )
    return corrected[None], coarse_new[None]


def solution(mesh):
    in_specs = (
        P("tm", "slab", None, None),
        P("tm", "slab", None, None),
        P(None, "slab", None, None),
        P("slab", None, None),
    )
    out_specs = (P("tm", "slab", None, None), P("tm", None, None, None))
    return jax.shard_map(
        per_device, mesh=mesh, in_specs=in_specs, out_specs=out_specs, check_vma=False
    )
```

```python
import functools

import jax
import jax.numpy as jnp
from jax import lax
from jax.experimental import pallas as pl
from jax.experimental.pallas import tpu as pltpu
from jax.sharding import Mesh
from jax.sharding import PartitionSpec as P

STEPS = 8
WIDE = 4
THIN = WIDE - 1
DEPTH = 8
AXES = ("group", "place", "chip", "core")
DIFFUSION_FINE = 0.15
DIFFUSION_COARSE = 0.0375
HIGH = lax.Precision.HIGHEST
HBM = pl.BlockSpec(memory_space=pltpu.HBM)
SMEM = pl.BlockSpec(memory_space=pltpu.SMEM)
VMEM = pl.BlockSpec(memory_space=pltpu.VMEM)
PARAMS = pltpu.CompilerParams(vmem_limit_bytes=24 * 2**20)


def f32(*shape):
    return jax.ShapeDtypeStruct(shape, jnp.float32)


def call(kernel, name, outs, in_specs, args, scratch=(), out_specs=None):
    return pl.pallas_call(
        kernel,
        out_shape=outs,
        in_specs=in_specs,
        out_specs=out_specs or ((VMEM,) * len(outs) if isinstance(outs, tuple) else VMEM),
        scratch_shapes=list(scratch),
        compiler_params=PARAMS,
        name=name,
    )(*args)


def pack_kernel(where, adj, force, vel, upt, near_out, vel_out, chip_out, sem):
    odd = lax.rem(where[0], 2)
    copies = []

    def add(src, dst):
        copies.append(pltpu.make_async_copy(src, dst, sem.at[len(copies)]))

    def z(c):
        return jnp.where(odd == 1, c, DEPTH - 1 - c)

    for i in range(WIDE):
        add(adj.at[z(DEPTH - WIDE + i)], near_out.at[i])
    for i in range(THIN):
        c = z(DEPTH - THIN + i)
        add(force.at[c], near_out.at[WIDE + i])
        add(upt.at[c], near_out.at[WIDE + THIN + i])
        for part in range(3):
            add(vel.at[part, c], vel_out.at[part * THIN + i])
    for i in range(WIDE):
        add(adj.at[z(i)], chip_out.at[i])
    for i in range(THIN):
        c = z(i)
        add(force.at[c], chip_out.at[WIDE + i])
        add(upt.at[c], chip_out.at[WIDE + THIN + i])
        for part in range(3):
            add(vel.at[part, c], chip_out.at[WIDE + (2 + part) * THIN + i])
    for copy in copies:
        copy.start()
    for copy in copies:
        copy.wait()


def pack(where, *arrays):
    _, rows, cols = arrays[0].shape
    arrays = [pltpu.with_memory_space_constraint(x, pltpu.HBM) for x in arrays]
    counts = (WIDE + 2 * THIN, 3 * THIN, WIDE + 5 * THIN)
    return call(
        pack_kernel,
        "pack",
        tuple(f32(count, rows, cols) for count in counts),
        [SMEM] + [HBM] * 4,
        (where, *arrays),
        [pltpu.SemaphoreType.DMA((sum(counts),))],
    )


def groups_of_four(rows, cols, value):
    i = lax.broadcasted_iota(jnp.int32, (rows, cols), 0)
    j = lax.broadcasted_iota(jnp.int32, (rows, cols), 1)
    if rows > cols:
        i = lax.shift_right_logical(i, 2)
    else:
        j = lax.shift_right_logical(j, 2)
    return jnp.where(i == j, value, 0.0)


def restrict_summed(summed):
    rows, cols = summed.shape
    down = jnp.dot(groups_of_four(rows // 4, rows, 1.0), summed, precision=HIGH)
    return jnp.dot(down, groups_of_four(cols, cols // 4, 1.0 / 64.0), precision=HIGH)


def restrict_kernel(adj, vel, upt, out):
    sums = []
    for read in (
        lambda z: adj[z],
        lambda z: vel[0, z],
        lambda z: vel[1, z],
        lambda z: vel[2, z],
        lambda z: upt[z],
    ):
        for z in range(0, DEPTH, 4):
            sums.append((read(z) + read(z + 1)) + (read(z + 2) + read(z + 3)))
    stacked = jnp.concatenate(sums, axis=0)
    out[...] = restrict_summed(stacked).reshape(out.shape)


def restrict_inputs(adj, vel, upt):
    depth, rows, cols = adj.shape
    return call(
        restrict_kernel,
        "restrict",
        f32(5 * depth // 4, rows // 4, cols // 4),
        [VMEM] * 3,
        (adj, vel, upt),
    )


def layer_step(state, now, i, coefs, sign, put):
    tiles, rows = state.shape[2], state.shape[3] - 16
    lane = lax.broadcasted_iota(jnp.int32, (8, 128), 1)
    first_lane, last_lane = lane == 0, lane == 127
    zero = jnp.zeros((8, 128), jnp.float32)
    for block in range(rows // 8):
        y = 8 + 8 * block
        mid = [state[now, i, t, pl.ds(y, 8)] for t in range(tiles)]
        ahead = [pltpu.roll(m, 127, 1) for m in mid]
        behind = [pltpu.roll(m, 1, 1) for m in mid]
        for t in range(tiles):
            xp = jnp.where(last_lane, ahead[t + 1] if t + 1 < tiles else zero, ahead[t])
            xm = jnp.where(first_lane, behind[t - 1] if t else zero, behind[t])
            zp = state[now, i + 1, t, pl.ds(y, 8)]
            zm = state[now, i - 1, t, pl.ds(y, 8)]
            yp = state[now, i, t, pl.ds(y + 1, 8)]
            ym = state[now, i, t, pl.ds(y - 1, 8)]
            at = (pl.ds(8 * block, 8), pl.ds(128 * t, 128))
            force, upt, vz, vy, vx = (ref[index + at] for ref, index in coefs)
            spread = ((zp + zm) + (yp + ym)) + (xp + xm)
            carried = vz * (sign * (zp - zm)) + vy * (yp - ym) + vx * (xp - xm)
            kept = ((1.0 - 6.0 * DIFFUSION_FINE) - upt) * mid[t]
            put(block, t, (DIFFUSION_FINE * spread + 0.5 * carried) + (kept + force))


def zero_pads(state):
    count, layers, tiles, rows, lanes = state.shape
    for edge in (0, rows - 8):
        state[:, :, :, pl.ds(edge, 8)] = jnp.zeros((count, layers, tiles, 8, lanes), jnp.float32)


def put_layer(state, which, i, value):
    rows = value.shape[0]
    for t in range(state.shape[2]):
        state[which, i, t, pl.ds(8, rows)] = value[:, 128 * t : 128 * (t + 1)]


def own_coefs(odd, force, vel, upt, c):
    z = jnp.where(odd == 1, c, DEPTH - 1 - c)
    return [(force, (z,)), (upt, (z,)), (vel, (0, z)), (vel, (1, z)), (vel, (2, z))]


def inner_kernel(last, where, force, vel, upt, chip_part, near_part, halo, chip, *refs):
    if last:
        edge, out, coarse, state = refs
    else:
        edge, out, state = refs
    odd = lax.rem(where[0], 2)
    sign = jnp.where(odd == 1, 1.0, -1.0)
    zero_pads(state)
    for h in range(1, WIDE + 1):
        put_layer(state, 0, WIDE - h, halo[h - 1])
    for c in range(DEPTH):
        value = chip_part[c] if c < WIDE else near_part[c - WIDE]
        put_layer(state, 0, WIDE + c, value)
        if c >= DEPTH - 2:
            edge[0, c - (DEPTH - 2)] = value
    for step in range(1, WIDE + 1):
        now, later = (step - 1) % 2, step % 2
        for c in range(step - WIDE, DEPTH - step):
            if c < 0:
                i = -c - 1
                coefs = [(chip, (WIDE + part * THIN + i,)) for part in range(5)]
            else:
                coefs = own_coefs(odd, force, vel, upt, c)

            def put(block, t, value, c=c, step=step, later=later):
                at = (pl.ds(8 * block, 8), pl.ds(128 * t, 128))
                if step == WIDE:
                    out[(c,) + at] = value
                    return
                state[later, WIDE + c, t, pl.ds(8 + 8 * block, 8)] = value
                if c >= DEPTH - 2 - step:
                    edge[(step, c - (DEPTH - 2 - step)) + at] = value

            layer_step(state, now, WIDE + c, coefs, sign, put)
    if last:
        coarse[...] = restrict_summed((out[0] + out[1]) + (out[2] + out[3]))


def inner(last, where, force, vel, upt, chip_part, near_part, halo, chip):
    _, rows, cols = force.shape
    outs = (f32(WIDE, 2, rows, cols), f32(WIDE, rows, cols))
    if last:
        outs += (f32(rows // 4, cols // 4),)
    return call(
        functools.partial(inner_kernel, last),
        "inner_last" if last else "inner_first",
        outs,
        [SMEM] + [VMEM] * 7,
        (where, force, vel, upt, chip_part, near_part, halo, chip),
        [pltpu.VMEM((2, DEPTH + WIDE, cols // 128, rows + 16, 128), jnp.float32)],
    )


def wedge_kernel(last, where, force, vel, upt, edge, halo, near, near_vel, *refs):
    if last:
        coarse_chip, stepped, out, begun, coarse, state = refs
    else:
        out, state = refs
    slab = where[0]
    odd = lax.rem(slab, 2)
    sign = jnp.where(odd == 1, 1.0, -1.0)
    alive = jnp.where(jnp.logical_or(slab == 1, slab == 2), 1.0, 0.0)
    zero_pads(state)
    for h in range(1, WIDE + 1):
        put_layer(state, 0, 1 + h, halo[WIDE - h])
    for step in range(1, WIDE + 1):
        now, later = (step - 1) % 2, step % 2
        for i in range(2):
            put_layer(state, now, i, edge[step - 1, i])
        for j in range(WIDE):
            c = DEPTH - step + j
            if c < DEPTH:
                coefs = own_coefs(odd, force, vel, upt, c)
            else:
                i = THIN - 1 - (c - DEPTH)
                coefs = [(near, (WIDE + i,)), (near, (WIDE + THIN + i,))]
                coefs += [(near_vel, (part * THIN + i,)) for part in range(3)]

            def put(block, t, value, c=c, j=j, step=step, later=later):
                if c >= DEPTH:
                    value = value * alive
                if step == WIDE:
                    out[j, pl.ds(8 * block, 8), pl.ds(128 * t, 128)] = value
                else:
                    state[later, 2 + j, t, pl.ds(8 + 8 * block, 8)] = value

            layer_step(state, now, 1 + j, coefs, sign, put)
    if last:
        near_coarse = restrict_summed((out[0] + out[1]) + (out[2] + out[3]))
        chip_coarse = coarse_chip[...]
        coarse[0] = jnp.where(odd == 1, chip_coarse, near_coarse)
        coarse[1] = jnp.where(odd == 1, near_coarse, chip_coarse)
        kept = jnp.where(where[1] == 1, 0.0, 1.0)
        part = coarse[...] - kept * stepped[pl.ds(2 * slab, 2)]
        for copy in range(begun.shape[0]):
            begun[copy] = part


def wedge(last, where, force, vel, upt, edge, halo, near, near_vel, more=(), copies=0):
    _, rows, cols = force.shape
    outs = (f32(WIDE, rows, cols),)
    if last:
        outs += (f32(copies, 2, rows // 4, cols // 4), f32(2, rows // 4, cols // 4))
    return call(
        functools.partial(wedge_kernel, last),
        "wedge_last" if last else "wedge_first",
        outs,
        [SMEM] + [VMEM] * (7 + len(more)),
        (where, force, vel, upt, edge, halo, near, near_vel) + more,
        [pltpu.VMEM((2, WIDE + 2, cols // 128, rows + 16, 128), jnp.float32)],
    )


NEIGHBOURS = ((0, 0, 0), (1, 0, 0), (-1, 0, 0), (0, 1, 0), (0, -1, 0), (0, 0, 1), (0, 0, -1))
STENCIL = sorted({tuple(a + b for a, b in zip(p, q)) for p in NEIGHBOURS for q in NEIGHBOURS})


def shifted(field, offset):
    dz, dy, dx = offset
    if dz:
        field = jnp.concatenate([field[dz:], field[:dz]], axis=0)
    for axis, by in ((1, dy), (2, dx)):
        if by:
            size = field.shape[axis]
            field = pltpu.roll(field, (size - by) % size, axis)
    return field


def coarse_step(field, coef):
    depth = len(field)
    rows, cols = field[0].shape
    moved = {0: field}
    for dy in (-2, -1, 1, 2):
        moved[dy] = [pltpu.roll(c, (rows - dy) % rows, 0) for c in field]

    def part(dx, z):
        total = None
        for k, offset in enumerate(STENCIL):
            if offset[2] != dx or not 0 <= z + offset[0] < depth:
                continue
            term = coef[k, z] * moved[offset[1]][z + offset[0]]
            total = term if total is None else total + term
        return total

    sides = []
    for z in range(depth):
        sides.append([pltpu.roll(part(dx, z), (cols - dx) % cols, 1) for dx in (-2, 2, -1, 1)])
    return [part(0, z) + ((s[0] + s[1]) + (s[2] + s[3])) for z, s in enumerate(sides)]


def steps(field, coef, count):
    def body(_, layers):
        return tuple(coarse_step(coarse_step(list(layers), coef), coef))

    if count >= 2:
        field = lax.fori_loop(0, count // 2, body, tuple(field))
    if count % 2:
        field = coarse_step(list(field), coef)
    return list(field)


def prepare_kernel(where, own, one, pair, coef, stepped, whole):
    slab = where[0]
    size = own.shape[0]
    depth = size // 5
    parts = (own, one, pair.at[pl.ds(0, size)], pair.at[pl.ds(size, size)])
    for flip, ref in enumerate(parts):
        first = lax.bitwise_xor(slab, flip) * depth
        for part in range(5):
            whole[part, pl.ds(first, depth)] = ref[pl.ds(part * depth, depth)]
    full = whole.shape[1:]
    half = {NEIGHBOURS[0]: (1.0 - 6.0 * DIFFUSION_COARSE) - 4.0 * whole[4]}
    for dim in range(3):
        v = whole[1 + dim]
        half[NEIGHBOURS[0]] -= jnp.abs(v)
        at = lax.broadcasted_iota(jnp.int32, full, dim)
        plus = DIFFUSION_COARSE + jnp.maximum(v, 0.0)
        minus = DIFFUSION_COARSE - jnp.minimum(v, 0.0)
        half[NEIGHBOURS[1 + 2 * dim]] = jnp.where(at == full[dim] - 1, 0.0, plus)
        half[NEIGHBOURS[2 + 2 * dim]] = jnp.where(at == 0, 0.0, minus)
    both = {}
    for p in NEIGHBOURS:
        for q in NEIGHBOURS:
            offset = tuple(a + b for a, b in zip(p, q))
            term = half[p] * shifted(half[q], p)
            both[offset] = both[offset] + term if offset in both else term
    for k, offset in enumerate(STENCIL):
        coef[k] = shifted(both[offset], (0, 0, -offset[2]))
    field = coarse_step([whole[0, z] for z in range(full[0])], coef)
    for z in range(full[0]):
        stepped[z] = field[z]


def prepare(where, parts):
    depth5, rows, cols = parts[0].shape
    full = (4 * depth5 // 5, rows, cols)
    return call(
        prepare_kernel,
        "prepare",
        (f32(len(STENCIL), *full), f32(*full)),
        [SMEM] + [VMEM] * 3,
        (where, *parts),
        [pltpu.VMEM((5,) + full, jnp.float32)],
    )


def outer_kernel(where, coef, own, other, out, whole, ends):
    slab, group, place = where[0], where[2], where[3]
    core = lax.rem(slab, 2)
    targets, half = out.shape[:2]
    count, depth = whole.shape[:2]
    chips = own.shape[0] // count
    part = own.shape[1]
    for g in range(count):
        for chip in range(chips):
            here = 2 * chip + core
            there = 2 * chip + 1 - core
            whole[g, pl.ds(here * part, part)] = own[g * chips + chip]
            whole[g, pl.ds(there * part, part)] = other[g * chips + chip]

    def body(i, layers):
        layers = steps(layers, coef, targets)
        return tuple(layers[z] + whole[count - 2 - i, z] for z in range(depth))

    later = jnp.where(group == count - 1, 0.0, 1.0)
    field = tuple(later * whole[count - 1, z] for z in range(depth))
    without = lax.fori_loop(0, count - 2 - group, body, field)
    stepped = steps(without, coef, targets)
    for z in range(depth):
        ends[0, z] = stepped[z] + whole[group, z]
        ends[1, z] = without[z]
    for target in range(targets):
        out[target] = ends[jnp.where(place >= target, 0, 1), pl.ds(core * half, half)]


def outer(targets, where, coef, own, other):
    full = coef.shape[1:]
    depth, rows, cols = full
    count = own.shape[0] * own.shape[1] * 2 // depth
    return call(
        outer_kernel,
        "outer",
        f32(targets, depth // 2, rows, cols),
        [SMEM] + [VMEM] * 3,
        (where, coef, own, other),
        [pltpu.VMEM((count,) + full, jnp.float32), pltpu.VMEM((2,) + full, jnp.float32)],
    )


def finish_kernel(where, coef, own, other, coarse, chip_part, near_part, *refs):
    corrected, coarse_new, whole = refs
    slab, place = where[0], where[3]
    odd = lax.rem(slab, 2)
    count, depth = whole.shape[:2]
    half = depth // 2
    for t in range(count):
        whole[t, pl.ds(odd * half, half)] = own[t]
        whole[t, pl.ds((1 - odd) * half, half)] = other[t]

    def term(j):
        return whole.at[lax.rem(place + j, count)]

    def body(i, layers):
        stepped = coarse_step(list(layers), coef)
        added = term(count - 2 - i)
        return tuple(stepped[z] + added[z] for z in range(depth))

    first = term(count - 1)
    field = lax.fori_loop(0, count - 1, body, tuple(first[z] for z in range(depth)))
    for z in range(depth):
        coarse_new[z] = field[z]
    part = coarse_new[pl.ds(2 * slab, 2)] - coarse[...]
    rows, cols = chip_part.shape[1:]
    flat = part.reshape(rows // 2, cols // 4)
    down = jnp.dot(groups_of_four(2 * rows, rows // 2, 1.0), flat, precision=HIGH)
    fine = jnp.dot(down, groups_of_four(cols // 4, cols, 1.0), precision=HIGH)
    lower, upper = fine[:rows], fine[rows:]
    for i in range(WIDE):
        z = jnp.where(odd == 1, i, DEPTH - 1 - i)
        corrected[z] = chip_part[i] + jnp.where(odd == 1, lower, upper)
        z = jnp.where(odd == 1, WIDE + i, DEPTH - 1 - WIDE - i)
        corrected[z] = near_part[i] + jnp.where(odd == 1, upper, lower)


def finish(where, *args):
    _, rows, cols = args[-1].shape
    full = args[0].shape[1:]
    return call(
        finish_kernel,
        "finish",
        (f32(DEPTH, rows, cols), f32(*full)),
        [SMEM] + [VMEM] * len(args),
        (where, *args),
        [pltpu.VMEM(args[1].shape[:1] + full, jnp.float32)],
    )


def per_device(adjoint_end, forcing, velocity, uptake):
    adj, force = adjoint_end[0], forcing[0]
    groups, places, chips, cores = (lax.axis_size(axis) for axis in AXES)
    group, place, chip_no, core = (lax.axis_index(axis) for axis in AXES)
    times, slabs = groups * places, chips * cores
    slab = chip_no * cores + core
    last_slice = jnp.logical_and(group == groups - 1, place == places - 1)
    where = jnp.stack([slab, last_slice.astype(slab.dtype), group, place]).astype(jnp.int32)

    def send(array, pairs):
        route = [(t0 * slabs + s0, t1 * slabs + s1) for (t0, s0), (t1, s1) in pairs]
        return lax.ppermute(array, AXES, route)

    def flipped(array, flip):
        return send(array, [((t, s ^ flip), (t, s)) for t in range(times) for s in range(slabs)])

    def to_next_chip(array, shift=0):
        pairs = [(1, 2), (2, 1)]
        return send(
            array, [((t, a), ((t + shift) % times, b)) for t in range(times) for a, b in pairs]
        )

    own = (force, velocity, uptake)
    near_pack, vel_pack, chip_pack = pack(where, adj, *own)
    near = to_next_chip(near_pack)
    near_vel = to_next_chip(vel_pack, times // 2)
    chip = flipped(chip_pack, 1)
    restricted = restrict_inputs(adj, velocity, uptake)
    restricted_one = flipped(restricted, 1)
    pair = flipped(jnp.concatenate([restricted, restricted_one]), 2)
    edge, chip_part = inner(False, where, *own, chip_pack, near_pack, chip, chip)
    chip_halo = flipped(chip_part, 1)
    near, near_vel, pair, edge = lax.optimization_barrier((near, near_vel, pair, edge))
    (near_part,) = wedge(False, where, *own, edge, near, near, near_vel)
    near_halo = to_next_chip(near_part)
    edge, chip_part, coarse_chip = inner(True, where, *own, chip_part, near_part, chip_halo, chip)
    coef, stepped = prepare(where, (restricted, restricted_one, pair))
    near_halo, edge, coef, stepped = lax.optimization_barrier((near_halo, edge, coef, stepped))
    near_part, begun, coarse = wedge(
        True, where, *own, edge, near_halo, near, near_vel, (coarse_chip, stepped), groups * chips
    )

    begun = lax.all_to_all(begun, ("group", "chip"), 0, 0)
    terms = outer(places, where, coef, begun, flipped(begun, 1))
    terms = lax.all_to_all(terms, "place", 0, 0)
    corrected, coarse_new = finish(
        where, coef, terms, flipped(terms, 1), coarse, chip_part, near_part
    )
    return corrected[None], coarse_new[None]


def solution(mesh):
    times, slabs = mesh.devices.shape
    places = 8 if times >= 16 else 2
    shape = (times // places, places, slabs // 2, 2)
    time, slab = AXES[:2], AXES[2:]
    return jax.shard_map(
        per_device,
        mesh=Mesh(mesh.devices.reshape(shape), AXES),
        in_specs=(P(time, slab), P(time, slab), P(None, slab), P(slab)),
        out_specs=(P(time, slab), P(time)),
        check_vma=False,
    )
```

```python
import functools

import jax
import jax.numpy as jnp
from jax import lax
from jax.experimental import pallas as pl
from jax.experimental.pallas import tpu as pltpu
from jax.sharding import Mesh
from jax.sharding import PartitionSpec as P

STEPS = 8
WIDE = 4
THIN = WIDE - 1
DEPTH = 8
CHIP_COUNTS = (WIDE + THIN, 2 * THIN, 2 * THIN)
NEAR_COUNTS = (WIDE + 2 * THIN, 3 * THIN)
AXES = ("group", "place", "chip", "core")
DIFFUSION_FINE = 0.15
DIFFUSION_COARSE = 0.0375
HIGH = lax.Precision.HIGHEST
HBM = pl.BlockSpec(memory_space=pltpu.HBM)
SMEM = pl.BlockSpec(memory_space=pltpu.SMEM)
VMEM = pl.BlockSpec(memory_space=pltpu.VMEM)
PARAMS = pltpu.CompilerParams(vmem_limit_bytes=24 * 2**20)


def f32(*shape):
    return jax.ShapeDtypeStruct(shape, jnp.float32)


def call(kernel, name, outs, in_specs, args, scratch=(), out_specs=None):
    return pl.pallas_call(
        kernel,
        out_shape=outs,
        in_specs=in_specs,
        out_specs=out_specs or ((VMEM,) * len(outs) if isinstance(outs, tuple) else VMEM),
        scratch_shapes=list(scratch),
        compiler_params=PARAMS,
        name=name,
        cost_estimate=pl.CostEstimate(flops=1, bytes_accessed=1, transcendentals=0),
    )(*args)


def pack_kernel(to_chip, where, adj, force, vel, upt, *refs):
    counts = CHIP_COUNTS if to_chip else NEAR_COUNTS
    *outs, sem = refs[-1 - len(counts) :]
    places = [out.at[i] for out, count in zip(outs, counts) for i in range(count)]
    odd = lax.rem(where[0], 2)

    def z(c):
        return jnp.where(odd == 1, c, DEPTH - 1 - c)

    sources = [adj.at[z(i if to_chip else DEPTH - WIDE + i)] for i in range(WIDE)]
    layers = [z(i if to_chip else DEPTH - THIN + i) for i in range(THIN)]
    for ref in (force, upt, vel.at[0], vel.at[1], vel.at[2]):
        sources += [ref.at[c] for c in layers]
    copies = [
        pltpu.make_async_copy(src, dst, sem.at[i])
        for i, (src, dst) in enumerate(zip(sources, places))
    ]
    for copy in copies:
        copy.start()
    for copy in copies:
        copy.wait()


def pack(to_chip, where, arrays, after=()):
    _, rows, cols = arrays[0].shape
    arrays = [pltpu.with_memory_space_constraint(x, pltpu.HBM) for x in arrays]
    counts = CHIP_COUNTS if to_chip else NEAR_COUNTS
    return call(
        functools.partial(pack_kernel, to_chip),
        "pack_chip" if to_chip else "pack_near",
        tuple(f32(count, rows, cols) for count in counts),
        [SMEM] + [HBM] * (4 + len(after)),
        (where, *arrays, *after),
        [pltpu.SemaphoreType.DMA((sum(counts),))],
    )


def groups_of_four(rows, cols, value):
    i = lax.broadcasted_iota(jnp.int32, (rows, cols), 0)
    j = lax.broadcasted_iota(jnp.int32, (rows, cols), 1)
    if rows > cols:
        i = lax.shift_right_logical(i, 2)
    else:
        j = lax.shift_right_logical(j, 2)
    return jnp.where(i == j, value, 0.0)


def put_tiles(summed, first, value):
    for t in range(summed.shape[0]):
        summed[t, pl.ds(first, value.shape[0])] = value[:, 128 * t : 128 * (t + 1)]


def restrict_summed(summed):
    tiles, rows, lanes = summed.shape
    down = []
    for t in range(tiles):
        parts = [summed[t, pl.ds(k, rows // 4, 4)] for k in range(4)]
        down.append((parts[0] + parts[1]) + (parts[2] + parts[3]))
    average = groups_of_four(tiles * lanes, tiles * lanes // 4, 1.0 / 64.0)
    return jnp.dot(jnp.concatenate(down, axis=1), average, precision=HIGH)


def restrict_kernel(adj, vel, upt, out, sums):
    rows = adj.shape[1]
    count = 0
    for read in (
        lambda z: adj[z],
        lambda z: vel[0, z],
        lambda z: vel[1, z],
        lambda z: vel[2, z],
        lambda z: upt[z],
    ):
        for z in range(0, DEPTH, 4):
            put_tiles(sums, count, (read(z) + read(z + 1)) + (read(z + 2) + read(z + 3)))
            count += rows
    out[...] = restrict_summed(sums).reshape(out.shape)


def restrict_inputs(adj, vel, upt):
    depth, rows, cols = adj.shape
    return call(
        restrict_kernel,
        "restrict",
        f32(5 * depth // 4, rows // 4, cols // 4),
        [VMEM] * 3,
        (adj, vel, upt),
        [pltpu.VMEM((cols // 128, 5 * depth // 4 * rows, 128), jnp.float32)],
    )


def layer_step(state, now, i, coefs, sign, put):
    tiles, rows = state.shape[2], state.shape[3] - 16
    lane = lax.broadcasted_iota(jnp.int32, (8, 128), 1)
    first_lane, last_lane = lane == 0, lane == 127
    zero = jnp.zeros((8, 128), jnp.float32)
    for block in range(rows // 8):
        y = 8 + 8 * block
        mid = [state[now, i, t, pl.ds(y, 8)] for t in range(tiles)]
        ahead = [pltpu.roll(m, 127, 1) for m in mid]
        behind = [pltpu.roll(m, 1, 1) for m in mid]
        for t in range(tiles):
            xp = jnp.where(last_lane, ahead[t + 1] if t + 1 < tiles else zero, ahead[t])
            xm = jnp.where(first_lane, behind[t - 1] if t else zero, behind[t])
            zp = state[now, i + 1, t, pl.ds(y, 8)]
            zm = state[now, i - 1, t, pl.ds(y, 8)]
            yp = state[now, i, t, pl.ds(y + 1, 8)]
            ym = state[now, i, t, pl.ds(y - 1, 8)]
            at = (pl.ds(8 * block, 8), pl.ds(128 * t, 128))
            force, upt, vz, vy, vx = (ref[index + at] for ref, index in coefs)
            spread = ((zp + zm) + (yp + ym)) + (xp + xm)
            carried = vz * (sign * (zp - zm)) + vy * (yp - ym) + vx * (xp - xm)
            kept = ((1.0 - 6.0 * DIFFUSION_FINE) - upt) * mid[t]
            put(block, t, (DIFFUSION_FINE * spread + 0.5 * carried) + (kept + force))


def zero_pads(state):
    count, layers, tiles, rows, lanes = state.shape
    for edge in (0, rows - 8):
        state[:, :, :, pl.ds(edge, 8)] = jnp.zeros((count, layers, tiles, 8, lanes), jnp.float32)


def put_layer(state, which, i, value):
    rows = value.shape[0]
    for t in range(state.shape[2]):
        state[which, i, t, pl.ds(8, rows)] = value[:, 128 * t : 128 * (t + 1)]


def own_coefs(odd, force, vel, upt, c):
    z = jnp.where(odd == 1, c, DEPTH - 1 - c)
    return [(force, (z,)), (upt, (z,)), (vel, (0, z)), (vel, (1, z)), (vel, (2, z))]


def inner_kernel(last, where, force, vel, upt, chip_part, near_part, halo, *refs):
    chip_a, chip_b, chip_c, *refs = refs
    if last:
        edge, out, coarse, state, summed = refs
    else:
        edge, out, state = refs
    odd = lax.rem(where[0], 2)
    sign = jnp.where(odd == 1, 1.0, -1.0)
    zero_pads(state)
    for h in range(1, WIDE + 1):
        put_layer(state, 0, WIDE - h, halo[h - 1])
    for c in range(DEPTH):
        value = chip_part[c] if c < WIDE else near_part[c - WIDE]
        put_layer(state, 0, WIDE + c, value)
        if c >= DEPTH - 2:
            edge[0, c - (DEPTH - 2)] = value
    for step in range(1, WIDE + 1):
        now, later = (step - 1) % 2, step % 2
        for c in range(step - WIDE, DEPTH - step):
            if c < 0:
                i = -c - 1
                coefs = [(chip_a, (WIDE + i,)), (chip_b, (i,)), (chip_b, (THIN + i,))]
                coefs += [(chip_c, (i,)), (chip_c, (THIN + i,))]
            else:
                coefs = own_coefs(odd, force, vel, upt, c)

            def put(block, t, value, c=c, step=step, later=later):
                at = (pl.ds(8 * block, 8), pl.ds(128 * t, 128))
                if step == WIDE:
                    out[(c,) + at] = value
                    return
                state[later, WIDE + c, t, pl.ds(8 + 8 * block, 8)] = value
                if c >= DEPTH - 2 - step:
                    edge[(step, c - (DEPTH - 2 - step)) + at] = value

            layer_step(state, now, WIDE + c, coefs, sign, put)
    if last:
        put_tiles(summed, 0, (out[0] + out[1]) + (out[2] + out[3]))
        coarse[...] = restrict_summed(summed)


def inner(last, where, force, vel, upt, chip_part, near_part, halo, chip):
    _, rows, cols = force.shape
    outs = (f32(WIDE, 2, rows, cols), f32(WIDE, rows, cols))
    scratch = [pltpu.VMEM((2, DEPTH + WIDE, cols // 128, rows + 16, 128), jnp.float32)]
    if last:
        outs += (f32(rows // 4, cols // 4),)
        scratch.append(pltpu.VMEM((cols // 128, rows, 128), jnp.float32))
    return call(
        functools.partial(inner_kernel, last),
        "inner_last" if last else "inner_first",
        outs,
        [SMEM] + [VMEM] * 9,
        (where, force, vel, upt, chip_part, near_part, halo, *chip),
        scratch,
    )


def wedge_kernel(last, where, force, vel, upt, edge, halo, near, near_vel, *refs):
    if last:
        coarse_chip, stepped, out, begun, coarse, state, summed = refs
    else:
        out, state = refs
    slab = where[0]
    odd = lax.rem(slab, 2)
    sign = jnp.where(odd == 1, 1.0, -1.0)
    alive = jnp.where(jnp.logical_or(slab == 1, slab == 2), 1.0, 0.0)
    zero_pads(state)
    for h in range(1, WIDE + 1):
        put_layer(state, 0, 1 + h, halo[WIDE - h])
    for step in range(1, WIDE + 1):
        now, later = (step - 1) % 2, step % 2
        for i in range(2):
            put_layer(state, now, i, edge[step - 1, i])
        for j in range(WIDE):
            c = DEPTH - step + j
            if c < DEPTH:
                coefs = own_coefs(odd, force, vel, upt, c)
            else:
                i = THIN - 1 - (c - DEPTH)
                coefs = [(near, (WIDE + i,)), (near, (WIDE + THIN + i,))]
                coefs += [(near_vel, (part * THIN + i,)) for part in range(3)]

            def put(block, t, value, c=c, j=j, step=step, later=later):
                if c >= DEPTH:
                    value = value * alive
                if step == WIDE:
                    out[j, pl.ds(8 * block, 8), pl.ds(128 * t, 128)] = value
                else:
                    state[later, 2 + j, t, pl.ds(8 + 8 * block, 8)] = value

            layer_step(state, now, 1 + j, coefs, sign, put)
    if last:
        put_tiles(summed, 0, (out[0] + out[1]) + (out[2] + out[3]))
        near_coarse = restrict_summed(summed)
        chip_coarse = coarse_chip[...]
        coarse[0] = jnp.where(odd == 1, chip_coarse, near_coarse)
        coarse[1] = jnp.where(odd == 1, near_coarse, chip_coarse)
        kept = jnp.where(where[1] == 1, 0.0, 1.0)
        part = coarse[...] - kept * stepped[pl.ds(2 * slab, 2)]
        for copy in range(begun.shape[0]):
            begun[copy] = part


def wedge(last, where, force, vel, upt, edge, halo, near, near_vel, more=(), copies=0):
    _, rows, cols = force.shape
    outs = (f32(WIDE, rows, cols),)
    scratch = [pltpu.VMEM((2, WIDE + 2, cols // 128, rows + 16, 128), jnp.float32)]
    if last:
        outs += (f32(copies, 2, rows // 4, cols // 4), f32(2, rows // 4, cols // 4))
        scratch.append(pltpu.VMEM((cols // 128, rows, 128), jnp.float32))
    return call(
        functools.partial(wedge_kernel, last),
        "wedge_last" if last else "wedge_first",
        outs,
        [SMEM] + [VMEM] * (7 + len(more)),
        (where, force, vel, upt, edge, halo, near, near_vel) + more,
        scratch,
    )


NEIGHBOURS = ((0, 0, 0), (1, 0, 0), (-1, 0, 0), (0, 1, 0), (0, -1, 0), (0, 0, 1), (0, 0, -1))
STENCIL = sorted({tuple(a + b for a, b in zip(p, q)) for p in NEIGHBOURS for q in NEIGHBOURS})


def shifted(field, offset):
    dz, dy, dx = offset
    if dz:
        field = jnp.concatenate([field[dz:], field[:dz]], axis=0)
    for axis, by in ((1, dy), (2, dx)):
        if by:
            size = field.shape[axis]
            field = pltpu.roll(field, (size - by) % size, axis)
    return field


def coarse_step(field, coef):
    depth = len(field)
    rows, cols = field[0].shape
    moved = {0: field}
    for dy in (-2, -1, 1, 2):
        moved[dy] = [pltpu.roll(c, (rows - dy) % rows, 0) for c in field]

    def part(dx, z):
        total = None
        for k, offset in enumerate(STENCIL):
            if offset[2] != dx or not 0 <= z + offset[0] < depth:
                continue
            term = coef[k, z] * moved[offset[1]][z + offset[0]]
            total = term if total is None else total + term
        return total

    sides = []
    for z in range(depth):
        sides.append([pltpu.roll(part(dx, z), (cols - dx) % cols, 1) for dx in (-2, 2, -1, 1)])
    return [part(0, z) + ((s[0] + s[1]) + (s[2] + s[3])) for z, s in enumerate(sides)]


def prepare_kernel(where, own, one, pair, coef, stepped, whole):
    slab = where[0]
    size = own.shape[0]
    depth = size // 5
    parts = (own, one, pair.at[pl.ds(0, size)], pair.at[pl.ds(size, size)])
    for flip, ref in enumerate(parts):
        first = lax.bitwise_xor(slab, flip) * depth
        for part in range(5):
            whole[part, pl.ds(first, depth)] = ref[pl.ds(part * depth, depth)]
    full = whole.shape[1:]
    half = {NEIGHBOURS[0]: (1.0 - 6.0 * DIFFUSION_COARSE) - 4.0 * whole[4]}
    for dim in range(3):
        v = whole[1 + dim]
        half[NEIGHBOURS[0]] -= jnp.abs(v)
        at = lax.broadcasted_iota(jnp.int32, full, dim)
        plus = DIFFUSION_COARSE + jnp.maximum(v, 0.0)
        minus = DIFFUSION_COARSE - jnp.minimum(v, 0.0)
        half[NEIGHBOURS[1 + 2 * dim]] = jnp.where(at == full[dim] - 1, 0.0, plus)
        half[NEIGHBOURS[2 + 2 * dim]] = jnp.where(at == 0, 0.0, minus)
    both = {}
    for p in NEIGHBOURS:
        for q in NEIGHBOURS:
            offset = tuple(a + b for a, b in zip(p, q))
            term = half[p] * shifted(half[q], p)
            both[offset] = both[offset] + term if offset in both else term
    for k, offset in enumerate(STENCIL):
        coef[k] = shifted(both[offset], (0, 0, -offset[2]))
    field = coarse_step([whole[0, z] for z in range(full[0])], coef)
    for z in range(full[0]):
        stepped[z] = field[z]


def prepare(where, parts):
    depth5, rows, cols = parts[0].shape
    full = (4 * depth5 // 5, rows, cols)
    return call(
        prepare_kernel,
        "prepare",
        (f32(len(STENCIL), *full), f32(*full)),
        [SMEM] + [VMEM] * 3,
        (where, *parts),
        [pltpu.VMEM((5,) + full, jnp.float32)],
    )


def outer_kernel(where, coef, own, other, out, whole, ends):
    slab, group, place = where[0], where[2], where[3]
    core = lax.rem(slab, 2)
    targets, half = out.shape[:2]
    count, depth = whole.shape[:2]
    chips = own.shape[0] // count
    part = own.shape[1]
    for g in range(count):
        for chip in range(chips):
            here = 2 * chip + core
            there = 2 * chip + 1 - core
            whole[g, pl.ds(here * part, part)] = own[g * chips + chip]
            whole[g, pl.ds(there * part, part)] = other[g * chips + chip]

    def keep(which, layers):
        for z in range(depth):
            ends[which, z] = layers[z]

    def body(i, layers):
        keep(1, layers)
        layers = list(layers)
        for _ in range(targets):
            layers = coarse_step(layers, coef)
        return tuple(layers[z] + whole[count - 2 - i, z] for z in range(depth))

    ends[1] = jnp.zeros(ends.shape[1:], jnp.float32)
    field = tuple(whole[count - 1, z] for z in range(depth))
    keep(0, lax.fori_loop(0, count - 1 - group, body, field))
    for target in range(targets):
        out[target] = ends[jnp.where(place >= target, 0, 1), pl.ds(core * half, half)]


def outer(targets, where, coef, own, other):
    full = coef.shape[1:]
    depth, rows, cols = full
    count = own.shape[0] * own.shape[1] * 2 // depth
    return call(
        outer_kernel,
        "outer",
        f32(targets, depth // 2, rows, cols),
        [SMEM] + [VMEM] * 3,
        (where, coef, own, other),
        [pltpu.VMEM((count,) + full, jnp.float32), pltpu.VMEM((2,) + full, jnp.float32)],
    )


def finish_kernel(where, coef, own, other, coarse, chip_part, near_part, *refs):
    corrected, coarse_new, whole, buffer, down, sem = refs
    slab, place = where[0], where[3]
    odd = lax.rem(slab, 2)
    count, depth = whole.shape[:2]
    half = depth // 2
    for t in range(count):
        whole[t, pl.ds(odd * half, half)] = own[t]
        whole[t, pl.ds((1 - odd) * half, half)] = other[t]

    def term(j):
        return whole.at[lax.rem(place + j, count)]

    def body(i, layers):
        stepped = coarse_step(list(layers), coef)
        added = term(count - 2 - i)
        return tuple(stepped[z] + added[z] for z in range(depth))

    first = term(count - 1)
    field = lax.fori_loop(0, count - 1, body, tuple(first[z] for z in range(depth)))
    for z in range(depth):
        coarse_new[z] = field[z]
    rows, cols = chip_part.shape[1:]
    part = (coarse_new[pl.ds(2 * slab, 2)] - coarse[...]).reshape(rows // 2, cols // 4)
    for row in range(rows // 2):
        down[pl.ds(4 * row, 4)] = jnp.broadcast_to(part[row : row + 1], (4, cols // 4))
    fine = jnp.dot(down[...], groups_of_four(cols // 4, cols, 1.0), precision=HIGH)
    lower, upper = fine[:rows], fine[rows:]
    chip_fine = jnp.where(odd == 1, lower, upper)
    near_fine = jnp.where(odd == 1, upper, lower)
    copies = []
    for c in range(DEPTH):
        buffer[c] = chip_part[c] + chip_fine if c < WIDE else near_part[c - WIDE] + near_fine
        z = jnp.where(odd == 1, c, DEPTH - 1 - c)
        copies.append(pltpu.make_async_copy(buffer.at[c], corrected.at[z], sem.at[c]))
        copies[c].start()
    for copy in copies:
        copy.wait()


def finish(where, *args):
    _, rows, cols = args[-1].shape
    full = args[0].shape[1:]
    return call(
        finish_kernel,
        "finish",
        (f32(DEPTH, rows, cols), f32(*full)),
        [SMEM] + [VMEM] * len(args),
        (where, *args),
        [
            pltpu.VMEM(args[1].shape[:1] + full, jnp.float32),
            pltpu.VMEM((DEPTH, rows, cols), jnp.float32),
            pltpu.VMEM((2 * rows, cols // 4), jnp.float32),
            pltpu.SemaphoreType.DMA((DEPTH,)),
        ],
        (HBM, VMEM),
    )


def per_device(adjoint_end, forcing, velocity, uptake):
    adj, force = adjoint_end[0], forcing[0]
    groups, places, chips, cores = (lax.axis_size(axis) for axis in AXES)
    group, place, chip_no, core = (lax.axis_index(axis) for axis in AXES)
    times, slabs = groups * places, chips * cores
    slab = chip_no * cores + core
    last_slice = jnp.logical_and(group == groups - 1, place == places - 1)
    where = jnp.stack([slab, last_slice.astype(slab.dtype), group, place]).astype(jnp.int32)

    def send(array, pairs):
        route = [(t0 * slabs + s0, t1 * slabs + s1) for (t0, s0), (t1, s1) in pairs]
        return lax.ppermute(array, AXES, route)

    def flipped(array, flip):
        return send(array, [((t, s ^ flip), (t, s)) for t in range(times) for s in range(slabs)])

    def to_next_chip(array, shift=0):
        pairs = [(1, 2), (2, 1)]
        return send(
            array, [((t, a), ((t + shift) % times, b)) for t in range(times) for a, b in pairs]
        )

    own = (force, velocity, uptake)
    near_pack, vel_pack = pack(False, where, (adj, *own))
    near = to_next_chip(near_pack)
    near_vel = to_next_chip(vel_pack, times // 2)
    restricted = restrict_inputs(adj, velocity, uptake)
    chip_packs = pack(True, where, (adj, *own), ())
    chip = [flipped(array, 1) for array in chip_packs]
    restricted_one = flipped(restricted, 1)
    pair = flipped(jnp.concatenate([restricted, restricted_one]), 2)
    edge, chip_part = inner(False, where, *own, chip_packs[0], near_pack, chip[0], chip)
    chip_halo = flipped(chip_part, 1)
    near, near_vel, pair, edge = lax.optimization_barrier((near, near_vel, pair, edge))
    (near_part,) = wedge(False, where, *own, edge, near, near, near_vel)
    near_halo = to_next_chip(near_part)
    edge, chip_part, coarse_chip = inner(True, where, *own, chip_part, near_part, chip_halo, chip)
    coef, stepped = prepare(where, (restricted, restricted_one, pair))
    near_halo, edge, coef, stepped = lax.optimization_barrier((near_halo, edge, coef, stepped))
    near_part, begun, coarse = wedge(
        True, where, *own, edge, near_halo, near, near_vel, (coarse_chip, stepped), groups * chips
    )

    begun = lax.all_to_all(begun, ("group", "chip"), 0, 0)
    terms = outer(places, where, coef, begun, flipped(begun, 1))
    terms = lax.all_to_all(terms, "place", 0, 0)
    corrected, coarse_new = finish(
        where, coef, terms, flipped(terms, 1), coarse, chip_part, near_part
    )
    return corrected[None], coarse_new[None]


def solution(mesh):
    times, slabs = mesh.devices.shape
    places = 8 if times >= 16 else 2
    shape = (times // places, places, slabs // 2, 2)
    time, slab = AXES[:2], AXES[2:]
    return jax.shard_map(
        per_device,
        mesh=Mesh(mesh.devices.reshape(shape), AXES),
        in_specs=(P(time, slab), P(time, slab), P(None, slab), P(slab)),
        out_specs=(P(time, slab), P(time)),
        check_vma=False,
    )
```

```python
import functools

import jax
import jax.numpy as jnp
from jax import lax
from jax.experimental import pallas as pl
from jax.experimental.pallas import tpu as pltpu
from jax.sharding import Mesh
from jax.sharding import PartitionSpec as P

STEPS = 8
WIDE = 4
THIN = WIDE - 1
DEPTH = 8
CHIP_COUNTS = (WIDE + THIN, 2 * THIN, 2 * THIN)
NEAR_COUNTS = (WIDE + 2 * THIN, 3 * THIN)
AXES = ("group", "place", "chip", "core")
DIFFUSION_FINE = 0.15
DIFFUSION_COARSE = 0.0375
HIGH = lax.Precision.HIGHEST
HBM = pl.BlockSpec(memory_space=pltpu.HBM)
SMEM = pl.BlockSpec(memory_space=pltpu.SMEM)
VMEM = pl.BlockSpec(memory_space=pltpu.VMEM)
PARAMS = pltpu.CompilerParams(vmem_limit_bytes=24 * 2**20)


def f32(*shape):
    return jax.ShapeDtypeStruct(shape, jnp.float32)


def call(kernel, name, outs, in_specs, args, scratch=(), out_specs=None):
    return pl.pallas_call(
        kernel,
        out_shape=outs,
        in_specs=in_specs,
        out_specs=out_specs or ((VMEM,) * len(outs) if isinstance(outs, tuple) else VMEM),
        scratch_shapes=list(scratch),
        compiler_params=PARAMS,
        name=name,
        cost_estimate=pl.CostEstimate(flops=1, bytes_accessed=1, transcendentals=0),
    )(*args)


def pack_kernel(to_chip, where, adj, force, vel, upt, *refs):
    counts = CHIP_COUNTS if to_chip else NEAR_COUNTS
    *outs, sem = refs[-1 - len(counts) :]
    places = [out.at[i] for out, count in zip(outs, counts) for i in range(count)]
    odd = lax.rem(where[0], 2)

    def z(c):
        return jnp.where(odd == 1, c, DEPTH - 1 - c)

    sources = [adj.at[z(i if to_chip else DEPTH - WIDE + i)] for i in range(WIDE)]
    layers = [z(i if to_chip else DEPTH - THIN + i) for i in range(THIN)]
    for ref in (force, upt, vel.at[0], vel.at[1], vel.at[2]):
        sources += [ref.at[c] for c in layers]
    copies = [
        pltpu.make_async_copy(src, dst, sem.at[i])
        for i, (src, dst) in enumerate(zip(sources, places))
    ]
    for copy in copies:
        copy.start()
    for copy in copies:
        copy.wait()


def pack(to_chip, where, arrays, after=()):
    _, rows, cols = arrays[0].shape
    arrays = [pltpu.with_memory_space_constraint(x, pltpu.HBM) for x in arrays]
    counts = CHIP_COUNTS if to_chip else NEAR_COUNTS
    return call(
        functools.partial(pack_kernel, to_chip),
        "pack_chip" if to_chip else "pack_near",
        tuple(f32(count, rows, cols) for count in counts),
        [SMEM] + [HBM] * (4 + len(after)),
        (where, *arrays, *after),
        [pltpu.SemaphoreType.DMA((sum(counts),))],
    )


def groups_of_four(rows, cols, value):
    i = lax.broadcasted_iota(jnp.int32, (rows, cols), 0)
    j = lax.broadcasted_iota(jnp.int32, (rows, cols), 1)
    if rows > cols:
        i = lax.shift_right_logical(i, 2)
    else:
        j = lax.shift_right_logical(j, 2)
    return jnp.where(i == j, value, 0.0)


def put_tiles(summed, first, value):
    for t in range(summed.shape[0]):
        summed[t, pl.ds(first, value.shape[0])] = value[:, 128 * t : 128 * (t + 1)]


def restrict_summed(summed):
    tiles, rows, lanes = summed.shape
    down = []
    for t in range(tiles):
        parts = [summed[t, pl.ds(k, rows // 4, 4)] for k in range(4)]
        down.append((parts[0] + parts[1]) + (parts[2] + parts[3]))
    average = groups_of_four(tiles * lanes, tiles * lanes // 4, 1.0 / 64.0)
    return jnp.dot(jnp.concatenate(down, axis=1), average, precision=HIGH)


def restrict_kernel(adj, vel, upt, out, sums):
    rows = adj.shape[1]
    count = 0
    for read in (
        lambda z: adj[z],
        lambda z: vel[0, z],
        lambda z: vel[1, z],
        lambda z: vel[2, z],
        lambda z: upt[z],
    ):
        for z in range(0, DEPTH, 4):
            put_tiles(sums, count, (read(z) + read(z + 1)) + (read(z + 2) + read(z + 3)))
            count += rows
    out[...] = restrict_summed(sums).reshape(out.shape)


def restrict_inputs(adj, vel, upt):
    depth, rows, cols = adj.shape
    return call(
        restrict_kernel,
        "restrict",
        f32(5 * depth // 4, rows // 4, cols // 4),
        [VMEM] * 3,
        (adj, vel, upt),
        [pltpu.VMEM((cols // 128, 5 * depth // 4 * rows, 128), jnp.float32)],
    )


def layer_step(state, now, i, coefs, sign, put):
    tiles, rows = state.shape[2], state.shape[3] - 16
    lane = lax.broadcasted_iota(jnp.int32, (8, 128), 1)
    first_lane, last_lane = lane == 0, lane == 127
    zero = jnp.zeros((8, 128), jnp.float32)
    for block in range(rows // 8):
        y = 8 + 8 * block
        mid = [state[now, i, t, pl.ds(y, 8)] for t in range(tiles)]
        ahead = [pltpu.roll(m, 127, 1) for m in mid]
        behind = [pltpu.roll(m, 1, 1) for m in mid]
        for t in range(tiles):
            xp = jnp.where(last_lane, ahead[t + 1] if t + 1 < tiles else zero, ahead[t])
            xm = jnp.where(first_lane, behind[t - 1] if t else zero, behind[t])
            zp = state[now, i + 1, t, pl.ds(y, 8)]
            zm = state[now, i - 1, t, pl.ds(y, 8)]
            yp = state[now, i, t, pl.ds(y + 1, 8)]
            ym = state[now, i, t, pl.ds(y - 1, 8)]
            at = (pl.ds(8 * block, 8), pl.ds(128 * t, 128))
            force, upt, vz, vy, vx = (ref[index + at] for ref, index in coefs)
            spread = ((zp + zm) + (yp + ym)) + (xp + xm)
            carried = vz * (sign * (zp - zm)) + vy * (yp - ym) + vx * (xp - xm)
            kept = ((1.0 - 6.0 * DIFFUSION_FINE) - upt) * mid[t]
            put(block, t, (DIFFUSION_FINE * spread + 0.5 * carried) + (kept + force))


def zero_pads(state):
    count, layers, tiles, rows, lanes = state.shape
    for edge in (0, rows - 8):
        state[:, :, :, pl.ds(edge, 8)] = jnp.zeros((count, layers, tiles, 8, lanes), jnp.float32)


def put_layer(state, which, i, value):
    rows = value.shape[0]
    for t in range(state.shape[2]):
        state[which, i, t, pl.ds(8, rows)] = value[:, 128 * t : 128 * (t + 1)]


def own_coefs(odd, force, vel, upt, c):
    z = jnp.where(odd == 1, c, DEPTH - 1 - c)
    return [(force, (z,)), (upt, (z,)), (vel, (0, z)), (vel, (1, z)), (vel, (2, z))]


def inner_kernel(last, where, force, vel, upt, chip_part, near_part, halo, *refs):
    chip_a, chip_b, chip_c, *refs = refs
    if last:
        edge, out, coarse, state, summed = refs
    else:
        edge, out, state = refs
    odd = lax.rem(where[0], 2)
    sign = jnp.where(odd == 1, 1.0, -1.0)
    zero_pads(state)
    for h in range(1, WIDE + 1):
        put_layer(state, 0, WIDE - h, halo[h - 1])
    for c in range(DEPTH):
        value = chip_part[c] if c < WIDE else near_part[c - WIDE]
        put_layer(state, 0, WIDE + c, value)
        if c >= DEPTH - 2:
            edge[0, c - (DEPTH - 2)] = value
    for step in range(1, WIDE + 1):
        now, later = (step - 1) % 2, step % 2
        for c in range(step - WIDE, DEPTH - step):
            if c < 0:
                i = -c - 1
                coefs = [(chip_a, (WIDE + i,)), (chip_b, (i,)), (chip_b, (THIN + i,))]
                coefs += [(chip_c, (i,)), (chip_c, (THIN + i,))]
            else:
                coefs = own_coefs(odd, force, vel, upt, c)

            def put(block, t, value, c=c, step=step, later=later):
                at = (pl.ds(8 * block, 8), pl.ds(128 * t, 128))
                if step == WIDE:
                    out[(c,) + at] = value
                    return
                state[later, WIDE + c, t, pl.ds(8 + 8 * block, 8)] = value
                if c >= DEPTH - 2 - step:
                    edge[(step, c - (DEPTH - 2 - step)) + at] = value

            layer_step(state, now, WIDE + c, coefs, sign, put)
    if last:
        put_tiles(summed, 0, (out[0] + out[1]) + (out[2] + out[3]))
        coarse[...] = restrict_summed(summed)


def inner(last, where, force, vel, upt, chip_part, near_part, halo, chip):
    _, rows, cols = force.shape
    outs = (f32(WIDE, 2, rows, cols), f32(WIDE, rows, cols))
    scratch = [pltpu.VMEM((2, DEPTH + WIDE, cols // 128, rows + 16, 128), jnp.float32)]
    if last:
        outs += (f32(rows // 4, cols // 4),)
        scratch.append(pltpu.VMEM((cols // 128, rows, 128), jnp.float32))
    return call(
        functools.partial(inner_kernel, last),
        "inner_last" if last else "inner_first",
        outs,
        [SMEM] + [VMEM] * 9,
        (where, force, vel, upt, chip_part, near_part, halo, *chip),
        scratch,
    )


def wedge_kernel(last, where, force, vel, upt, edge, halo, near, near_vel, *refs):
    if last:
        coarse_chip, stepped, out, begun, coarse, state, summed = refs
    else:
        out, state = refs
    slab = where[0]
    odd = lax.rem(slab, 2)
    sign = jnp.where(odd == 1, 1.0, -1.0)
    alive = jnp.where(jnp.logical_or(slab == 1, slab == 2), 1.0, 0.0)
    zero_pads(state)
    for h in range(1, WIDE + 1):
        put_layer(state, 0, 1 + h, halo[WIDE - h])
    for step in range(1, WIDE + 1):
        now, later = (step - 1) % 2, step % 2
        for i in range(2):
            put_layer(state, now, i, edge[step - 1, i])
        for j in range(WIDE):
            c = DEPTH - step + j
            if c < DEPTH:
                coefs = own_coefs(odd, force, vel, upt, c)
            else:
                i = THIN - 1 - (c - DEPTH)
                coefs = [(near, (WIDE + i,)), (near, (WIDE + THIN + i,))]
                coefs += [(near_vel, (part * THIN + i,)) for part in range(3)]

            def put(block, t, value, c=c, j=j, step=step, later=later):
                if c >= DEPTH:
                    value = value * alive
                if step == WIDE:
                    out[j, pl.ds(8 * block, 8), pl.ds(128 * t, 128)] = value
                else:
                    state[later, 2 + j, t, pl.ds(8 + 8 * block, 8)] = value

            layer_step(state, now, 1 + j, coefs, sign, put)
    if last:
        put_tiles(summed, 0, (out[0] + out[1]) + (out[2] + out[3]))
        near_coarse = restrict_summed(summed)
        chip_coarse = coarse_chip[...]
        coarse[0] = jnp.where(odd == 1, chip_coarse, near_coarse)
        coarse[1] = jnp.where(odd == 1, near_coarse, chip_coarse)
        kept = jnp.where(where[1] == 1, 0.0, 1.0)
        part = coarse[...] - kept * stepped[pl.ds(2 * slab, 2)]
        for copy in range(begun.shape[0]):
            begun[copy] = part


def wedge(last, where, force, vel, upt, edge, halo, near, near_vel, more=(), copies=0):
    _, rows, cols = force.shape
    outs = (f32(WIDE, rows, cols),)
    scratch = [pltpu.VMEM((2, WIDE + 2, cols // 128, rows + 16, 128), jnp.float32)]
    if last:
        outs += (f32(copies, 2, rows // 4, cols // 4), f32(2, rows // 4, cols // 4))
        scratch.append(pltpu.VMEM((cols // 128, rows, 128), jnp.float32))
    return call(
        functools.partial(wedge_kernel, last),
        "wedge_last" if last else "wedge_first",
        outs,
        [SMEM] + [VMEM] * (7 + len(more)),
        (where, force, vel, upt, edge, halo, near, near_vel) + more,
        scratch,
    )


NEIGHBOURS = ((0, 0, 0), (1, 0, 0), (-1, 0, 0), (0, 1, 0), (0, -1, 0), (0, 0, 1), (0, 0, -1))
STENCIL = sorted({tuple(a + b for a, b in zip(p, q)) for p in NEIGHBOURS for q in NEIGHBOURS})


def shifted(field, offset):
    dz, dy, dx = offset
    if dz:
        field = jnp.concatenate([field[dz:], field[:dz]], axis=0)
    for axis, by in ((1, dy), (2, dx)):
        if by:
            size = field.shape[axis]
            field = pltpu.roll(field, (size - by) % size, axis)
    return field


def coarse_step(field, coef):
    depth = len(field)
    rows, cols = field[0].shape
    moved = {0: field}
    for dy in (-2, -1, 1, 2):
        moved[dy] = [pltpu.roll(c, (rows - dy) % rows, 0) for c in field]

    def part(dx, z):
        total = None
        for k, offset in enumerate(STENCIL):
            if offset[2] != dx or not 0 <= z + offset[0] < depth:
                continue
            term = coef[k, z] * moved[offset[1]][z + offset[0]]
            total = term if total is None else total + term
        return total

    sides = []
    for z in range(depth):
        sides.append([pltpu.roll(part(dx, z), (cols - dx) % cols, 1) for dx in (-2, 2, -1, 1)])
    return [part(0, z) + ((s[0] + s[1]) + (s[2] + s[3])) for z, s in enumerate(sides)]


def prepare_kernel(where, own, one, pair, coef, stepped, whole):
    slab = where[0]
    size = own.shape[0]
    depth = size // 5
    parts = (own, one, pair.at[pl.ds(0, size)], pair.at[pl.ds(size, size)])
    for flip, ref in enumerate(parts):
        first = lax.bitwise_xor(slab, flip) * depth
        for part in range(5):
            whole[part, pl.ds(first, depth)] = ref[pl.ds(part * depth, depth)]
    full = whole.shape[1:]
    half = {NEIGHBOURS[0]: (1.0 - 6.0 * DIFFUSION_COARSE) - 4.0 * whole[4]}
    for dim in range(3):
        v = whole[1 + dim]
        half[NEIGHBOURS[0]] -= jnp.abs(v)
        at = lax.broadcasted_iota(jnp.int32, full, dim)
        plus = DIFFUSION_COARSE + jnp.maximum(v, 0.0)
        minus = DIFFUSION_COARSE - jnp.minimum(v, 0.0)
        half[NEIGHBOURS[1 + 2 * dim]] = jnp.where(at == full[dim] - 1, 0.0, plus)
        half[NEIGHBOURS[2 + 2 * dim]] = jnp.where(at == 0, 0.0, minus)
    both = {}
    for p in NEIGHBOURS:
        for q in NEIGHBOURS:
            offset = tuple(a + b for a, b in zip(p, q))
            term = half[p] * shifted(half[q], p)
            both[offset] = both[offset] + term if offset in both else term
    for k, offset in enumerate(STENCIL):
        coef[k] = shifted(both[offset], (0, 0, -offset[2]))
    field = coarse_step([whole[0, z] for z in range(full[0])], coef)
    for z in range(full[0]):
        stepped[z] = field[z]


def prepare(where, parts):
    depth5, rows, cols = parts[0].shape
    full = (4 * depth5 // 5, rows, cols)
    return call(
        prepare_kernel,
        "prepare",
        (f32(len(STENCIL), *full), f32(*full)),
        [SMEM] + [VMEM] * 3,
        (where, *parts),
        [pltpu.VMEM((5,) + full, jnp.float32)],
    )


def outer_kernel(where, coef, own, other, out, whole, ends):
    slab, group, place = where[0], where[2], where[3]
    core = lax.rem(slab, 2)
    targets = out.shape[0]
    count, depth = whole.shape[:2]
    chips = own.shape[0] // count
    part = own.shape[1]
    for g in range(count):
        for chip in range(chips):
            here = 2 * chip + core
            there = 2 * chip + 1 - core
            whole[g, pl.ds(here * part, part)] = own[g * chips + chip]
            whole[g, pl.ds(there * part, part)] = other[g * chips + chip]

    def keep(which, layers):
        for z in range(depth):
            ends[which, z] = layers[z]

    def body(i, layers):
        keep(1, layers)
        layers = list(layers)
        for _ in range(targets):
            layers = coarse_step(layers, coef)
        return tuple(layers[z] + whole[count - 2 - i, z] for z in range(depth))

    ends[1] = jnp.zeros(ends.shape[1:], jnp.float32)
    field = tuple(whole[count - 1, z] for z in range(depth))
    keep(0, lax.fori_loop(0, count - 1 - group, body, field))
    for target in range(targets):
        out[target] = ends[jnp.where(place >= target, 0, 1)]


def outer(targets, where, coef, own, other):
    full = coef.shape[1:]
    depth = full[0]
    count = own.shape[0] * own.shape[1] * 2 // depth
    return call(
        outer_kernel,
        "outer",
        f32(targets, *full),
        [SMEM] + [VMEM] * 3,
        (where, coef, own, other),
        [pltpu.VMEM((count,) + full, jnp.float32), pltpu.VMEM((2,) + full, jnp.float32)],
    )


def finish_kernel(where, coef, terms, coarse, chip_part, near_part, *refs):
    corrected, coarse_new, down = refs
    slab, place = where[0], where[3]
    odd = lax.rem(slab, 2)
    count, depth = terms.shape[:2]

    def term(j):
        return terms.at[lax.rem(place + j, count)]

    def body(i, layers):
        stepped = coarse_step(list(layers), coef)
        added = term(count - 2 - i)
        return tuple(stepped[z] + added[z] for z in range(depth))

    first = term(count - 1)
    field = lax.fori_loop(0, count - 1, body, tuple(first[z] for z in range(depth)))
    for z in range(depth):
        coarse_new[z] = field[z]
    rows, cols = chip_part.shape[1:]
    part = (coarse_new[pl.ds(2 * slab, 2)] - coarse[...]).reshape(rows // 2, cols // 4)
    for row in range(rows // 2):
        down[pl.ds(4 * row, 4)] = jnp.broadcast_to(part[row : row + 1], (4, cols // 4))
    fine = jnp.dot(down[...], groups_of_four(cols // 4, cols, 1.0), precision=HIGH)
    lower, upper = fine[:rows], fine[rows:]
    chip_fine = jnp.where(odd == 1, lower, upper)
    near_fine = jnp.where(odd == 1, upper, lower)
    for c in range(DEPTH):
        z = jnp.where(odd == 1, c, DEPTH - 1 - c)
        corrected[z] = chip_part[c] + chip_fine if c < WIDE else near_part[c - WIDE] + near_fine


def finish(where, *args):
    _, rows, cols = args[-1].shape
    full = args[0].shape[1:]
    return call(
        finish_kernel,
        "finish",
        (f32(DEPTH, rows, cols), f32(*full)),
        [SMEM] + [VMEM] * len(args),
        (where, *args),
        [pltpu.VMEM((2 * rows, cols // 4), jnp.float32)],
    )


def per_device(adjoint_end, forcing, velocity, uptake):
    adj, force = adjoint_end[0], forcing[0]
    groups, places, chips, cores = (lax.axis_size(axis) for axis in AXES)
    group, place, chip_no, core = (lax.axis_index(axis) for axis in AXES)
    times, slabs = groups * places, chips * cores
    slab = chip_no * cores + core
    last_slice = jnp.logical_and(group == groups - 1, place == places - 1)
    where = jnp.stack([slab, last_slice.astype(slab.dtype), group, place]).astype(jnp.int32)

    def send(array, pairs):
        route = [(t0 * slabs + s0, t1 * slabs + s1) for (t0, s0), (t1, s1) in pairs]
        return lax.ppermute(array, AXES, route)

    def flipped(array, flip):
        return send(array, [((t, s ^ flip), (t, s)) for t in range(times) for s in range(slabs)])

    def to_next_chip(array, shift=0):
        pairs = [(1, 2), (2, 1)]
        return send(
            array, [((t, a), ((t + shift) % times, b)) for t in range(times) for a, b in pairs]
        )

    own = (force, velocity, uptake)
    near_pack, vel_pack = pack(False, where, (adj, *own))
    near = to_next_chip(near_pack)
    near_vel = to_next_chip(vel_pack, times // 2)
    restricted = restrict_inputs(adj, velocity, uptake)
    chip_packs = pack(True, where, (adj, *own), ())
    chip = [flipped(array, 1) for array in chip_packs]
    restricted_one = flipped(restricted, 1)
    pair = flipped(jnp.concatenate([restricted, restricted_one]), 2)
    edge, chip_part = inner(False, where, *own, chip_packs[0], near_pack, chip[0], chip)
    chip_halo = flipped(chip_part, 1)
    near, near_vel, pair, edge = lax.optimization_barrier((near, near_vel, pair, edge))
    (near_part,) = wedge(False, where, *own, edge, near, near, near_vel)
    near_halo = to_next_chip(near_part)
    edge, chip_part, coarse_chip = inner(True, where, *own, chip_part, near_part, chip_halo, chip)
    coef, stepped = prepare(where, (restricted, restricted_one, pair))
    near_halo, edge, coef, stepped = lax.optimization_barrier((near_halo, edge, coef, stepped))
    near_part, begun, coarse = wedge(
        True, where, *own, edge, near_halo, near, near_vel, (coarse_chip, stepped), groups * chips
    )

    begun = lax.all_to_all(begun, ("group", "chip"), 0, 0)
    terms = outer(places, where, coef, begun, flipped(begun, 1))
    terms = lax.all_to_all(terms, "place", 0, 0)
    corrected, coarse_new = finish(where, coef, terms, coarse, chip_part, near_part)
    return corrected[None], coarse_new[None]


def solution(mesh):
    times, slabs = mesh.devices.shape
    places = 8 if times >= 16 else 2
    shape = (times // places, places, slabs // 2, 2)
    time, slab = AXES[:2], AXES[2:]
    return jax.shard_map(
        per_device,
        mesh=Mesh(mesh.devices.reshape(shape), AXES),
        in_specs=(P(time, slab), P(time, slab), P(None, slab), P(slab)),
        out_specs=(P(time, slab), P(time)),
        check_vma=False,
    )
```

```python
import functools

import jax
import jax.numpy as jnp
from jax import lax
from jax.experimental import pallas as pl
from jax.experimental.pallas import tpu as pltpu
from jax.sharding import Mesh
from jax.sharding import PartitionSpec as P

STEPS = 8
WIDE = 4
THIN = WIDE - 1
DEPTH = 8
CHIP_COUNTS = (7, 6, 6)
STAIRS = 4
KNOWN = 2
SHARED = 3
AXES = ("group", "place", "chip", "core")
DIFFUSION_FINE = 0.15
DIFFUSION_COARSE = 0.0375
HIGH = lax.Precision.HIGHEST
HBM = pl.BlockSpec(memory_space=pltpu.HBM)
SMEM = pl.BlockSpec(memory_space=pltpu.SMEM)
VMEM = pl.BlockSpec(memory_space=pltpu.VMEM)
PARAMS = pltpu.CompilerParams(vmem_limit_bytes=24 * 2**20)


def f32(*shape):
    return jax.ShapeDtypeStruct(shape, jnp.float32)


def call(kernel, name, outs, in_specs, args, scratch=(), out_specs=None):
    return pl.pallas_call(
        kernel,
        out_shape=outs,
        in_specs=in_specs,
        out_specs=out_specs or ((VMEM,) * len(outs) if isinstance(outs, tuple) else VMEM),
        scratch_shapes=list(scratch),
        compiler_params=PARAMS,
        name=name,
        cost_estimate=pl.CostEstimate(flops=1, bytes_accessed=1, transcendentals=0),
    )(*args)


def layer_of(odd, c):
    return jnp.where(odd == 1, c, DEPTH - 1 - c)


def pack_kernel(where, adj, force, vel, upt, near, near_rest, *refs):
    chip, (edge, coefs, state, sem) = refs[: len(CHIP_COUNTS)], refs[len(CHIP_COUNTS) :]
    odd = lax.rem(where[0], 2)
    sign = jnp.where(odd == 1, 1.0, -1.0)
    copies = []

    def add(src, dst):
        copies.append(pltpu.make_async_copy(src, dst, sem.at[len(copies)]))

    for i in range(WIDE):
        add(adj.at[layer_of(odd, DEPTH - WIDE + i)], edge.at[i])
    parts = (force, upt, vel.at[0], vel.at[1], vel.at[2])
    for part, ref in enumerate(parts):
        add(ref.at[layer_of(odd, DEPTH - 3)], coefs.at[part])
        for h in range(KNOWN):
            out, at = near_place(near, near_rest, part, h)
            add(ref.at[layer_of(odd, DEPTH - 1 - h)], out.at[at])
    needed = len(copies)
    sources = [adj.at[layer_of(odd, c)] for c in range(WIDE)]
    for ref in parts:
        sources += [ref.at[layer_of(odd, c)] for c in range(THIN)]
    places = [out.at[i] for out, count in zip(chip, CHIP_COUNTS) for i in range(count)]
    for src, dst in zip(sources, places):
        add(src, dst)
    for copy in copies:
        copy.start()
    zero_pads(state)
    for copy in copies[:needed]:
        copy.wait()
    for i in range(WIDE):
        put_layer(state, 0, i, edge[i])
    near[0] = edge[WIDE - 1]
    near[1] = edge[WIDE - 2]
    second = near_coefs(near, near_rest, 1)
    put_stairs(state, (second, [(coefs, (part,)) for part in range(5)]), sign, near, 0)
    for copy in copies[needed:]:
        copy.wait()


def near_place(near, near_rest, part, h):
    at = part * KNOWN + h
    return (near, STAIRS + at) if at < SHARED else (near_rest, at - SHARED)


def near_coefs(near, near_rest, h):
    places = [near_place(near, near_rest, part, h) for part in range(5)]
    return [(ref, (at,)) for ref, at in places]


def put_stairs(state, coefs, sign, out, first):
    for which in range(2):

        def put(block, t, value, which=which):
            out[2 + which, pl.ds(8 * block, 8), pl.ds(128 * t, 128)] = value

        layer_step(state, 0, first + WIDE - 2 - which, coefs[which], sign, put)


def pack(where, *arrays):
    _, rows, cols = arrays[0].shape
    arrays = [pltpu.with_memory_space_constraint(x, pltpu.HBM) for x in arrays]
    counts = (STAIRS + SHARED, 5 * KNOWN - SHARED) + CHIP_COUNTS
    return call(
        pack_kernel,
        "pack",
        tuple(f32(count, rows, cols) for count in counts),
        [SMEM] + [HBM] * 4,
        (where, *arrays),
        [
            pltpu.VMEM((WIDE, rows, cols), jnp.float32),
            pltpu.VMEM((5, rows, cols), jnp.float32),
            pltpu.VMEM((1, WIDE, cols // 128, rows + 16, 128), jnp.float32),
            pltpu.SemaphoreType.DMA((WIDE + 5 * (KNOWN + 1) + sum(CHIP_COUNTS),)),
        ],
    )


def groups_of_four(rows, cols, value):
    i = lax.broadcasted_iota(jnp.int32, (rows, cols), 0)
    j = lax.broadcasted_iota(jnp.int32, (rows, cols), 1)
    if rows > cols:
        i = lax.shift_right_logical(i, 2)
    else:
        j = lax.shift_right_logical(j, 2)
    return jnp.where(i == j, value, 0.0)


def put_tiles(summed, first, value):
    for t in range(summed.shape[0]):
        summed[t, pl.ds(first, value.shape[0])] = value[:, 128 * t : 128 * (t + 1)]


def restrict_summed(summed):
    tiles, rows, lanes = summed.shape
    down = []
    for t in range(tiles):
        parts = [summed[t, pl.ds(k, rows // 4, 4)] for k in range(4)]
        down.append((parts[0] + parts[1]) + (parts[2] + parts[3]))
    average = groups_of_four(tiles * lanes, tiles * lanes // 4, 1.0 / 64.0)
    return jnp.dot(jnp.concatenate(down, axis=1), average, precision=HIGH)


def restrict_kernel(adj, vel, upt, out, sums):
    rows = adj.shape[1]
    count = 0
    for read in (
        lambda z: adj[z],
        lambda z: vel[0, z],
        lambda z: vel[1, z],
        lambda z: vel[2, z],
        lambda z: upt[z],
    ):
        for z in range(0, DEPTH, 4):
            put_tiles(sums, count, (read(z) + read(z + 1)) + (read(z + 2) + read(z + 3)))
            count += rows
    out[...] = restrict_summed(sums).reshape(out.shape)


def restrict_inputs(adj, vel, upt):
    depth, rows, cols = adj.shape
    return call(
        restrict_kernel,
        "restrict",
        f32(5 * depth // 4, rows // 4, cols // 4),
        [VMEM] * 3,
        (adj, vel, upt),
        [pltpu.VMEM((cols // 128, 5 * depth // 4 * rows, 128), jnp.float32)],
    )


def layer_step(state, now, i, coefs, sign, put):
    tiles, rows = state.shape[2], state.shape[3] - 16
    lane = lax.broadcasted_iota(jnp.int32, (8, 128), 1)
    first_lane, last_lane = lane == 0, lane == 127
    zero = jnp.zeros((8, 128), jnp.float32)
    for block in range(rows // 8):
        y = 8 + 8 * block
        mid = [state[now, i, t, pl.ds(y, 8)] for t in range(tiles)]
        ahead = [pltpu.roll(m, 127, 1) for m in mid]
        behind = [pltpu.roll(m, 1, 1) for m in mid]
        for t in range(tiles):
            xp = jnp.where(last_lane, ahead[t + 1] if t + 1 < tiles else zero, ahead[t])
            xm = jnp.where(first_lane, behind[t - 1] if t else zero, behind[t])
            zp = state[now, i + 1, t, pl.ds(y, 8)]
            zm = state[now, i - 1, t, pl.ds(y, 8)]
            yp = state[now, i, t, pl.ds(y + 1, 8)]
            ym = state[now, i, t, pl.ds(y - 1, 8)]
            at = (pl.ds(8 * block, 8), pl.ds(128 * t, 128))
            force, upt, vz, vy, vx = (ref[index + at] for ref, index in coefs)
            spread = ((zp + zm) + (yp + ym)) + (xp + xm)
            carried = vz * (sign * (zp - zm)) + vy * (yp - ym) + vx * (xp - xm)
            kept = ((1.0 - 6.0 * DIFFUSION_FINE) - upt) * mid[t]
            put(block, t, (DIFFUSION_FINE * spread + 0.5 * carried) + (kept + force))


def zero_pads(state):
    count, layers, tiles, rows, lanes = state.shape
    for edge in (0, rows - 8):
        state[:, :, :, pl.ds(edge, 8)] = jnp.zeros((count, layers, tiles, 8, lanes), jnp.float32)


def put_layer(state, which, i, value):
    rows = value.shape[0]
    for t in range(state.shape[2]):
        state[which, i, t, pl.ds(8, rows)] = value[:, 128 * t : 128 * (t + 1)]


def own_coefs(odd, force, vel, upt, c):
    z = layer_of(odd, c)
    return [(force, (z,)), (upt, (z,)), (vel, (0, z)), (vel, (1, z)), (vel, (2, z))]


def chip_coefs(halo, i):
    places = [(ref, at) for ref, count in zip(halo, CHIP_COUNTS) for at in range(count)]
    return [(ref, (at,)) for ref, at in places[WIDE + i :: THIN]]


def inner_kernel(last, where, force, vel, upt, *refs):
    begin = 2 if last else 1
    own, halo = refs[:begin], refs[begin]
    chip, refs = refs[begin + 1 :][: len(CHIP_COUNTS)], refs[begin + 1 + len(CHIP_COUNTS) :]
    if last:
        edge, out, coarse, state, summed = refs
    else:
        edge, out, state = refs
    odd = lax.rem(where[0], 2)
    sign = jnp.where(odd == 1, 1.0, -1.0)
    zero_pads(state)
    for h in range(1, WIDE + 1):
        put_layer(state, 0, WIDE - h, halo[h - 1])
    for c in range(DEPTH):
        value = own[c // WIDE][c % WIDE] if last else own[0][layer_of(odd, c)]
        put_layer(state, 0, WIDE + c, value)
        if c >= DEPTH - 2:
            edge[0, c - (DEPTH - 2)] = value
    for step in range(1, WIDE + 1):
        now, later = (step - 1) % 2, step % 2
        for c in range(step - WIDE, DEPTH - step):
            if c < 0:
                i = -c - 1
                coefs = chip_coefs(chip, i)
            else:
                coefs = own_coefs(odd, force, vel, upt, c)

            def put(block, t, value, c=c, step=step, later=later):
                at = (pl.ds(8 * block, 8), pl.ds(128 * t, 128))
                if step == WIDE:
                    out[(c,) + at] = value
                    return
                state[later, WIDE + c, t, pl.ds(8 + 8 * block, 8)] = value
                if c >= DEPTH - 2 - step:
                    edge[(step, c - (DEPTH - 2 - step)) + at] = value

            layer_step(state, now, WIDE + c, coefs, sign, put)
    if last:
        put_tiles(summed, 0, (out[0] + out[1]) + (out[2] + out[3]))
        coarse[...] = restrict_summed(summed)


def inner(last, where, force, vel, upt, own, halo, chip):
    _, rows, cols = force.shape
    outs = (f32(WIDE, 2, rows, cols), f32(WIDE, rows, cols))
    scratch = [pltpu.VMEM((2, DEPTH + WIDE, cols // 128, rows + 16, 128), jnp.float32)]
    if last:
        outs += (f32(rows // 4, cols // 4),)
        scratch.append(pltpu.VMEM((cols // 128, rows, 128), jnp.float32))
    return call(
        functools.partial(inner_kernel, last),
        "inner_last" if last else "inner_first",
        outs,
        [SMEM] + [VMEM] * (4 + len(own) + len(chip)),
        (where, force, vel, upt, *own, halo, *chip),
        scratch,
    )


def wedge_kernel(last, where, force, vel, upt, edge, halo, near, near_rest, *refs):
    if last:
        coarse_chip, stepped, out, begun, coarse, state, summed = refs
    else:
        out, ahead, state = refs
    slab = where[0]
    odd = lax.rem(slab, 2)
    sign = jnp.where(odd == 1, 1.0, -1.0)
    alive = jnp.where(jnp.logical_or(slab == 1, slab == 2), 1.0, 0.0)
    zero_pads(state)
    put_layer(state, 0, 2, halo[0])
    put_layer(state, 0, 3, halo[1])
    for step in range(1, WIDE + 1):
        now, later = (step - 1) % 2, step % 2
        for i in range(2):
            put_layer(state, now, i, edge[step - 1, i])
        if step == 2:
            put_layer(state, now, 4, halo[2])
            put_layer(state, now, 5, halo[3])
        for j in range(2 if step == 1 else WIDE):
            c = DEPTH - step + j
            if c < DEPTH:
                coefs = own_coefs(odd, force, vel, upt, c)
            else:
                coefs = near_coefs(near, near_rest, c - DEPTH)

            def put(block, t, value, c=c, j=j, step=step, later=later):
                if c >= DEPTH:
                    value = value * alive
                if step == WIDE:
                    out[j, pl.ds(8 * block, 8), pl.ds(128 * t, 128)] = value
                if step < WIDE or not last:
                    state[later, 2 + j, t, pl.ds(8 + 8 * block, 8)] = value

            layer_step(state, now, 1 + j, coefs, sign, put)
    if not last:
        ahead[0] = out[WIDE - 1]
        ahead[1] = out[WIDE - 2]
        coefs = [own_coefs(odd, force, vel, upt, c) for c in (DEPTH - 2, DEPTH - 3)]
        put_stairs(state, coefs, sign, ahead, 2)
    if last:
        put_tiles(summed, 0, (out[0] + out[1]) + (out[2] + out[3]))
        near_coarse = restrict_summed(summed)
        chip_coarse = coarse_chip[...]
        coarse[0] = jnp.where(odd == 1, chip_coarse, near_coarse)
        coarse[1] = jnp.where(odd == 1, near_coarse, chip_coarse)
        kept = jnp.where(where[1] == 1, 0.0, 1.0)
        part = coarse[...] - kept * stepped[pl.ds(2 * slab, 2)]
        for copy in range(begun.shape[0]):
            begun[copy] = part


def wedge(last, where, force, vel, upt, edge, halo, near, near_rest, more=(), copies=0):
    _, rows, cols = force.shape
    outs = (f32(WIDE, rows, cols),)
    if not last:
        outs += (f32(STAIRS, rows, cols),)
    scratch = [pltpu.VMEM((2, WIDE + 2, cols // 128, rows + 16, 128), jnp.float32)]
    if last:
        outs += (f32(copies, 2, rows // 4, cols // 4), f32(2, rows // 4, cols // 4))
        scratch.append(pltpu.VMEM((cols // 128, rows, 128), jnp.float32))
    return call(
        functools.partial(wedge_kernel, last),
        "wedge_last" if last else "wedge_first",
        outs,
        [SMEM] + [VMEM] * (7 + len(more)),
        (where, force, vel, upt, edge, halo, near, near_rest) + more,
        scratch,
    )


NEIGHBOURS = ((0, 0, 0), (1, 0, 0), (-1, 0, 0), (0, 1, 0), (0, -1, 0), (0, 0, 1), (0, 0, -1))
STENCIL = sorted({tuple(a + b for a, b in zip(p, q)) for p in NEIGHBOURS for q in NEIGHBOURS})


def shifted(field, offset):
    dz, dy, dx = offset
    if dz:
        field = jnp.concatenate([field[dz:], field[:dz]], axis=0)
    for axis, by in ((1, dy), (2, dx)):
        if by:
            size = field.shape[axis]
            field = pltpu.roll(field, (size - by) % size, axis)
    return field


def coarse_step(field, coef):
    depth = len(field)
    rows, cols = field[0].shape
    moved = {0: field}
    for dy in (-2, -1, 1, 2):
        moved[dy] = [pltpu.roll(c, (rows - dy) % rows, 0) for c in field]

    def part(dx, z):
        total = None
        for k, offset in enumerate(STENCIL):
            if offset[2] != dx or not 0 <= z + offset[0] < depth:
                continue
            term = coef[k, z] * moved[offset[1]][z + offset[0]]
            total = term if total is None else total + term
        return total

    sides = []
    for z in range(depth):
        sides.append([pltpu.roll(part(dx, z), (cols - dx) % cols, 1) for dx in (-2, 2, -1, 1)])
    return [part(0, z) + ((s[0] + s[1]) + (s[2] + s[3])) for z, s in enumerate(sides)]


def prepare_kernel(where, own, one, pair, coef, stepped, whole):
    slab = where[0]
    size = own.shape[0]
    depth = size // 5
    parts = (own, one, pair.at[pl.ds(0, size)], pair.at[pl.ds(size, size)])
    for flip, ref in enumerate(parts):
        first = lax.bitwise_xor(slab, flip) * depth
        for part in range(5):
            whole[part, pl.ds(first, depth)] = ref[pl.ds(part * depth, depth)]
    full = whole.shape[1:]
    half = {NEIGHBOURS[0]: (1.0 - 6.0 * DIFFUSION_COARSE) - 4.0 * whole[4]}
    for dim in range(3):
        v = whole[1 + dim]
        half[NEIGHBOURS[0]] -= jnp.abs(v)
        at = lax.broadcasted_iota(jnp.int32, full, dim)
        plus = DIFFUSION_COARSE + jnp.maximum(v, 0.0)
        minus = DIFFUSION_COARSE - jnp.minimum(v, 0.0)
        half[NEIGHBOURS[1 + 2 * dim]] = jnp.where(at == full[dim] - 1, 0.0, plus)
        half[NEIGHBOURS[2 + 2 * dim]] = jnp.where(at == 0, 0.0, minus)
    both = {}
    for p in NEIGHBOURS:
        for q in NEIGHBOURS:
            offset = tuple(a + b for a, b in zip(p, q))
            term = half[p] * shifted(half[q], p)
            both[offset] = both[offset] + term if offset in both else term
    for k, offset in enumerate(STENCIL):
        coef[k] = shifted(both[offset], (0, 0, -offset[2]))
    field = coarse_step([whole[0, z] for z in range(full[0])], coef)
    for z in range(full[0]):
        stepped[z] = field[z]


def prepare(where, parts):
    depth5, rows, cols = parts[0].shape
    full = (4 * depth5 // 5, rows, cols)
    return call(
        prepare_kernel,
        "prepare",
        (f32(len(STENCIL), *full), f32(*full)),
        [SMEM] + [VMEM] * 3,
        (where, *parts),
        [pltpu.VMEM((5,) + full, jnp.float32)],
    )


def outer_kernel(where, coef, own, other, out, whole, ends):
    slab, group, place = where[0], where[2], where[3]
    core = lax.rem(slab, 2)
    targets, half = out.shape[:2]
    count, depth = whole.shape[:2]
    chips = own.shape[0] // count
    part = own.shape[1]
    for g in range(count):
        for chip in range(chips):
            here = 2 * chip + core
            there = 2 * chip + 1 - core
            whole[g, pl.ds(here * part, part)] = own[g * chips + chip]
            whole[g, pl.ds(there * part, part)] = other[g * chips + chip]

    def keep(which, layers):
        for z in range(depth):
            ends[which, z] = layers[z]

    def body(i, layers):
        keep(1, layers)
        layers = list(layers)
        for _ in range(targets):
            layers = coarse_step(layers, coef)
        return tuple(layers[z] + whole[count - 2 - i, z] for z in range(depth))

    ends[1] = jnp.zeros(ends.shape[1:], jnp.float32)
    field = tuple(whole[count - 1, z] for z in range(depth))
    keep(0, lax.fori_loop(0, count - 1 - group, body, field))
    for target in range(targets):
        out[target] = ends[jnp.where(place >= target, 0, 1), pl.ds(core * half, half)]


def outer(targets, where, coef, own, other):
    full = coef.shape[1:]
    depth, rows, cols = full
    count = own.shape[0] * own.shape[1] * 2 // depth
    return call(
        outer_kernel,
        "outer",
        f32(targets, depth // 2, rows, cols),
        [SMEM] + [VMEM] * 3,
        (where, coef, own, other),
        [pltpu.VMEM((count,) + full, jnp.float32), pltpu.VMEM((2,) + full, jnp.float32)],
    )


def finish_kernel(where, coef, own, other, coarse, chip_part, near_part, *refs):
    corrected, coarse_new, whole, down = refs
    slab, place = where[0], where[3]
    odd = lax.rem(slab, 2)
    count, depth = whole.shape[:2]
    half = depth // 2
    for t in range(count):
        whole[t, pl.ds(odd * half, half)] = own[t]
        whole[t, pl.ds((1 - odd) * half, half)] = other[t]

    def term(j):
        return whole.at[lax.rem(place + j, count)]

    def body(i, layers):
        stepped = coarse_step(list(layers), coef)
        added = term(count - 2 - i)
        return tuple(stepped[z] + added[z] for z in range(depth))

    first = term(count - 1)
    field = lax.fori_loop(0, count - 1, body, tuple(first[z] for z in range(depth)))
    for z in range(depth):
        coarse_new[z] = field[z]
    rows, cols = chip_part.shape[1:]
    part = (coarse_new[pl.ds(2 * slab, 2)] - coarse[...]).reshape(rows // 2, cols // 4)
    for row in range(rows // 2):
        down[pl.ds(4 * row, 4)] = jnp.broadcast_to(part[row : row + 1], (4, cols // 4))
    fine = jnp.dot(down[...], groups_of_four(cols // 4, cols, 1.0), precision=HIGH)
    lower, upper = fine[:rows], fine[rows:]
    chip_fine = jnp.where(odd == 1, lower, upper)
    near_fine = jnp.where(odd == 1, upper, lower)
    for c in range(DEPTH):
        z = jnp.where(odd == 1, c, DEPTH - 1 - c)
        corrected[z] = chip_part[c] + chip_fine if c < WIDE else near_part[c - WIDE] + near_fine


def finish(where, *args):
    _, rows, cols = args[-1].shape
    full = args[0].shape[1:]
    return call(
        finish_kernel,
        "finish",
        (f32(DEPTH, rows, cols), f32(*full)),
        [SMEM] + [VMEM] * len(args),
        (where, *args),
        [
            pltpu.VMEM(args[1].shape[:1] + full, jnp.float32),
            pltpu.VMEM((2 * rows, cols // 4), jnp.float32),
        ],
    )


def per_device(adjoint_end, forcing, velocity, uptake):
    adj, force = adjoint_end[0], forcing[0]
    groups, places, chips, cores = (lax.axis_size(axis) for axis in AXES)
    group, place, chip_no, core = (lax.axis_index(axis) for axis in AXES)
    times, slabs = groups * places, chips * cores
    slab = chip_no * cores + core
    last_slice = jnp.logical_and(group == groups - 1, place == places - 1)
    where = jnp.stack([slab, last_slice.astype(slab.dtype), group, place]).astype(jnp.int32)

    def send(array, pairs):
        route = [(t0 * slabs + s0, t1 * slabs + s1) for (t0, s0), (t1, s1) in pairs]
        return lax.ppermute(array, AXES, route)

    def flipped(array, flip):
        return send(array, [((t, s ^ flip), (t, s)) for t in range(times) for s in range(slabs)])

    def to_next_chip(array, shift=0):
        pairs = [(1, 2), (2, 1)]
        return send(
            array, [((t, a), ((t + shift) % times, b)) for t in range(times) for a, b in pairs]
        )

    own = (force, velocity, uptake)
    near_pack, rest_pack, *chip_packs = pack(where, adj, *own)
    near = to_next_chip(near_pack)
    near_rest = to_next_chip(rest_pack, times // 2)
    restricted = restrict_inputs(adj, velocity, uptake)
    chip = [flipped(array, 1) for array in chip_packs]
    restricted_one = flipped(restricted, 1)
    pair = flipped(jnp.concatenate([restricted, restricted_one]), 2)
    edge, chip_part = inner(False, where, *own, (adj,), chip[0], chip)
    chip_halo = flipped(chip_part, 1)
    near, near_rest, pair, edge = lax.optimization_barrier((near, near_rest, pair, edge))
    near_part, ahead = wedge(False, where, *own, edge, near, near, near_rest)
    near_halo = to_next_chip(ahead)
    edge, chip_part, coarse_chip = inner(True, where, *own, (chip_part, near_part), chip_halo, chip)
    coef, stepped = prepare(where, (restricted, restricted_one, pair))
    near_halo, edge, coef, stepped = lax.optimization_barrier((near_halo, edge, coef, stepped))
    near_part, begun, coarse = wedge(
        True, where, *own, edge, near_halo, near, near_rest, (coarse_chip, stepped), groups * chips
    )

    begun = lax.all_to_all(begun, ("group", "chip"), 0, 0)
    terms = outer(places, where, coef, begun, flipped(begun, 1))
    terms = lax.all_to_all(terms, "place", 0, 0)
    corrected, coarse_new = finish(
        where, coef, terms, flipped(terms, 1), coarse, chip_part, near_part
    )
    return corrected[None], coarse_new[None]


def solution(mesh):
    times, slabs = mesh.devices.shape
    places = 8 if times >= 16 else 2
    shape = (times // places, places, slabs // 2, 2)
    time, slab = AXES[:2], AXES[2:]
    return jax.shard_map(
        per_device,
        mesh=Mesh(mesh.devices.reshape(shape), AXES),
        in_specs=(P(time, slab), P(time, slab), P(None, slab), P(slab)),
        out_specs=(P(time, slab), P(time)),
        check_vma=False,
    )
```

```python
import functools

import jax
import jax.numpy as jnp
from jax import lax
from jax.experimental import pallas as pl
from jax.experimental.pallas import tpu as pltpu
from jax.sharding import Mesh
from jax.sharding import PartitionSpec as P

STEPS = 8
WIDE = 4
THIN = WIDE - 1
DEPTH = 8
STAIRS = 4
KNOWN = 2
CHIP_COUNTS = (5, 5, 4)
NEAR_COUNTS = (7, 7)
AXES = ("group", "place", "chip", "core")
DIFFUSION_FINE = 0.15
DIFFUSION_COARSE = 0.0375
HIGH = lax.Precision.HIGHEST
HBM = pl.BlockSpec(memory_space=pltpu.HBM)
SMEM = pl.BlockSpec(memory_space=pltpu.SMEM)
VMEM = pl.BlockSpec(memory_space=pltpu.VMEM)
PARAMS = pltpu.CompilerParams(vmem_limit_bytes=24 * 2**20)


def f32(*shape):
    return jax.ShapeDtypeStruct(shape, jnp.float32)


def call(kernel, name, outs, in_specs, args, scratch=(), out_specs=None):
    return pl.pallas_call(
        kernel,
        out_shape=outs,
        in_specs=in_specs,
        out_specs=out_specs or ((VMEM,) * len(outs) if isinstance(outs, tuple) else VMEM),
        scratch_shapes=list(scratch),
        compiler_params=PARAMS,
        name=name,
        cost_estimate=pl.CostEstimate(flops=1, bytes_accessed=1, transcendentals=0),
    )(*args)


def layer_of(odd, c):
    return jnp.where(odd == 1, c, DEPTH - 1 - c)


def places_of(refs, counts):
    return [(ref, at) for ref, count in zip(refs, counts) for at in range(count)]


def halo_coefs(refs, counts, h):
    places = places_of(refs, counts)[STAIRS + h :: KNOWN]
    return [(ref, (at,)) for ref, at in places]


def pack_kernel(to_chip, where, adj, force, vel, upt, *refs):
    counts = CHIP_COUNTS if to_chip else NEAR_COUNTS
    outs, (edge, coefs, state, sem) = refs[: len(counts)], refs[len(counts) :]
    places = [ref.at[at] for ref, at in places_of(outs, counts)]
    odd = lax.rem(where[0], 2)
    sign = jnp.where(odd == 1, 1.0, -1.0) * (1.0 if to_chip else -1.0)
    layers = [layer_of(odd, i if to_chip else DEPTH - 1 - i) for i in range(WIDE)]
    copies = []

    def add(src, dst):
        copies.append(pltpu.make_async_copy(src, dst, sem.at[len(copies)]))

    for i in range(WIDE):
        add(adj.at[layers[i]], edge.at[i])
    for part, ref in enumerate((force, upt, vel.at[0], vel.at[1], vel.at[2])):
        for h in range(KNOWN):
            add(ref.at[layers[h]], places[STAIRS + part * KNOWN + h])
        add(ref.at[layers[KNOWN]], coefs.at[part])
    for copy in copies:
        copy.start()
    zero_pads(state)
    for copy in copies:
        copy.wait()
    for i in range(WIDE):
        put_layer(state, 0, i, edge[i])
    outs[0][0] = edge[0]
    outs[0][1] = edge[1]
    third = [(coefs, (part,)) for part in range(5)]
    put_stairs(state, (halo_coefs(outs, counts, 1), third), sign, outs[0], (1, 2))


def put_stairs(state, coefs, sign, out, centers):
    for which in range(2):

        def put(block, t, value, which=which):
            out[2 + which, pl.ds(8 * block, 8), pl.ds(128 * t, 128)] = value

        layer_step(state, 0, centers[which], coefs[which], sign, put)


def pack(to_chip, where, *arrays):
    _, rows, cols = arrays[0].shape
    arrays = [pltpu.with_memory_space_constraint(x, pltpu.HBM) for x in arrays]
    counts = CHIP_COUNTS if to_chip else NEAR_COUNTS
    return call(
        functools.partial(pack_kernel, to_chip),
        "pack_chip" if to_chip else "pack_near",
        tuple(f32(count, rows, cols) for count in counts),
        [SMEM] + [HBM] * 4,
        (where, *arrays),
        [
            pltpu.VMEM((WIDE, rows, cols), jnp.float32),
            pltpu.VMEM((5, rows, cols), jnp.float32),
            pltpu.VMEM((1, WIDE, cols // 128, rows + 16, 128), jnp.float32),
            pltpu.SemaphoreType.DMA((WIDE + 5 * (KNOWN + 1),)),
        ],
    )


def groups_of_four(rows, cols, value):
    i = lax.broadcasted_iota(jnp.int32, (rows, cols), 0)
    j = lax.broadcasted_iota(jnp.int32, (rows, cols), 1)
    if rows > cols:
        i = lax.shift_right_logical(i, 2)
    else:
        j = lax.shift_right_logical(j, 2)
    return jnp.where(i == j, value, 0.0)


def put_tiles(summed, first, value):
    for t in range(summed.shape[0]):
        summed[t, pl.ds(first, value.shape[0])] = value[:, 128 * t : 128 * (t + 1)]


def restrict_summed(summed):
    tiles, rows, lanes = summed.shape
    down = []
    for t in range(tiles):
        parts = [summed[t, pl.ds(k, rows // 4, 4)] for k in range(4)]
        down.append((parts[0] + parts[1]) + (parts[2] + parts[3]))
    average = groups_of_four(tiles * lanes, tiles * lanes // 4, 1.0 / 64.0)
    return jnp.dot(jnp.concatenate(down, axis=1), average, precision=HIGH)


def restrict_kernel(adj, vel, upt, out, sums):
    rows = adj.shape[1]
    count = 0
    for read in (
        lambda z: adj[z],
        lambda z: vel[0, z],
        lambda z: vel[1, z],
        lambda z: vel[2, z],
        lambda z: upt[z],
    ):
        for z in range(0, DEPTH, 4):
            put_tiles(sums, count, (read(z) + read(z + 1)) + (read(z + 2) + read(z + 3)))
            count += rows
    out[...] = restrict_summed(sums).reshape(out.shape)


def restrict_inputs(adj, vel, upt):
    depth, rows, cols = adj.shape
    return call(
        restrict_kernel,
        "restrict",
        f32(5 * depth // 4, rows // 4, cols // 4),
        [VMEM] * 3,
        (adj, vel, upt),
        [pltpu.VMEM((cols // 128, 5 * depth // 4 * rows, 128), jnp.float32)],
    )


def layer_step(state, now, i, coefs, sign, put):
    tiles, rows = state.shape[2], state.shape[3] - 16
    lane = lax.broadcasted_iota(jnp.int32, (8, 128), 1)
    first_lane, last_lane = lane == 0, lane == 127
    zero = jnp.zeros((8, 128), jnp.float32)
    for block in range(rows // 8):
        y = 8 + 8 * block
        mid = [state[now, i, t, pl.ds(y, 8)] for t in range(tiles)]
        ahead = [pltpu.roll(m, 127, 1) for m in mid]
        behind = [pltpu.roll(m, 1, 1) for m in mid]
        for t in range(tiles):
            xp = jnp.where(last_lane, ahead[t + 1] if t + 1 < tiles else zero, ahead[t])
            xm = jnp.where(first_lane, behind[t - 1] if t else zero, behind[t])
            zp = state[now, i + 1, t, pl.ds(y, 8)]
            zm = state[now, i - 1, t, pl.ds(y, 8)]
            yp = state[now, i, t, pl.ds(y + 1, 8)]
            ym = state[now, i, t, pl.ds(y - 1, 8)]
            at = (pl.ds(8 * block, 8), pl.ds(128 * t, 128))
            force, upt, vz, vy, vx = (ref[index + at] for ref, index in coefs)
            spread = ((zp + zm) + (yp + ym)) + (xp + xm)
            carried = vz * (sign * (zp - zm)) + vy * (yp - ym) + vx * (xp - xm)
            kept = ((1.0 - 6.0 * DIFFUSION_FINE) - upt) * mid[t]
            put(block, t, (DIFFUSION_FINE * spread + 0.5 * carried) + (kept + force))


def zero_pads(state):
    count, layers, tiles, rows, lanes = state.shape
    for edge in (0, rows - 8):
        state[:, :, :, pl.ds(edge, 8)] = jnp.zeros((count, layers, tiles, 8, lanes), jnp.float32)


def put_layer(state, which, i, value):
    rows = value.shape[0]
    for t in range(state.shape[2]):
        state[which, i, t, pl.ds(8, rows)] = value[:, 128 * t : 128 * (t + 1)]


def own_coefs(odd, force, vel, upt, c):
    z = layer_of(odd, c)
    return [(force, (z,)), (upt, (z,)), (vel, (0, z)), (vel, (1, z)), (vel, (2, z))]


def inner_kernel(last, where, force, vel, upt, *refs):
    begin = 2 if last else 1
    own, halo = refs[:begin], refs[begin]
    chip, refs = refs[begin + 1 :][: len(CHIP_COUNTS)], refs[begin + 1 + len(CHIP_COUNTS) :]
    if last:
        edge, out, coarse, state, summed = refs
    else:
        edge, out, ahead, state = refs
    odd = lax.rem(where[0], 2)
    sign = jnp.where(odd == 1, 1.0, -1.0)
    zero_pads(state)
    put_layer(state, 0, WIDE - 1, halo[0])
    put_layer(state, 0, WIDE - 2, halo[1])
    for c in range(DEPTH):
        value = own[c // WIDE][c % WIDE] if last else own[0][layer_of(odd, c)]
        put_layer(state, 0, WIDE + c, value)
        if c >= DEPTH - 2:
            edge[0, c - (DEPTH - 2)] = value
    for step in range(1, WIDE + 1):
        now, later = (step - 1) % 2, step % 2
        if step == 2:
            put_layer(state, now, WIDE - 2, halo[2])
            put_layer(state, now, WIDE - 3, halo[3])
        for c in range(-min(step, WIDE - step), DEPTH - step):
            if c < 0:
                coefs = halo_coefs(chip, CHIP_COUNTS, -c - 1)
            else:
                coefs = own_coefs(odd, force, vel, upt, c)

            def put(block, t, value, c=c, step=step, later=later):
                at = (pl.ds(8 * block, 8), pl.ds(128 * t, 128))
                if step == WIDE:
                    out[(c,) + at] = value
                if step < WIDE or not last:
                    state[later, WIDE + c, t, pl.ds(8 + 8 * block, 8)] = value
                if step < WIDE and c >= DEPTH - 2 - step:
                    edge[(step, c - (DEPTH - 2 - step)) + at] = value

            layer_step(state, now, WIDE + c, coefs, sign, put)
    if not last:
        ahead[0] = out[0]
        ahead[1] = out[1]
        coefs = [own_coefs(odd, force, vel, upt, c) for c in (1, 2)]
        put_stairs(state, coefs, sign, ahead, (WIDE + 1, WIDE + 2))
    if last:
        put_tiles(summed, 0, (out[0] + out[1]) + (out[2] + out[3]))
        coarse[...] = restrict_summed(summed)


def inner(last, where, force, vel, upt, own, halo, chip):
    _, rows, cols = force.shape
    outs = (f32(WIDE, 2, rows, cols), f32(WIDE, rows, cols))
    if not last:
        outs += (f32(STAIRS, rows, cols),)
    scratch = [pltpu.VMEM((2, DEPTH + WIDE, cols // 128, rows + 16, 128), jnp.float32)]
    if last:
        outs += (f32(rows // 4, cols // 4),)
        scratch.append(pltpu.VMEM((cols // 128, rows, 128), jnp.float32))
    return call(
        functools.partial(inner_kernel, last),
        "inner_last" if last else "inner_first",
        outs,
        [SMEM] + [VMEM] * (4 + len(own) + len(chip)),
        (where, force, vel, upt, *own, halo, *chip),
        scratch,
    )


def wedge_kernel(last, where, force, vel, upt, edge, halo, near, near_rest, *refs):
    if last:
        coarse_chip, stepped, out, begun, coarse, state, summed = refs
    else:
        out, ahead, state = refs
    slab = where[0]
    odd = lax.rem(slab, 2)
    sign = jnp.where(odd == 1, 1.0, -1.0)
    alive = jnp.where(jnp.logical_or(slab == 1, slab == 2), 1.0, 0.0)
    zero_pads(state)
    put_layer(state, 0, 2, halo[0])
    put_layer(state, 0, 3, halo[1])
    for step in range(1, WIDE + 1):
        now, later = (step - 1) % 2, step % 2
        for i in range(2):
            put_layer(state, now, i, edge[step - 1, i])
        if step == 2:
            put_layer(state, now, 4, halo[2])
            put_layer(state, now, 5, halo[3])
        for j in range(2 if step == 1 else WIDE):
            c = DEPTH - step + j
            if c < DEPTH:
                coefs = own_coefs(odd, force, vel, upt, c)
            else:
                coefs = halo_coefs((near, near_rest), NEAR_COUNTS, c - DEPTH)

            def put(block, t, value, c=c, j=j, step=step, later=later):
                if c >= DEPTH:
                    value = value * alive
                if step == WIDE:
                    out[j, pl.ds(8 * block, 8), pl.ds(128 * t, 128)] = value
                if step < WIDE or not last:
                    state[later, 2 + j, t, pl.ds(8 + 8 * block, 8)] = value

            layer_step(state, now, 1 + j, coefs, sign, put)
    if not last:
        ahead[0] = out[WIDE - 1]
        ahead[1] = out[WIDE - 2]
        coefs = [own_coefs(odd, force, vel, upt, c) for c in (DEPTH - 2, DEPTH - 3)]
        put_stairs(state, coefs, sign, ahead, (WIDE, WIDE - 1))
    if last:
        put_tiles(summed, 0, (out[0] + out[1]) + (out[2] + out[3]))
        near_coarse = restrict_summed(summed)
        chip_coarse = coarse_chip[...]
        coarse[0] = jnp.where(odd == 1, chip_coarse, near_coarse)
        coarse[1] = jnp.where(odd == 1, near_coarse, chip_coarse)
        kept = jnp.where(where[1] == 1, 0.0, 1.0)
        part = coarse[...] - kept * stepped[pl.ds(2 * slab, 2)]
        for copy in range(begun.shape[0]):
            begun[copy] = part


def wedge(last, where, force, vel, upt, edge, halo, near, near_rest, more=(), copies=0):
    _, rows, cols = force.shape
    outs = (f32(WIDE, rows, cols),)
    if not last:
        outs += (f32(STAIRS, rows, cols),)
    scratch = [pltpu.VMEM((2, WIDE + 2, cols // 128, rows + 16, 128), jnp.float32)]
    if last:
        outs += (f32(copies, 2, rows // 4, cols // 4), f32(2, rows // 4, cols // 4))
        scratch.append(pltpu.VMEM((cols // 128, rows, 128), jnp.float32))
    return call(
        functools.partial(wedge_kernel, last),
        "wedge_last" if last else "wedge_first",
        outs,
        [SMEM] + [VMEM] * (7 + len(more)),
        (where, force, vel, upt, edge, halo, near, near_rest) + more,
        scratch,
    )


NEIGHBOURS = ((0, 0, 0), (1, 0, 0), (-1, 0, 0), (0, 1, 0), (0, -1, 0), (0, 0, 1), (0, 0, -1))
STENCIL = sorted({tuple(a + b for a, b in zip(p, q)) for p in NEIGHBOURS for q in NEIGHBOURS})


def shifted(field, offset):
    dz, dy, dx = offset
    if dz:
        field = jnp.concatenate([field[dz:], field[:dz]], axis=0)
    for axis, by in ((1, dy), (2, dx)):
        if by:
            size = field.shape[axis]
            field = pltpu.roll(field, (size - by) % size, axis)
    return field


def coarse_step(field, coef):
    depth = len(field)
    rows, cols = field[0].shape
    moved = {0: field}
    for dy in (-2, -1, 1, 2):
        moved[dy] = [pltpu.roll(c, (rows - dy) % rows, 0) for c in field]

    def part(dx, z):
        total = None
        for k, offset in enumerate(STENCIL):
            if offset[2] != dx or not 0 <= z + offset[0] < depth:
                continue
            term = coef[k, z] * moved[offset[1]][z + offset[0]]
            total = term if total is None else total + term
        return total

    sides = []
    for z in range(depth):
        sides.append([pltpu.roll(part(dx, z), (cols - dx) % cols, 1) for dx in (-2, 2, -1, 1)])
    return [part(0, z) + ((s[0] + s[1]) + (s[2] + s[3])) for z, s in enumerate(sides)]


def prepare_kernel(where, own, one, pair, coef, stepped, whole):
    slab = where[0]
    size = own.shape[0]
    depth = size // 5
    parts = (own, one, pair.at[pl.ds(0, size)], pair.at[pl.ds(size, size)])
    for flip, ref in enumerate(parts):
        first = lax.bitwise_xor(slab, flip) * depth
        for part in range(5):
            whole[part, pl.ds(first, depth)] = ref[pl.ds(part * depth, depth)]
    full = whole.shape[1:]
    half = {NEIGHBOURS[0]: (1.0 - 6.0 * DIFFUSION_COARSE) - 4.0 * whole[4]}
    for dim in range(3):
        v = whole[1 + dim]
        half[NEIGHBOURS[0]] -= jnp.abs(v)
        at = lax.broadcasted_iota(jnp.int32, full, dim)
        plus = DIFFUSION_COARSE + jnp.maximum(v, 0.0)
        minus = DIFFUSION_COARSE - jnp.minimum(v, 0.0)
        half[NEIGHBOURS[1 + 2 * dim]] = jnp.where(at == full[dim] - 1, 0.0, plus)
        half[NEIGHBOURS[2 + 2 * dim]] = jnp.where(at == 0, 0.0, minus)
    both = {}
    for p in NEIGHBOURS:
        for q in NEIGHBOURS:
            offset = tuple(a + b for a, b in zip(p, q))
            term = half[p] * shifted(half[q], p)
            both[offset] = both[offset] + term if offset in both else term
    for k, offset in enumerate(STENCIL):
        coef[k] = shifted(both[offset], (0, 0, -offset[2]))
    field = coarse_step([whole[0, z] for z in range(full[0])], coef)
    for z in range(full[0]):
        stepped[z] = field[z]


def prepare(where, parts):
    depth5, rows, cols = parts[0].shape
    full = (4 * depth5 // 5, rows, cols)
    return call(
        prepare_kernel,
        "prepare",
        (f32(len(STENCIL), *full), f32(*full)),
        [SMEM] + [VMEM] * 3,
        (where, *parts),
        [pltpu.VMEM((5,) + full, jnp.float32)],
    )


def outer_kernel(where, coef, own, other, out, whole, ends):
    slab, group, place = where[0], where[2], where[3]
    core = lax.rem(slab, 2)
    targets, half = out.shape[:2]
    count, depth = whole.shape[:2]
    chips = own.shape[0] // count
    part = own.shape[1]
    for g in range(count):
        for chip in range(chips):
            here = 2 * chip + core
            there = 2 * chip + 1 - core
            whole[g, pl.ds(here * part, part)] = own[g * chips + chip]
            whole[g, pl.ds(there * part, part)] = other[g * chips + chip]

    def keep(which, layers):
        for z in range(depth):
            ends[which, z] = layers[z]

    def body(i, layers):
        keep(1, layers)
        layers = list(layers)
        for _ in range(targets):
            layers = coarse_step(layers, coef)
        return tuple(layers[z] + whole[count - 2 - i, z] for z in range(depth))

    ends[1] = jnp.zeros(ends.shape[1:], jnp.float32)
    field = tuple(whole[count - 1, z] for z in range(depth))
    keep(0, lax.fori_loop(0, count - 1 - group, body, field))
    for target in range(targets):
        out[target] = ends[jnp.where(place >= target, 0, 1), pl.ds(core * half, half)]


def outer(targets, where, coef, own, other):
    full = coef.shape[1:]
    depth, rows, cols = full
    count = own.shape[0] * own.shape[1] * 2 // depth
    return call(
        outer_kernel,
        "outer",
        f32(targets, depth // 2, rows, cols),
        [SMEM] + [VMEM] * 3,
        (where, coef, own, other),
        [pltpu.VMEM((count,) + full, jnp.float32), pltpu.VMEM((2,) + full, jnp.float32)],
    )


def finish_kernel(where, coef, own, other, coarse, chip_part, near_part, *refs):
    corrected, coarse_new, whole, down = refs
    slab, place = where[0], where[3]
    odd = lax.rem(slab, 2)
    count, depth = whole.shape[:2]
    half = depth // 2
    for t in range(count):
        whole[t, pl.ds(odd * half, half)] = own[t]
        whole[t, pl.ds((1 - odd) * half, half)] = other[t]

    def term(j):
        return whole.at[lax.rem(place + j, count)]

    def body(i, layers):
        stepped = coarse_step(list(layers), coef)
        added = term(count - 2 - i)
        return tuple(stepped[z] + added[z] for z in range(depth))

    first = term(count - 1)
    field = lax.fori_loop(0, count - 1, body, tuple(first[z] for z in range(depth)))
    for z in range(depth):
        coarse_new[z] = field[z]
    rows, cols = chip_part.shape[1:]
    part = (coarse_new[pl.ds(2 * slab, 2)] - coarse[...]).reshape(rows // 2, cols // 4)
    for row in range(rows // 2):
        down[pl.ds(4 * row, 4)] = jnp.broadcast_to(part[row : row + 1], (4, cols // 4))
    fine = jnp.dot(down[...], groups_of_four(cols // 4, cols, 1.0), precision=HIGH)
    lower, upper = fine[:rows], fine[rows:]
    chip_fine = jnp.where(odd == 1, lower, upper)
    near_fine = jnp.where(odd == 1, upper, lower)
    for c in range(DEPTH):
        z = jnp.where(odd == 1, c, DEPTH - 1 - c)
        corrected[z] = chip_part[c] + chip_fine if c < WIDE else near_part[c - WIDE] + near_fine


def finish(where, *args):
    _, rows, cols = args[-1].shape
    full = args[0].shape[1:]
    return call(
        finish_kernel,
        "finish",
        (f32(DEPTH, rows, cols), f32(*full)),
        [SMEM] + [VMEM] * len(args),
        (where, *args),
        [
            pltpu.VMEM(args[1].shape[:1] + full, jnp.float32),
            pltpu.VMEM((2 * rows, cols // 4), jnp.float32),
        ],
    )


def per_device(adjoint_end, forcing, velocity, uptake):
    adj, force = adjoint_end[0], forcing[0]
    groups, places, chips, cores = (lax.axis_size(axis) for axis in AXES)
    group, place, chip_no, core = (lax.axis_index(axis) for axis in AXES)
    times, slabs = groups * places, chips * cores
    slab = chip_no * cores + core
    last_slice = jnp.logical_and(group == groups - 1, place == places - 1)
    where = jnp.stack([slab, last_slice.astype(slab.dtype), group, place]).astype(jnp.int32)

    def send(array, pairs):
        route = [(t0 * slabs + s0, t1 * slabs + s1) for (t0, s0), (t1, s1) in pairs]
        return lax.ppermute(array, AXES, route)

    def flipped(array, flip):
        return send(array, [((t, s ^ flip), (t, s)) for t in range(times) for s in range(slabs)])

    def to_next_chip(array, shift=0):
        pairs = [(1, 2), (2, 1)]
        return send(
            array, [((t, a), ((t + shift) % times, b)) for t in range(times) for a, b in pairs]
        )

    own = (force, velocity, uptake)
    near_pack, rest_pack = pack(False, where, adj, *own)
    near = to_next_chip(near_pack)
    near_rest = to_next_chip(rest_pack, times // 2)
    restricted = restrict_inputs(adj, velocity, uptake)
    chip = [flipped(array, 1) for array in pack(True, where, adj, *own)]
    restricted_one = flipped(restricted, 1)
    pair = flipped(jnp.concatenate([restricted, restricted_one]), 2)
    edge, chip_part, ahead = inner(False, where, *own, (adj,), chip[0], chip)
    chip_halo = flipped(ahead, 1)
    near, near_rest, pair, edge = lax.optimization_barrier((near, near_rest, pair, edge))
    near_part, ahead = wedge(False, where, *own, edge, near, near, near_rest)
    near_halo = to_next_chip(ahead)
    edge, chip_part, coarse_chip = inner(True, where, *own, (chip_part, near_part), chip_halo, chip)
    coef, stepped = prepare(where, (restricted, restricted_one, pair))
    near_halo, edge, coef, stepped = lax.optimization_barrier((near_halo, edge, coef, stepped))
    near_part, begun, coarse = wedge(
        True, where, *own, edge, near_halo, near, near_rest, (coarse_chip, stepped), groups * chips
    )

    begun = lax.all_to_all(begun, ("group", "chip"), 0, 0)
    terms = outer(places, where, coef, begun, flipped(begun, 1))
    terms = lax.all_to_all(terms, "place", 0, 0)
    corrected, coarse_new = finish(
        where, coef, terms, flipped(terms, 1), coarse, chip_part, near_part
    )
    return corrected[None], coarse_new[None]


def solution(mesh):
    times, slabs = mesh.devices.shape
    places = 8 if times >= 16 else 2
    shape = (times // places, places, slabs // 2, 2)
    time, slab = AXES[:2], AXES[2:]
    return jax.shard_map(
        per_device,
        mesh=Mesh(mesh.devices.reshape(shape), AXES),
        in_specs=(P(time, slab), P(time, slab), P(None, slab), P(slab)),
        out_specs=(P(time, slab), P(time)),
        check_vma=False,
    )
```

```python
import functools

import jax
import jax.numpy as jnp
from jax import lax
from jax.experimental import pallas as pl
from jax.experimental.pallas import tpu as pltpu
from jax.sharding import Mesh
from jax.sharding import PartitionSpec as P

STEPS = 8
WIDE = 4
THIN = WIDE - 1
DEPTH = 8
STAIRS = 4
KNOWN = 2
CHIP_COUNTS = (5, 5, 4)
NEAR_COUNTS = (7, 7)
AXES = ("group", "place", "chip", "core")
DIFFUSION_FINE = 0.15
DIFFUSION_COARSE = 0.0375
HIGH = lax.Precision.HIGHEST
HBM = pl.BlockSpec(memory_space=pltpu.HBM)
SMEM = pl.BlockSpec(memory_space=pltpu.SMEM)
VMEM = pl.BlockSpec(memory_space=pltpu.VMEM)
PARAMS = pltpu.CompilerParams(vmem_limit_bytes=24 * 2**20)


def f32(*shape):
    return jax.ShapeDtypeStruct(shape, jnp.float32)


def call(kernel, name, outs, in_specs, args, scratch=(), out_specs=None):
    return pl.pallas_call(
        kernel,
        out_shape=outs,
        in_specs=in_specs,
        out_specs=out_specs or ((VMEM,) * len(outs) if isinstance(outs, tuple) else VMEM),
        scratch_shapes=list(scratch),
        compiler_params=PARAMS,
        name=name,
        cost_estimate=pl.CostEstimate(flops=1, bytes_accessed=1, transcendentals=0),
    )(*args)


def layer_of(odd, c):
    return jnp.where(odd == 1, c, DEPTH - 1 - c)


def places_of(refs, counts):
    return [(ref, at) for ref, count in zip(refs, counts) for at in range(count)]


def halo_coefs(refs, counts, h):
    places = places_of(refs, counts)[STAIRS + h :: KNOWN]
    return [(ref, (at,)) for ref, at in places]


def pack_near_kernel(where, adj, force, vel, upt, *refs):
    outs, (edge, coefs, state, sem) = refs[: len(NEAR_COUNTS)], refs[len(NEAR_COUNTS) :]
    places = [ref.at[at] for ref, at in places_of(outs, NEAR_COUNTS)]
    odd = lax.rem(where[0], 2)
    sign = jnp.where(odd == 1, -1.0, 1.0)
    layers = [layer_of(odd, DEPTH - 1 - i) for i in range(WIDE)]
    copies = []

    def add(src, dst):
        copies.append(pltpu.make_async_copy(src, dst, sem.at[len(copies)]))

    for i in range(WIDE):
        add(adj.at[layers[i]], edge.at[i])
    for part, ref in enumerate((force, upt, vel.at[0], vel.at[1], vel.at[2])):
        for h in range(KNOWN):
            add(ref.at[layers[h]], places[STAIRS + part * KNOWN + h])
        add(ref.at[layers[KNOWN]], coefs.at[part])
    for copy in copies:
        copy.start()
    zero_pads(state)
    for copy in copies:
        copy.wait()
    for i in range(WIDE):
        put_layer(state, 0, i, edge[i])
    outs[0][0] = edge[0]
    outs[0][1] = edge[1]
    third = [(coefs, (part,)) for part in range(5)]
    put_stairs(state, (halo_coefs(outs, NEAR_COUNTS, 1), third), sign, outs[0], (1, 2))


def pack_chip_kernel(where, adj, force, vel, upt, *refs):
    *outs, state = refs
    places = places_of(outs, CHIP_COUNTS)
    odd = lax.rem(where[0], 2)
    sign = jnp.where(odd == 1, 1.0, -1.0)
    zero_pads(state)
    for c in range(WIDE):
        put_layer(state, 0, c, adj[layer_of(odd, c)])
    for c in range(KNOWN):
        outs[0][c] = adj[layer_of(odd, c)]
        for part, (src, index) in enumerate(own_coefs(odd, force, vel, upt, c)):
            dst, at = places[STAIRS + part * KNOWN + c]
            dst[at] = src[index]
    coefs = [own_coefs(odd, force, vel, upt, c) for c in (1, 2)]
    put_stairs(state, coefs, sign, outs[0], (1, 2))


def put_stairs(state, coefs, sign, out, centers):
    for which in range(2):

        def put(block, t, value, which=which):
            out[2 + which, pl.ds(8 * block, 8), pl.ds(128 * t, 128)] = value

        layer_step(state, 0, centers[which], coefs[which], sign, put)


def pack(to_chip, where, *arrays):
    _, rows, cols = arrays[0].shape
    counts = CHIP_COUNTS if to_chip else NEAR_COUNTS
    scratch = [pltpu.VMEM((1, WIDE, cols // 128, rows + 16, 128), jnp.float32)]
    if not to_chip:
        arrays = [pltpu.with_memory_space_constraint(x, pltpu.HBM) for x in arrays]
        scratch = [
            pltpu.VMEM((WIDE, rows, cols), jnp.float32),
            pltpu.VMEM((5, rows, cols), jnp.float32),
            *scratch,
            pltpu.SemaphoreType.DMA((WIDE + 5 * (KNOWN + 1),)),
        ]
    return call(
        pack_chip_kernel if to_chip else pack_near_kernel,
        "pack_chip" if to_chip else "pack_near",
        tuple(f32(count, rows, cols) for count in counts),
        [SMEM] + [VMEM if to_chip else HBM] * 4,
        (where, *arrays),
        scratch,
    )


def groups_of_four(rows, cols, value):
    i = lax.broadcasted_iota(jnp.int32, (rows, cols), 0)
    j = lax.broadcasted_iota(jnp.int32, (rows, cols), 1)
    if rows > cols:
        i = lax.shift_right_logical(i, 2)
    else:
        j = lax.shift_right_logical(j, 2)
    return jnp.where(i == j, value, 0.0)


def put_tiles(summed, first, value):
    for t in range(summed.shape[0]):
        summed[t, pl.ds(first, value.shape[0])] = value[:, 128 * t : 128 * (t + 1)]


def restrict_summed(summed):
    tiles, rows, lanes = summed.shape
    down = []
    for t in range(tiles):
        parts = [summed[t, pl.ds(k, rows // 4, 4)] for k in range(4)]
        down.append((parts[0] + parts[1]) + (parts[2] + parts[3]))
    average = groups_of_four(tiles * lanes, tiles * lanes // 4, 1.0 / 64.0)
    return jnp.dot(jnp.concatenate(down, axis=1), average, precision=HIGH)


def restrict_kernel(adj, vel, upt, out, sums):
    rows = adj.shape[1]
    count = 0
    for read in (
        lambda z: adj[z],
        lambda z: vel[0, z],
        lambda z: vel[1, z],
        lambda z: vel[2, z],
        lambda z: upt[z],
    ):
        for z in range(0, DEPTH, 4):
            put_tiles(sums, count, (read(z) + read(z + 1)) + (read(z + 2) + read(z + 3)))
            count += rows
    out[...] = restrict_summed(sums).reshape(out.shape)


def restrict_inputs(adj, vel, upt):
    depth, rows, cols = adj.shape
    return call(
        restrict_kernel,
        "restrict",
        f32(5 * depth // 4, rows // 4, cols // 4),
        [VMEM] * 3,
        (adj, vel, upt),
        [pltpu.VMEM((cols // 128, 5 * depth // 4 * rows, 128), jnp.float32)],
    )


def layer_step(state, now, i, coefs, sign, put):
    tiles, rows = state.shape[2], state.shape[3] - 16
    lane = lax.broadcasted_iota(jnp.int32, (8, 128), 1)
    first_lane, last_lane = lane == 0, lane == 127
    zero = jnp.zeros((8, 128), jnp.float32)
    for block in range(rows // 8):
        y = 8 + 8 * block
        mid = [state[now, i, t, pl.ds(y, 8)] for t in range(tiles)]
        ahead = [pltpu.roll(m, 127, 1) for m in mid]
        behind = [pltpu.roll(m, 1, 1) for m in mid]
        for t in range(tiles):
            xp = jnp.where(last_lane, ahead[t + 1] if t + 1 < tiles else zero, ahead[t])
            xm = jnp.where(first_lane, behind[t - 1] if t else zero, behind[t])
            zp = state[now, i + 1, t, pl.ds(y, 8)]
            zm = state[now, i - 1, t, pl.ds(y, 8)]
            yp = state[now, i, t, pl.ds(y + 1, 8)]
            ym = state[now, i, t, pl.ds(y - 1, 8)]
            at = (pl.ds(8 * block, 8), pl.ds(128 * t, 128))
            force, upt, vz, vy, vx = (ref[index + at] for ref, index in coefs)
            spread = ((zp + zm) + (yp + ym)) + (xp + xm)
            carried = vz * (sign * (zp - zm)) + vy * (yp - ym) + vx * (xp - xm)
            kept = ((1.0 - 6.0 * DIFFUSION_FINE) - upt) * mid[t]
            put(block, t, (DIFFUSION_FINE * spread + 0.5 * carried) + (kept + force))


def zero_pads(state):
    count, layers, tiles, rows, lanes = state.shape
    for edge in (0, rows - 8):
        state[:, :, :, pl.ds(edge, 8)] = jnp.zeros((count, layers, tiles, 8, lanes), jnp.float32)


def put_layer(state, which, i, value):
    rows = value.shape[0]
    for t in range(state.shape[2]):
        state[which, i, t, pl.ds(8, rows)] = value[:, 128 * t : 128 * (t + 1)]


def own_coefs(odd, force, vel, upt, c):
    z = layer_of(odd, c)
    return [(force, (z,)), (upt, (z,)), (vel, (0, z)), (vel, (1, z)), (vel, (2, z))]


def inner_kernel(last, where, force, vel, upt, *refs):
    begin = 2 if last else 1
    own, halo = refs[:begin], refs[begin]
    chip, refs = refs[begin + 1 :][: len(CHIP_COUNTS)], refs[begin + 1 + len(CHIP_COUNTS) :]
    if last:
        edge, out, coarse, state, summed = refs
    else:
        edge, out, ahead, state = refs
    odd = lax.rem(where[0], 2)
    sign = jnp.where(odd == 1, 1.0, -1.0)
    zero_pads(state)
    put_layer(state, 0, WIDE - 1, halo[0])
    put_layer(state, 0, WIDE - 2, halo[1])
    for c in range(DEPTH):
        value = own[c // WIDE][c % WIDE] if last else own[0][layer_of(odd, c)]
        put_layer(state, 0, WIDE + c, value)
        if c >= DEPTH - 2:
            edge[0, c - (DEPTH - 2)] = value
    for step in range(1, WIDE + 1):
        now, later = (step - 1) % 2, step % 2
        if step == 2:
            put_layer(state, now, WIDE - 2, halo[2])
            put_layer(state, now, WIDE - 3, halo[3])
        for c in range(-min(step, WIDE - step), DEPTH - step):
            if c < 0:
                coefs = halo_coefs(chip, CHIP_COUNTS, -c - 1)
            else:
                coefs = own_coefs(odd, force, vel, upt, c)

            def put(block, t, value, c=c, step=step, later=later):
                at = (pl.ds(8 * block, 8), pl.ds(128 * t, 128))
                if step == WIDE:
                    out[(c,) + at] = value
                if step < WIDE or not last:
                    state[later, WIDE + c, t, pl.ds(8 + 8 * block, 8)] = value
                if step < WIDE and c >= DEPTH - 2 - step:
                    edge[(step, c - (DEPTH - 2 - step)) + at] = value

            layer_step(state, now, WIDE + c, coefs, sign, put)
    if not last:
        ahead[0] = out[0]
        ahead[1] = out[1]
        coefs = [own_coefs(odd, force, vel, upt, c) for c in (1, 2)]
        put_stairs(state, coefs, sign, ahead, (WIDE + 1, WIDE + 2))
    if last:
        put_tiles(summed, 0, (out[0] + out[1]) + (out[2] + out[3]))
        coarse[...] = restrict_summed(summed)


def inner(last, where, force, vel, upt, own, halo, chip):
    _, rows, cols = force.shape
    outs = (f32(WIDE, 2, rows, cols), f32(WIDE, rows, cols))
    if not last:
        outs += (f32(STAIRS, rows, cols),)
    scratch = [pltpu.VMEM((2, DEPTH + WIDE, cols // 128, rows + 16, 128), jnp.float32)]
    if last:
        outs += (f32(rows // 4, cols // 4),)
        scratch.append(pltpu.VMEM((cols // 128, rows, 128), jnp.float32))
    return call(
        functools.partial(inner_kernel, last),
        "inner_last" if last else "inner_first",
        outs,
        [SMEM] + [VMEM] * (4 + len(own) + len(chip)),
        (where, force, vel, upt, *own, halo, *chip),
        scratch,
    )


def wedge_kernel(last, where, force, vel, upt, edge, halo, near, near_rest, *refs):
    if last:
        coarse_chip, stepped, out, begun, coarse, state, summed = refs
    else:
        out, ahead, state = refs
    slab = where[0]
    odd = lax.rem(slab, 2)
    sign = jnp.where(odd == 1, 1.0, -1.0)
    alive = jnp.where(jnp.logical_or(slab == 1, slab == 2), 1.0, 0.0)
    zero_pads(state)
    put_layer(state, 0, 2, halo[0])
    put_layer(state, 0, 3, halo[1])
    for step in range(1, WIDE + 1):
        now, later = (step - 1) % 2, step % 2
        for i in range(2):
            put_layer(state, now, i, edge[step - 1, i])
        if step == 2:
            put_layer(state, now, 4, halo[2])
            put_layer(state, now, 5, halo[3])
        for j in range(2 if step == 1 else WIDE):
            c = DEPTH - step + j
            if c < DEPTH:
                coefs = own_coefs(odd, force, vel, upt, c)
            else:
                coefs = halo_coefs((near, near_rest), NEAR_COUNTS, c - DEPTH)

            def put(block, t, value, c=c, j=j, step=step, later=later):
                if c >= DEPTH:
                    value = value * alive
                if step == WIDE:
                    out[j, pl.ds(8 * block, 8), pl.ds(128 * t, 128)] = value
                if step < WIDE or not last:
                    state[later, 2 + j, t, pl.ds(8 + 8 * block, 8)] = value

            layer_step(state, now, 1 + j, coefs, sign, put)
    if not last:
        ahead[0] = out[WIDE - 1]
        ahead[1] = out[WIDE - 2]
        coefs = [own_coefs(odd, force, vel, upt, c) for c in (DEPTH - 2, DEPTH - 3)]
        put_stairs(state, coefs, sign, ahead, (WIDE, WIDE - 1))
    if last:
        put_tiles(summed, 0, (out[0] + out[1]) + (out[2] + out[3]))
        near_coarse = restrict_summed(summed)
        chip_coarse = coarse_chip[...]
        coarse[0] = jnp.where(odd == 1, chip_coarse, near_coarse)
        coarse[1] = jnp.where(odd == 1, near_coarse, chip_coarse)
        kept = jnp.where(where[1] == 1, 0.0, 1.0)
        part = coarse[...] - kept * stepped[pl.ds(2 * slab, 2)]
        for copy in range(begun.shape[0]):
            begun[copy] = part


def wedge(last, where, force, vel, upt, edge, halo, near, near_rest, more=(), copies=0):
    _, rows, cols = force.shape
    outs = (f32(WIDE, rows, cols),)
    if not last:
        outs += (f32(STAIRS, rows, cols),)
    scratch = [pltpu.VMEM((2, WIDE + 2, cols // 128, rows + 16, 128), jnp.float32)]
    if last:
        outs += (f32(copies, 2, rows // 4, cols // 4), f32(2, rows // 4, cols // 4))
        scratch.append(pltpu.VMEM((cols // 128, rows, 128), jnp.float32))
    return call(
        functools.partial(wedge_kernel, last),
        "wedge_last" if last else "wedge_first",
        outs,
        [SMEM] + [VMEM] * (7 + len(more)),
        (where, force, vel, upt, edge, halo, near, near_rest) + more,
        scratch,
    )


NEIGHBOURS = ((0, 0, 0), (1, 0, 0), (-1, 0, 0), (0, 1, 0), (0, -1, 0), (0, 0, 1), (0, 0, -1))
STENCIL = sorted({tuple(a + b for a, b in zip(p, q)) for p in NEIGHBOURS for q in NEIGHBOURS})


def shifted(field, offset):
    dz, dy, dx = offset
    if dz:
        field = jnp.concatenate([field[dz:], field[:dz]], axis=0)
    for axis, by in ((1, dy), (2, dx)):
        if by:
            size = field.shape[axis]
            field = pltpu.roll(field, (size - by) % size, axis)
    return field


def coarse_step(field, coef):
    depth = len(field)
    rows, cols = field[0].shape
    moved = {0: field}
    for dy in (-2, -1, 1, 2):
        moved[dy] = [pltpu.roll(c, (rows - dy) % rows, 0) for c in field]

    def part(dx, z):
        total = None
        for k, offset in enumerate(STENCIL):
            if offset[2] != dx or not 0 <= z + offset[0] < depth:
                continue
            term = coef[k, z] * moved[offset[1]][z + offset[0]]
            total = term if total is None else total + term
        return total

    sides = []
    for z in range(depth):
        sides.append([pltpu.roll(part(dx, z), (cols - dx) % cols, 1) for dx in (-2, 2, -1, 1)])
    return [part(0, z) + ((s[0] + s[1]) + (s[2] + s[3])) for z, s in enumerate(sides)]


def prepare_kernel(where, own, one, pair, coef, stepped, whole):
    slab = where[0]
    size = own.shape[0]
    depth = size // 5
    parts = (own, one, pair.at[pl.ds(0, size)], pair.at[pl.ds(size, size)])
    for flip, ref in enumerate(parts):
        first = lax.bitwise_xor(slab, flip) * depth
        for part in range(5):
            whole[part, pl.ds(first, depth)] = ref[pl.ds(part * depth, depth)]
    full = whole.shape[1:]
    half = {NEIGHBOURS[0]: (1.0 - 6.0 * DIFFUSION_COARSE) - 4.0 * whole[4]}
    for dim in range(3):
        v = whole[1 + dim]
        half[NEIGHBOURS[0]] -= jnp.abs(v)
        at = lax.broadcasted_iota(jnp.int32, full, dim)
        plus = DIFFUSION_COARSE + jnp.maximum(v, 0.0)
        minus = DIFFUSION_COARSE - jnp.minimum(v, 0.0)
        half[NEIGHBOURS[1 + 2 * dim]] = jnp.where(at == full[dim] - 1, 0.0, plus)
        half[NEIGHBOURS[2 + 2 * dim]] = jnp.where(at == 0, 0.0, minus)
    both = {}
    for p in NEIGHBOURS:
        for q in NEIGHBOURS:
            offset = tuple(a + b for a, b in zip(p, q))
            term = half[p] * shifted(half[q], p)
            both[offset] = both[offset] + term if offset in both else term
    for k, offset in enumerate(STENCIL):
        coef[k] = shifted(both[offset], (0, 0, -offset[2]))
    field = coarse_step([whole[0, z] for z in range(full[0])], coef)
    for z in range(full[0]):
        stepped[z] = field[z]


def prepare(where, parts):
    depth5, rows, cols = parts[0].shape
    full = (4 * depth5 // 5, rows, cols)
    return call(
        prepare_kernel,
        "prepare",
        (f32(len(STENCIL), *full), f32(*full)),
        [SMEM] + [VMEM] * 3,
        (where, *parts),
        [pltpu.VMEM((5,) + full, jnp.float32)],
    )


def outer_kernel(where, coef, own, other, out, whole, ends):
    slab, group, place = where[0], where[2], where[3]
    core = lax.rem(slab, 2)
    targets, half = out.shape[:2]
    count, depth = whole.shape[:2]
    chips = own.shape[0] // count
    part = own.shape[1]
    for g in range(count):
        for chip in range(chips):
            here = 2 * chip + core
            there = 2 * chip + 1 - core
            whole[g, pl.ds(here * part, part)] = own[g * chips + chip]
            whole[g, pl.ds(there * part, part)] = other[g * chips + chip]

    def keep(which, layers):
        for z in range(depth):
            ends[which, z] = layers[z]

    def body(i, layers):
        keep(1, layers)
        layers = list(layers)
        for _ in range(targets):
            layers = coarse_step(layers, coef)
        return tuple(layers[z] + whole[count - 2 - i, z] for z in range(depth))

    ends[1] = jnp.zeros(ends.shape[1:], jnp.float32)
    field = tuple(whole[count - 1, z] for z in range(depth))
    keep(0, lax.fori_loop(0, count - 1 - group, body, field))
    for target in range(targets):
        out[target] = ends[jnp.where(place >= target, 0, 1), pl.ds(core * half, half)]


def outer(targets, where, coef, own, other):
    full = coef.shape[1:]
    depth, rows, cols = full
    count = own.shape[0] * own.shape[1] * 2 // depth
    return call(
        outer_kernel,
        "outer",
        f32(targets, depth // 2, rows, cols),
        [SMEM] + [VMEM] * 3,
        (where, coef, own, other),
        [pltpu.VMEM((count,) + full, jnp.float32), pltpu.VMEM((2,) + full, jnp.float32)],
    )


def finish_kernel(where, coef, own, other, coarse, chip_part, near_part, *refs):
    corrected, coarse_new, whole, down = refs
    slab, place = where[0], where[3]
    odd = lax.rem(slab, 2)
    count, depth = whole.shape[:2]
    half = depth // 2
    for t in range(count):
        whole[t, pl.ds(odd * half, half)] = own[t]
        whole[t, pl.ds((1 - odd) * half, half)] = other[t]

    def term(j):
        return whole.at[lax.rem(place + j, count)]

    def body(i, layers):
        stepped = coarse_step(list(layers), coef)
        added = term(count - 2 - i)
        return tuple(stepped[z] + added[z] for z in range(depth))

    first = term(count - 1)
    field = lax.fori_loop(0, count - 1, body, tuple(first[z] for z in range(depth)))
    for z in range(depth):
        coarse_new[z] = field[z]
    rows, cols = chip_part.shape[1:]
    part = (coarse_new[pl.ds(2 * slab, 2)] - coarse[...]).reshape(rows // 2, cols // 4)
    for row in range(rows // 2):
        down[pl.ds(4 * row, 4)] = jnp.broadcast_to(part[row : row + 1], (4, cols // 4))
    fine = jnp.dot(down[...], groups_of_four(cols // 4, cols, 1.0), precision=HIGH)
    lower, upper = fine[:rows], fine[rows:]
    chip_fine = jnp.where(odd == 1, lower, upper)
    near_fine = jnp.where(odd == 1, upper, lower)
    for c in range(DEPTH):
        z = jnp.where(odd == 1, c, DEPTH - 1 - c)
        corrected[z] = chip_part[c] + chip_fine if c < WIDE else near_part[c - WIDE] + near_fine


def finish(where, *args):
    _, rows, cols = args[-1].shape
    full = args[0].shape[1:]
    return call(
        finish_kernel,
        "finish",
        (f32(DEPTH, rows, cols), f32(*full)),
        [SMEM] + [VMEM] * len(args),
        (where, *args),
        [
            pltpu.VMEM(args[1].shape[:1] + full, jnp.float32),
            pltpu.VMEM((2 * rows, cols // 4), jnp.float32),
        ],
    )


def per_device(adjoint_end, forcing, velocity, uptake):
    adj, force = adjoint_end[0], forcing[0]
    groups, places, chips, cores = (lax.axis_size(axis) for axis in AXES)
    group, place, chip_no, core = (lax.axis_index(axis) for axis in AXES)
    times, slabs = groups * places, chips * cores
    slab = chip_no * cores + core
    last_slice = jnp.logical_and(group == groups - 1, place == places - 1)
    where = jnp.stack([slab, last_slice.astype(slab.dtype), group, place]).astype(jnp.int32)

    def send(array, pairs):
        route = [(t0 * slabs + s0, t1 * slabs + s1) for (t0, s0), (t1, s1) in pairs]
        return lax.ppermute(array, AXES, route)

    def flipped(array, flip):
        return send(array, [((t, s ^ flip), (t, s)) for t in range(times) for s in range(slabs)])

    def to_next_chip(array, shift=0):
        pairs = [(1, 2), (2, 1)]
        return send(
            array, [((t, a), ((t + shift) % times, b)) for t in range(times) for a, b in pairs]
        )

    own = (force, velocity, uptake)
    near_pack, rest_pack = pack(False, where, adj, *own)
    near = to_next_chip(near_pack)
    near_rest = to_next_chip(rest_pack, times // 2)
    restricted = restrict_inputs(adj, velocity, uptake)
    chip = [flipped(array, 1) for array in pack(True, where, adj, *own)]
    restricted_one = flipped(restricted, 1)
    pair = flipped(jnp.concatenate([restricted, restricted_one]), 2)
    edge, chip_part, ahead = inner(False, where, *own, (adj,), chip[0], chip)
    chip_halo = flipped(ahead, 1)
    near, near_rest, pair, edge = lax.optimization_barrier((near, near_rest, pair, edge))
    near_part, ahead = wedge(False, where, *own, edge, near, near, near_rest)
    near_halo = to_next_chip(ahead)
    edge, chip_part, coarse_chip = inner(True, where, *own, (chip_part, near_part), chip_halo, chip)
    coef, stepped = prepare(where, (restricted, restricted_one, pair))
    near_halo, edge, coef, stepped = lax.optimization_barrier((near_halo, edge, coef, stepped))
    near_part, begun, coarse = wedge(
        True, where, *own, edge, near_halo, near, near_rest, (coarse_chip, stepped), groups * chips
    )

    begun = lax.all_to_all(begun, ("group", "chip"), 0, 0)
    terms = outer(places, where, coef, begun, flipped(begun, 1))
    terms = lax.all_to_all(terms, "place", 0, 0)
    corrected, coarse_new = finish(
        where, coef, terms, flipped(terms, 1), coarse, chip_part, near_part
    )
    return corrected[None], coarse_new[None]


def solution(mesh):
    times, slabs = mesh.devices.shape
    places = 8 if times >= 16 else 2
    shape = (times // places, places, slabs // 2, 2)
    time, slab = AXES[:2], AXES[2:]
    return jax.shard_map(
        per_device,
        mesh=Mesh(mesh.devices.reshape(shape), AXES),
        in_specs=(P(time, slab), P(time, slab), P(None, slab), P(slab)),
        out_specs=(P(time, slab), P(time)),
        check_vma=False,
    )
```

```python
import functools

import jax
import jax.numpy as jnp
from jax import lax
from jax.experimental import pallas as pl
from jax.experimental.pallas import tpu as pltpu
from jax.sharding import Mesh
from jax.sharding import PartitionSpec as P

STEPS = 8
WIDE = 4
THIN = WIDE - 1
DEPTH = 8
STAIRS = 4
KNOWN = 2
CHIP_COUNTS = (5, 5, 4)
NEAR_COUNTS = (8, 6)
AXES = ("group", "place", "chip", "core")
DIFFUSION_FINE = 0.15
DIFFUSION_COARSE = 0.0375
HIGH = lax.Precision.HIGHEST
HBM = pl.BlockSpec(memory_space=pltpu.HBM)
SMEM = pl.BlockSpec(memory_space=pltpu.SMEM)
VMEM = pl.BlockSpec(memory_space=pltpu.VMEM)
PARAMS = pltpu.CompilerParams(vmem_limit_bytes=24 * 2**20)


def f32(*shape):
    return jax.ShapeDtypeStruct(shape, jnp.float32)


def call(kernel, name, outs, in_specs, args, scratch=(), out_specs=None):
    return pl.pallas_call(
        kernel,
        out_shape=outs,
        in_specs=in_specs,
        out_specs=out_specs or ((VMEM,) * len(outs) if isinstance(outs, tuple) else VMEM),
        scratch_shapes=list(scratch),
        compiler_params=PARAMS,
        name=name,
        cost_estimate=pl.CostEstimate(flops=1, bytes_accessed=1, transcendentals=0),
    )(*args)


def layer_of(odd, c):
    return jnp.where(odd == 1, c, DEPTH - 1 - c)


def places_of(refs, counts):
    return [(ref, at) for ref, count in zip(refs, counts) for at in range(count)]


def halo_coefs(refs, counts, h):
    places = places_of(refs, counts)[STAIRS + h :: KNOWN]
    return [(ref, (at,)) for ref, at in places]


def pack_near_kernel(where, adj, force, vel, upt, *refs):
    outs, (edge, coefs, state, sem) = refs[: len(NEAR_COUNTS)], refs[len(NEAR_COUNTS) :]
    places = [ref.at[at] for ref, at in places_of(outs, NEAR_COUNTS)]
    odd = lax.rem(where[0], 2)
    sign = jnp.where(odd == 1, -1.0, 1.0)
    layers = [layer_of(odd, DEPTH - 1 - i) for i in range(WIDE)]
    copies = []

    def add(src, dst):
        copies.append(pltpu.make_async_copy(src, dst, sem.at[len(copies)]))

    for i in range(WIDE):
        add(adj.at[layers[i]], edge.at[i])
    for part, ref in enumerate((force, upt, vel.at[0], vel.at[1], vel.at[2])):
        for h in range(KNOWN):
            add(ref.at[layers[h]], places[STAIRS + part * KNOWN + h])
        add(ref.at[layers[KNOWN]], coefs.at[part])
    for copy in copies:
        copy.start()
    zero_pads(state)
    for copy in copies:
        copy.wait()
    for i in range(WIDE):
        put_layer(state, 0, i, edge[i])
    outs[0][0] = edge[0]
    outs[0][1] = edge[1]
    third = [(coefs, (part,)) for part in range(5)]
    put_stairs(state, (halo_coefs(outs, NEAR_COUNTS, 1), third), sign, outs[0], (1, 2))


def pack_chip_kernel(where, adj, force, vel, upt, *refs):
    *outs, state = refs
    places = places_of(outs, CHIP_COUNTS)
    odd = lax.rem(where[0], 2)
    sign = jnp.where(odd == 1, 1.0, -1.0)
    zero_pads(state)
    for c in range(WIDE):
        put_layer(state, 0, c, adj[layer_of(odd, c)])
    for c in range(KNOWN):
        outs[0][c] = adj[layer_of(odd, c)]
        for part, (src, index) in enumerate(own_coefs(odd, force, vel, upt, c)):
            dst, at = places[STAIRS + part * KNOWN + c]
            dst[at] = src[index]
    coefs = [own_coefs(odd, force, vel, upt, c) for c in (1, 2)]
    put_stairs(state, coefs, sign, outs[0], (1, 2))


def put_stairs(state, coefs, sign, out, centers):
    for which in range(2):

        def put(block, t, value, which=which):
            out[2 + which, pl.ds(8 * block, 8), pl.ds(128 * t, 128)] = value

        layer_step(state, 0, centers[which], coefs[which], sign, put)


def pack(to_chip, where, *arrays):
    _, rows, cols = arrays[0].shape
    counts = CHIP_COUNTS if to_chip else NEAR_COUNTS
    scratch = [pltpu.VMEM((1, WIDE, cols // 128, rows + 16, 128), jnp.float32)]
    if not to_chip:
        arrays = [pltpu.with_memory_space_constraint(x, pltpu.HBM) for x in arrays]
        scratch = [
            pltpu.VMEM((WIDE, rows, cols), jnp.float32),
            pltpu.VMEM((5, rows, cols), jnp.float32),
            *scratch,
            pltpu.SemaphoreType.DMA((WIDE + 5 * (KNOWN + 1),)),
        ]
    return call(
        pack_chip_kernel if to_chip else pack_near_kernel,
        "pack_chip" if to_chip else "pack_near",
        tuple(f32(count, rows, cols) for count in counts),
        [SMEM] + [VMEM if to_chip else HBM] * 4,
        (where, *arrays),
        scratch,
    )


def groups_of_four(rows, cols, value):
    i = lax.broadcasted_iota(jnp.int32, (rows, cols), 0)
    j = lax.broadcasted_iota(jnp.int32, (rows, cols), 1)
    if rows > cols:
        i = lax.shift_right_logical(i, 2)
    else:
        j = lax.shift_right_logical(j, 2)
    return jnp.where(i == j, value, 0.0)


def put_tiles(summed, first, value):
    for t in range(summed.shape[0]):
        summed[t, pl.ds(first, value.shape[0])] = value[:, 128 * t : 128 * (t + 1)]


def restrict_summed(summed):
    tiles, rows, lanes = summed.shape
    down = []
    for t in range(tiles):
        parts = [summed[t, pl.ds(k, rows // 4, 4)] for k in range(4)]
        down.append((parts[0] + parts[1]) + (parts[2] + parts[3]))
    average = groups_of_four(tiles * lanes, tiles * lanes // 4, 1.0 / 64.0)
    return jnp.dot(jnp.concatenate(down, axis=1), average, precision=HIGH)


def restrict_kernel(adj, vel, upt, out, sums):
    rows = adj.shape[1]
    count = 0
    for read in (
        lambda z: adj[z],
        lambda z: vel[0, z],
        lambda z: vel[1, z],
        lambda z: vel[2, z],
        lambda z: upt[z],
    ):
        for z in range(0, DEPTH, 4):
            put_tiles(sums, count, (read(z) + read(z + 1)) + (read(z + 2) + read(z + 3)))
            count += rows
    out[...] = restrict_summed(sums).reshape(out.shape)


def restrict_inputs(adj, vel, upt):
    depth, rows, cols = adj.shape
    return call(
        restrict_kernel,
        "restrict",
        f32(5 * depth // 4, rows // 4, cols // 4),
        [VMEM] * 3,
        (adj, vel, upt),
        [pltpu.VMEM((cols // 128, 5 * depth // 4 * rows, 128), jnp.float32)],
    )


def layer_step(state, now, i, coefs, sign, put):
    tiles, rows = state.shape[2], state.shape[3] - 16
    lane = lax.broadcasted_iota(jnp.int32, (8, 128), 1)
    first_lane, last_lane = lane == 0, lane == 127
    zero = jnp.zeros((8, 128), jnp.float32)
    for block in range(rows // 8):
        y = 8 + 8 * block
        mid = [state[now, i, t, pl.ds(y, 8)] for t in range(tiles)]
        ahead = [pltpu.roll(m, 127, 1) for m in mid]
        behind = [pltpu.roll(m, 1, 1) for m in mid]
        for t in range(tiles):
            xp = jnp.where(last_lane, ahead[t + 1] if t + 1 < tiles else zero, ahead[t])
            xm = jnp.where(first_lane, behind[t - 1] if t else zero, behind[t])
            zp = state[now, i + 1, t, pl.ds(y, 8)]
            zm = state[now, i - 1, t, pl.ds(y, 8)]
            yp = state[now, i, t, pl.ds(y + 1, 8)]
            ym = state[now, i, t, pl.ds(y - 1, 8)]
            at = (pl.ds(8 * block, 8), pl.ds(128 * t, 128))
            force, upt, vz, vy, vx = (ref[index + at] for ref, index in coefs)
            spread = ((zp + zm) + (yp + ym)) + (xp + xm)
            carried = vz * (sign * (zp - zm)) + vy * (yp - ym) + vx * (xp - xm)
            kept = ((1.0 - 6.0 * DIFFUSION_FINE) - upt) * mid[t]
            put(block, t, (DIFFUSION_FINE * spread + 0.5 * carried) + (kept + force))


def zero_pads(state):
    count, layers, tiles, rows, lanes = state.shape
    for edge in (0, rows - 8):
        state[:, :, :, pl.ds(edge, 8)] = jnp.zeros((count, layers, tiles, 8, lanes), jnp.float32)


def put_layer(state, which, i, value):
    rows = value.shape[0]
    for t in range(state.shape[2]):
        state[which, i, t, pl.ds(8, rows)] = value[:, 128 * t : 128 * (t + 1)]


def own_coefs(odd, force, vel, upt, c):
    z = layer_of(odd, c)
    return [(force, (z,)), (upt, (z,)), (vel, (0, z)), (vel, (1, z)), (vel, (2, z))]


def inner_kernel(last, where, force, vel, upt, *refs):
    begin = 2 if last else 1
    own, halo = refs[:begin], refs[begin]
    chip, refs = refs[begin + 1 :][: len(CHIP_COUNTS)], refs[begin + 1 + len(CHIP_COUNTS) :]
    if last:
        edge, out, coarse, state, summed = refs
    else:
        edge, out, ahead, state = refs
    odd = lax.rem(where[0], 2)
    sign = jnp.where(odd == 1, 1.0, -1.0)
    zero_pads(state)
    put_layer(state, 0, WIDE - 1, halo[0])
    put_layer(state, 0, WIDE - 2, halo[1])
    for c in range(DEPTH):
        value = own[c // WIDE][c % WIDE] if last else own[0][layer_of(odd, c)]
        put_layer(state, 0, WIDE + c, value)
        if c >= DEPTH - 2:
            edge[0, c - (DEPTH - 2)] = value
    for step in range(1, WIDE + 1):
        now, later = (step - 1) % 2, step % 2
        if step == 2:
            put_layer(state, now, WIDE - 2, halo[2])
            put_layer(state, now, WIDE - 3, halo[3])
        for c in range(-min(step, WIDE - step), DEPTH - step):
            if c < 0:
                coefs = halo_coefs(chip, CHIP_COUNTS, -c - 1)
            else:
                coefs = own_coefs(odd, force, vel, upt, c)

            def put(block, t, value, c=c, step=step, later=later):
                at = (pl.ds(8 * block, 8), pl.ds(128 * t, 128))
                if step == WIDE:
                    out[(c,) + at] = value
                if step < WIDE or not last:
                    state[later, WIDE + c, t, pl.ds(8 + 8 * block, 8)] = value
                if step < WIDE and c >= DEPTH - 2 - step:
                    edge[(step, c - (DEPTH - 2 - step)) + at] = value

            layer_step(state, now, WIDE + c, coefs, sign, put)
    if not last:
        ahead[0] = out[0]
        ahead[1] = out[1]
        coefs = [own_coefs(odd, force, vel, upt, c) for c in (1, 2)]
        put_stairs(state, coefs, sign, ahead, (WIDE + 1, WIDE + 2))
    if last:
        put_tiles(summed, 0, (out[0] + out[1]) + (out[2] + out[3]))
        coarse[...] = restrict_summed(summed)


def inner(last, where, force, vel, upt, own, halo, chip):
    _, rows, cols = force.shape
    outs = (f32(WIDE, 2, rows, cols), f32(WIDE, rows, cols))
    if not last:
        outs += (f32(STAIRS, rows, cols),)
    scratch = [pltpu.VMEM((2, DEPTH + WIDE, cols // 128, rows + 16, 128), jnp.float32)]
    if last:
        outs += (f32(rows // 4, cols // 4),)
        scratch.append(pltpu.VMEM((cols // 128, rows, 128), jnp.float32))
    return call(
        functools.partial(inner_kernel, last),
        "inner_last" if last else "inner_first",
        outs,
        [SMEM] + [VMEM] * (4 + len(own) + len(chip)),
        (where, force, vel, upt, *own, halo, *chip),
        scratch,
    )


def wedge_kernel(last, where, force, vel, upt, edge, halo, near, near_rest, *refs):
    if last:
        coarse_chip, stepped, out, begun, coarse, state, summed = refs
    else:
        out, ahead, state = refs
    slab = where[0]
    odd = lax.rem(slab, 2)
    sign = jnp.where(odd == 1, 1.0, -1.0)
    alive = jnp.where(jnp.logical_or(slab == 1, slab == 2), 1.0, 0.0)
    zero_pads(state)
    put_layer(state, 0, 2, halo[0])
    put_layer(state, 0, 3, halo[1])
    for step in range(1, WIDE + 1):
        now, later = (step - 1) % 2, step % 2
        for i in range(2):
            put_layer(state, now, i, edge[step - 1, i])
        if step == 2:
            put_layer(state, now, 4, halo[2])
            put_layer(state, now, 5, halo[3])
        for j in range(2 if step == 1 else WIDE):
            c = DEPTH - step + j
            if c < DEPTH:
                coefs = own_coefs(odd, force, vel, upt, c)
            else:
                coefs = halo_coefs((near, near_rest), NEAR_COUNTS, c - DEPTH)

            def put(block, t, value, c=c, j=j, step=step, later=later):
                if c >= DEPTH:
                    value = value * alive
                if step == WIDE:
                    out[j, pl.ds(8 * block, 8), pl.ds(128 * t, 128)] = value
                if step < WIDE or not last:
                    state[later, 2 + j, t, pl.ds(8 + 8 * block, 8)] = value

            layer_step(state, now, 1 + j, coefs, sign, put)
    if not last:
        ahead[0] = out[WIDE - 1]
        ahead[1] = out[WIDE - 2]
        coefs = [own_coefs(odd, force, vel, upt, c) for c in (DEPTH - 2, DEPTH - 3)]
        put_stairs(state, coefs, sign, ahead, (WIDE, WIDE - 1))
    if last:
        put_tiles(summed, 0, (out[0] + out[1]) + (out[2] + out[3]))
        near_coarse = restrict_summed(summed)
        chip_coarse = coarse_chip[...]
        coarse[0] = jnp.where(odd == 1, chip_coarse, near_coarse)
        coarse[1] = jnp.where(odd == 1, near_coarse, chip_coarse)
        kept = jnp.where(where[1] == 1, 0.0, 1.0)
        part = coarse[...] - kept * stepped[pl.ds(2 * slab, 2)]
        for copy in range(begun.shape[0]):
            begun[copy] = part


def wedge(last, where, force, vel, upt, edge, halo, near, near_rest, more=(), copies=0):
    _, rows, cols = force.shape
    outs = (f32(WIDE, rows, cols),)
    if not last:
        outs += (f32(STAIRS, rows, cols),)
    scratch = [pltpu.VMEM((2, WIDE + 2, cols // 128, rows + 16, 128), jnp.float32)]
    if last:
        outs += (f32(copies, 2, rows // 4, cols // 4), f32(2, rows // 4, cols // 4))
        scratch.append(pltpu.VMEM((cols // 128, rows, 128), jnp.float32))
    return call(
        functools.partial(wedge_kernel, last),
        "wedge_last" if last else "wedge_first",
        outs,
        [SMEM] + [VMEM] * (7 + len(more)),
        (where, force, vel, upt, edge, halo, near, near_rest) + more,
        scratch,
    )


NEIGHBOURS = ((0, 0, 0), (1, 0, 0), (-1, 0, 0), (0, 1, 0), (0, -1, 0), (0, 0, 1), (0, 0, -1))
STENCIL = sorted({tuple(a + b for a, b in zip(p, q)) for p in NEIGHBOURS for q in NEIGHBOURS})


def shifted(field, offset):
    dz, dy, dx = offset
    if dz:
        field = jnp.concatenate([field[dz:], field[:dz]], axis=0)
    for axis, by in ((1, dy), (2, dx)):
        if by:
            size = field.shape[axis]
            field = pltpu.roll(field, (size - by) % size, axis)
    return field


def coarse_step(field, coef):
    depth = len(field)
    rows, cols = field[0].shape
    moved = {0: field}
    for dy in (-2, -1, 1, 2):
        moved[dy] = [pltpu.roll(c, (rows - dy) % rows, 0) for c in field]

    def part(dx, z):
        total = None
        for k, offset in enumerate(STENCIL):
            if offset[2] != dx or not 0 <= z + offset[0] < depth:
                continue
            term = coef[k, z] * moved[offset[1]][z + offset[0]]
            total = term if total is None else total + term
        return total

    sides = []
    for z in range(depth):
        sides.append([pltpu.roll(part(dx, z), (cols - dx) % cols, 1) for dx in (-2, 2, -1, 1)])
    return [part(0, z) + ((s[0] + s[1]) + (s[2] + s[3])) for z, s in enumerate(sides)]


def prepare_kernel(where, own, one, pair, coef, stepped, whole):
    slab = where[0]
    size = own.shape[0]
    depth = size // 5
    parts = (own, one, pair.at[pl.ds(0, size)], pair.at[pl.ds(size, size)])
    for flip, ref in enumerate(parts):
        first = lax.bitwise_xor(slab, flip) * depth
        for part in range(5):
            whole[part, pl.ds(first, depth)] = ref[pl.ds(part * depth, depth)]
    full = whole.shape[1:]
    half = {NEIGHBOURS[0]: (1.0 - 6.0 * DIFFUSION_COARSE) - 4.0 * whole[4]}
    for dim in range(3):
        v = whole[1 + dim]
        half[NEIGHBOURS[0]] -= jnp.abs(v)
        at = lax.broadcasted_iota(jnp.int32, full, dim)
        plus = DIFFUSION_COARSE + jnp.maximum(v, 0.0)
        minus = DIFFUSION_COARSE - jnp.minimum(v, 0.0)
        half[NEIGHBOURS[1 + 2 * dim]] = jnp.where(at == full[dim] - 1, 0.0, plus)
        half[NEIGHBOURS[2 + 2 * dim]] = jnp.where(at == 0, 0.0, minus)
    both = {}
    for p in NEIGHBOURS:
        for q in NEIGHBOURS:
            offset = tuple(a + b for a, b in zip(p, q))
            term = half[p] * shifted(half[q], p)
            both[offset] = both[offset] + term if offset in both else term
    for k, offset in enumerate(STENCIL):
        coef[k] = shifted(both[offset], (0, 0, -offset[2]))
    field = coarse_step([whole[0, z] for z in range(full[0])], coef)
    for z in range(full[0]):
        stepped[z] = field[z]


def prepare(where, parts):
    depth5, rows, cols = parts[0].shape
    full = (4 * depth5 // 5, rows, cols)
    return call(
        prepare_kernel,
        "prepare",
        (f32(len(STENCIL), *full), f32(*full)),
        [SMEM] + [VMEM] * 3,
        (where, *parts),
        [pltpu.VMEM((5,) + full, jnp.float32)],
    )


def outer_kernel(where, coef, own, other, out, whole, ends):
    slab, group, place = where[0], where[2], where[3]
    core = lax.rem(slab, 2)
    targets, half = out.shape[:2]
    count, depth = whole.shape[:2]
    chips = own.shape[0] // count
    part = own.shape[1]
    for g in range(count):
        for chip in range(chips):
            here = 2 * chip + core
            there = 2 * chip + 1 - core
            whole[g, pl.ds(here * part, part)] = own[g * chips + chip]
            whole[g, pl.ds(there * part, part)] = other[g * chips + chip]

    def keep(which, layers):
        for z in range(depth):
            ends[which, z] = layers[z]

    def body(i, layers):
        keep(1, layers)
        layers = list(layers)
        for _ in range(targets):
            layers = coarse_step(layers, coef)
        return tuple(layers[z] + whole[count - 2 - i, z] for z in range(depth))

    ends[1] = jnp.zeros(ends.shape[1:], jnp.float32)
    field = tuple(whole[count - 1, z] for z in range(depth))
    keep(0, lax.fori_loop(0, count - 1 - group, body, field))
    for target in range(targets):
        out[target] = ends[jnp.where(place >= target, 0, 1), pl.ds(core * half, half)]


def outer(targets, where, coef, own, other):
    full = coef.shape[1:]
    depth, rows, cols = full
    count = own.shape[0] * own.shape[1] * 2 // depth
    return call(
        outer_kernel,
        "outer",
        f32(targets, depth // 2, rows, cols),
        [SMEM] + [VMEM] * 3,
        (where, coef, own, other),
        [pltpu.VMEM((count,) + full, jnp.float32), pltpu.VMEM((2,) + full, jnp.float32)],
    )


def finish_kernel(where, coef, own, other, coarse, chip_part, near_part, *refs):
    corrected, coarse_new, whole, down = refs
    slab, place = where[0], where[3]
    odd = lax.rem(slab, 2)
    count, depth = whole.shape[:2]
    half = depth // 2
    for t in range(count):
        whole[t, pl.ds(odd * half, half)] = own[t]
        whole[t, pl.ds((1 - odd) * half, half)] = other[t]

    def term(j):
        return whole.at[lax.rem(place + j, count)]

    def body(i, layers):
        stepped = coarse_step(list(layers), coef)
        added = term(count - 2 - i)
        return tuple(stepped[z] + added[z] for z in range(depth))

    first = term(count - 1)
    field = lax.fori_loop(0, count - 1, body, tuple(first[z] for z in range(depth)))
    for z in range(depth):
        coarse_new[z] = field[z]
    rows, cols = chip_part.shape[1:]
    part = (coarse_new[pl.ds(2 * slab, 2)] - coarse[...]).reshape(rows // 2, cols // 4)
    for row in range(rows // 2):
        down[pl.ds(4 * row, 4)] = jnp.broadcast_to(part[row : row + 1], (4, cols // 4))
    fine = jnp.dot(down[...], groups_of_four(cols // 4, cols, 1.0), precision=HIGH)
    lower, upper = fine[:rows], fine[rows:]
    chip_fine = jnp.where(odd == 1, lower, upper)
    near_fine = jnp.where(odd == 1, upper, lower)
    for c in range(DEPTH):
        z = jnp.where(odd == 1, c, DEPTH - 1 - c)
        corrected[z] = chip_part[c] + chip_fine if c < WIDE else near_part[c - WIDE] + near_fine


def finish(where, *args):
    _, rows, cols = args[-1].shape
    full = args[0].shape[1:]
    return call(
        finish_kernel,
        "finish",
        (f32(DEPTH, rows, cols), f32(*full)),
        [SMEM] + [VMEM] * len(args),
        (where, *args),
        [
            pltpu.VMEM(args[1].shape[:1] + full, jnp.float32),
            pltpu.VMEM((2 * rows, cols // 4), jnp.float32),
        ],
    )


def per_device(adjoint_end, forcing, velocity, uptake):
    adj, force = adjoint_end[0], forcing[0]
    groups, places, chips, cores = (lax.axis_size(axis) for axis in AXES)
    group, place, chip_no, core = (lax.axis_index(axis) for axis in AXES)
    times, slabs = groups * places, chips * cores
    slab = chip_no * cores + core
    last_slice = jnp.logical_and(group == groups - 1, place == places - 1)
    where = jnp.stack([slab, last_slice.astype(slab.dtype), group, place]).astype(jnp.int32)

    def send(array, pairs):
        route = [(t0 * slabs + s0, t1 * slabs + s1) for (t0, s0), (t1, s1) in pairs]
        return lax.ppermute(array, AXES, route)

    def flipped(array, flip):
        return send(array, [((t, s ^ flip), (t, s)) for t in range(times) for s in range(slabs)])

    def to_next_chip(array, shift=0):
        pairs = [(1, 2), (2, 1)]
        return send(
            array, [((t, a), ((t + shift) % times, b)) for t in range(times) for a, b in pairs]
        )

    own = (force, velocity, uptake)
    near_pack, rest_pack = pack(False, where, adj, *own)
    near = to_next_chip(near_pack)
    near_rest = to_next_chip(rest_pack, times // 2)
    restricted = restrict_inputs(adj, velocity, uptake)
    chip = [flipped(array, 1) for array in pack(True, where, adj, *own)]
    restricted_one = flipped(restricted, 1)
    pair = flipped(jnp.concatenate([restricted, restricted_one]), 2)
    edge, chip_part, ahead = inner(False, where, *own, (adj,), chip[0], chip)
    chip_halo = flipped(ahead, 1)
    near, near_rest, pair, edge = lax.optimization_barrier((near, near_rest, pair, edge))
    near_part, ahead = wedge(False, where, *own, edge, near, near, near_rest)
    near_halo = to_next_chip(ahead)
    edge, chip_part, coarse_chip = inner(True, where, *own, (chip_part, near_part), chip_halo, chip)
    coef, stepped = prepare(where, (restricted, restricted_one, pair))
    near_halo, edge, coef, stepped = lax.optimization_barrier((near_halo, edge, coef, stepped))
    near_part, begun, coarse = wedge(
        True, where, *own, edge, near_halo, near, near_rest, (coarse_chip, stepped), groups * chips
    )

    begun = lax.all_to_all(begun, ("group", "chip"), 0, 0)
    terms = outer(places, where, coef, begun, flipped(begun, 1))
    terms = lax.all_to_all(terms, "place", 0, 0)
    corrected, coarse_new = finish(
        where, coef, terms, flipped(terms, 1), coarse, chip_part, near_part
    )
    return corrected[None], coarse_new[None]


def solution(mesh):
    times, slabs = mesh.devices.shape
    places = 8 if times >= 16 else 2
    shape = (times // places, places, slabs // 2, 2)
    time, slab = AXES[:2], AXES[2:]
    return jax.shard_map(
        per_device,
        mesh=Mesh(mesh.devices.reshape(shape), AXES),
        in_specs=(P(time, slab), P(time, slab), P(None, slab), P(slab)),
        out_specs=(P(time, slab), P(time)),
        check_vma=False,
    )
```

```python
import functools

import jax
import jax.numpy as jnp
from jax import lax
from jax.experimental import pallas as pl
from jax.experimental.pallas import tpu as pltpu
from jax.sharding import Mesh
from jax.sharding import PartitionSpec as P

STEPS = 8
WIDE = 4
THIN = WIDE - 1
DEPTH = 8
STAIRS = 4
KNOWN = 2
CHIP_COUNTS = (5, 5, 4)
NEAR_COUNTS = (7, 7)
AXES = ("group", "place", "chip", "core")
DIFFUSION_FINE = 0.15
DIFFUSION_COARSE = 0.0375
HIGH = lax.Precision.HIGHEST
HBM = pl.BlockSpec(memory_space=pltpu.HBM)
SMEM = pl.BlockSpec(memory_space=pltpu.SMEM)
VMEM = pl.BlockSpec(memory_space=pltpu.VMEM)
PARAMS = pltpu.CompilerParams(vmem_limit_bytes=24 * 2**20)


def f32(*shape):
    return jax.ShapeDtypeStruct(shape, jnp.float32)


def call(kernel, name, outs, in_specs, args, scratch=(), out_specs=None):
    return pl.pallas_call(
        kernel,
        out_shape=outs,
        in_specs=in_specs,
        out_specs=out_specs or ((VMEM,) * len(outs) if isinstance(outs, tuple) else VMEM),
        scratch_shapes=list(scratch),
        compiler_params=PARAMS,
        name=name,
        cost_estimate=pl.CostEstimate(flops=1, bytes_accessed=1, transcendentals=0),
    )(*args)


def layer_of(odd, c):
    return jnp.where(odd == 1, c, DEPTH - 1 - c)


def places_of(refs, counts):
    return [(ref, at) for ref, count in zip(refs, counts) for at in range(count)]


def halo_coefs(refs, counts, h):
    places = places_of(refs, counts)[STAIRS + h :: KNOWN]
    return [(ref, (at,)) for ref, at in places]


def pack_near_kernel(where, adj, force, vel, upt, *refs):
    outs, (edge, coefs, state, sem) = refs[: len(NEAR_COUNTS)], refs[len(NEAR_COUNTS) :]
    places = [ref.at[at] for ref, at in places_of(outs, NEAR_COUNTS)]
    odd = lax.rem(where[0], 2)
    sign = jnp.where(odd == 1, -1.0, 1.0)
    layers = [layer_of(odd, DEPTH - 1 - i) for i in range(WIDE)]
    copies = []

    def add(src, dst):
        copies.append(pltpu.make_async_copy(src, dst, sem.at[len(copies)]))

    for i in range(WIDE):
        add(adj.at[layers[i]], edge.at[i])
    for part, ref in enumerate((force, upt, vel.at[0], vel.at[1], vel.at[2])):
        for h in range(KNOWN):
            add(ref.at[layers[h]], places[STAIRS + part * KNOWN + h])
        add(ref.at[layers[KNOWN]], coefs.at[part])
    for copy in copies:
        copy.start()
    zero_pads(state)
    for copy in copies:
        copy.wait()
    for i in range(WIDE):
        put_layer(state, 0, i, edge[i])
    outs[0][0] = edge[0]
    outs[0][1] = edge[1]
    third = [(coefs, (part,)) for part in range(5)]
    put_stairs(state, (halo_coefs(outs, NEAR_COUNTS, 1), third), sign, outs[0], (1, 2))


def pack_chip_kernel(where, adj, force, vel, upt, *refs):
    *outs, state = refs
    places = places_of(outs, CHIP_COUNTS)
    odd = lax.rem(where[0], 2)
    sign = jnp.where(odd == 1, 1.0, -1.0)
    zero_pads(state)
    for c in range(WIDE):
        put_layer(state, 0, c, adj[layer_of(odd, c)])
    for c in range(KNOWN):
        outs[0][c] = adj[layer_of(odd, c)]
        for part, (src, index) in enumerate(own_coefs(odd, force, vel, upt, c)):
            dst, at = places[STAIRS + part * KNOWN + c]
            dst[at] = src[index]
    coefs = [own_coefs(odd, force, vel, upt, c) for c in (1, 2)]
    put_stairs(state, coefs, sign, outs[0], (1, 2))


def put_stairs(state, coefs, sign, out, centers):
    for which in range(2):

        def put(block, t, value, which=which):
            out[2 + which, pl.ds(8 * block, 8), pl.ds(128 * t, 128)] = value

        layer_step(state, 0, centers[which], coefs[which], sign, put)


def pack(to_chip, where, *arrays):
    _, rows, cols = arrays[0].shape
    counts = CHIP_COUNTS if to_chip else NEAR_COUNTS
    scratch = [pltpu.VMEM((1, WIDE, cols // 128, rows + 16, 128), jnp.float32)]
    if not to_chip:
        arrays = [pltpu.with_memory_space_constraint(x, pltpu.HBM) for x in arrays]
        scratch = [
            pltpu.VMEM((WIDE, rows, cols), jnp.float32),
            pltpu.VMEM((5, rows, cols), jnp.float32),
            *scratch,
            pltpu.SemaphoreType.DMA((WIDE + 5 * (KNOWN + 1),)),
        ]
    return call(
        pack_chip_kernel if to_chip else pack_near_kernel,
        "pack_chip" if to_chip else "pack_near",
        tuple(f32(count, rows, cols) for count in counts),
        [SMEM] + [VMEM if to_chip else HBM] * 4,
        (where, *arrays),
        scratch,
    )


def groups_of_four(rows, cols, value):
    i = lax.broadcasted_iota(jnp.int32, (rows, cols), 0)
    j = lax.broadcasted_iota(jnp.int32, (rows, cols), 1)
    if rows > cols:
        i = lax.shift_right_logical(i, 2)
    else:
        j = lax.shift_right_logical(j, 2)
    return jnp.where(i == j, value, 0.0)


def put_tiles(summed, first, value):
    for t in range(summed.shape[0]):
        summed[t, pl.ds(first, value.shape[0])] = value[:, 128 * t : 128 * (t + 1)]


def restrict_summed(summed):
    tiles, rows, lanes = summed.shape
    down = []
    for t in range(tiles):
        parts = [summed[t, pl.ds(k, rows // 4, 4)] for k in range(4)]
        down.append((parts[0] + parts[1]) + (parts[2] + parts[3]))
    average = groups_of_four(tiles * lanes, tiles * lanes // 4, 1.0 / 64.0)
    return jnp.dot(jnp.concatenate(down, axis=1), average, precision=HIGH)


def restrict_kernel(adj, vel, upt, out, sums):
    rows = adj.shape[1]
    count = 0
    for read in (
        lambda z: adj[z],
        lambda z: vel[0, z],
        lambda z: vel[1, z],
        lambda z: vel[2, z],
        lambda z: upt[z],
    ):
        for z in range(0, DEPTH, 4):
            put_tiles(sums, count, (read(z) + read(z + 1)) + (read(z + 2) + read(z + 3)))
            count += rows
    out[...] = restrict_summed(sums).reshape(out.shape)


def restrict_inputs(adj, vel, upt):
    depth, rows, cols = adj.shape
    return call(
        restrict_kernel,
        "restrict",
        f32(5 * depth // 4, rows // 4, cols // 4),
        [VMEM] * 3,
        (adj, vel, upt),
        [pltpu.VMEM((cols // 128, 5 * depth // 4 * rows, 128), jnp.float32)],
    )


def layer_step(state, now, i, coefs, sign, put):
    tiles, rows = state.shape[2], state.shape[3] - 16
    lane = lax.broadcasted_iota(jnp.int32, (8, 128), 1)
    first_lane, last_lane = lane == 0, lane == 127
    zero = jnp.zeros((8, 128), jnp.float32)
    for block in range(rows // 8):
        y = 8 + 8 * block
        mid = [state[now, i, t, pl.ds(y, 8)] for t in range(tiles)]
        ahead = [pltpu.roll(m, 127, 1) for m in mid]
        behind = [pltpu.roll(m, 1, 1) for m in mid]
        for t in range(tiles):
            xp = jnp.where(last_lane, ahead[t + 1] if t + 1 < tiles else zero, ahead[t])
            xm = jnp.where(first_lane, behind[t - 1] if t else zero, behind[t])
            zp = state[now, i + 1, t, pl.ds(y, 8)]
            zm = state[now, i - 1, t, pl.ds(y, 8)]
            yp = state[now, i, t, pl.ds(y + 1, 8)]
            ym = state[now, i, t, pl.ds(y - 1, 8)]
            at = (pl.ds(8 * block, 8), pl.ds(128 * t, 128))
            force, upt, vz, vy, vx = (ref[index + at] for ref, index in coefs)
            spread = ((zp + zm) + (yp + ym)) + (xp + xm)
            carried = vz * (sign * (zp - zm)) + vy * (yp - ym) + vx * (xp - xm)
            kept = ((1.0 - 6.0 * DIFFUSION_FINE) - upt) * mid[t]
            put(block, t, (DIFFUSION_FINE * spread + 0.5 * carried) + (kept + force))


def zero_pads(state):
    count, layers, tiles, rows, lanes = state.shape
    for edge in (0, rows - 8):
        state[:, :, :, pl.ds(edge, 8)] = jnp.zeros((count, layers, tiles, 8, lanes), jnp.float32)


def put_layer(state, which, i, value):
    rows = value.shape[0]
    for t in range(state.shape[2]):
        state[which, i, t, pl.ds(8, rows)] = value[:, 128 * t : 128 * (t + 1)]


def own_coefs(odd, force, vel, upt, c):
    z = layer_of(odd, c)
    return [(force, (z,)), (upt, (z,)), (vel, (0, z)), (vel, (1, z)), (vel, (2, z))]


def inner_kernel(last, where, force, vel, upt, *refs):
    begin = 2 if last else 1
    own, halo = refs[:begin], refs[begin]
    chip, refs = refs[begin + 1 :][: len(CHIP_COUNTS)], refs[begin + 1 + len(CHIP_COUNTS) :]
    if last:
        edge, out, coarse, state, summed = refs
    else:
        edge, out, ahead, state = refs
    odd = lax.rem(where[0], 2)
    sign = jnp.where(odd == 1, 1.0, -1.0)
    zero_pads(state)
    put_layer(state, 0, WIDE - 1, halo[0])
    put_layer(state, 0, WIDE - 2, halo[1])
    for c in range(DEPTH):
        value = own[c // WIDE][c % WIDE] if last else own[0][layer_of(odd, c)]
        put_layer(state, 0, WIDE + c, value)
        if c >= DEPTH - 2:
            edge[0, c - (DEPTH - 2)] = value
    for step in range(1, WIDE + 1):
        now, later = (step - 1) % 2, step % 2
        if step == 2:
            put_layer(state, now, WIDE - 2, halo[2])
            put_layer(state, now, WIDE - 3, halo[3])
        for c in range(-min(step, WIDE - step), DEPTH - step):
            if c < 0:
                coefs = halo_coefs(chip, CHIP_COUNTS, -c - 1)
            else:
                coefs = own_coefs(odd, force, vel, upt, c)

            def put(block, t, value, c=c, step=step, later=later):
                at = (pl.ds(8 * block, 8), pl.ds(128 * t, 128))
                if step == WIDE:
                    out[(c,) + at] = value
                if step < WIDE or not last:
                    state[later, WIDE + c, t, pl.ds(8 + 8 * block, 8)] = value
                if step < WIDE and c >= DEPTH - 2 - step:
                    edge[(step, c - (DEPTH - 2 - step)) + at] = value

            layer_step(state, now, WIDE + c, coefs, sign, put)
    if not last:
        ahead[0] = out[0]
        ahead[1] = out[1]
        coefs = [own_coefs(odd, force, vel, upt, c) for c in (1, 2)]
        put_stairs(state, coefs, sign, ahead, (WIDE + 1, WIDE + 2))
    if last:
        put_tiles(summed, 0, (out[0] + out[1]) + (out[2] + out[3]))
        coarse[...] = restrict_summed(summed)


def inner(last, where, force, vel, upt, own, halo, chip):
    _, rows, cols = force.shape
    outs = (f32(WIDE, 2, rows, cols), f32(WIDE, rows, cols))
    if not last:
        outs += (f32(STAIRS, rows, cols),)
    scratch = [pltpu.VMEM((2, DEPTH + WIDE, cols // 128, rows + 16, 128), jnp.float32)]
    if last:
        outs += (f32(rows // 4, cols // 4),)
        scratch.append(pltpu.VMEM((cols // 128, rows, 128), jnp.float32))
    return call(
        functools.partial(inner_kernel, last),
        "inner_last" if last else "inner_first",
        outs,
        [SMEM] + [VMEM] * (4 + len(own) + len(chip)),
        (where, force, vel, upt, *own, halo, *chip),
        scratch,
    )


def wedge_kernel(last, where, force, vel, upt, edge, halo, near, near_rest, *refs):
    if last:
        coarse_chip, stepped, out, begun, coarse, state, summed = refs
    else:
        out, ahead, state = refs
    slab = where[0]
    odd = lax.rem(slab, 2)
    sign = jnp.where(odd == 1, 1.0, -1.0)
    alive = jnp.where(jnp.logical_or(slab == 1, slab == 2), 1.0, 0.0)
    zero_pads(state)
    put_layer(state, 0, 2, halo[0])
    put_layer(state, 0, 3, halo[1])
    for step in range(1, WIDE + 1):
        now, later = (step - 1) % 2, step % 2
        for i in range(2):
            put_layer(state, now, i, edge[step - 1, i])
        if step == 2:
            put_layer(state, now, 4, halo[2])
            put_layer(state, now, 5, halo[3])
        for j in range(2 if step == 1 else WIDE):
            c = DEPTH - step + j
            if c < DEPTH:
                coefs = own_coefs(odd, force, vel, upt, c)
            else:
                coefs = halo_coefs((near, near_rest), NEAR_COUNTS, c - DEPTH)

            def put(block, t, value, c=c, j=j, step=step, later=later):
                if c >= DEPTH:
                    value = value * alive
                if step == WIDE:
                    out[j, pl.ds(8 * block, 8), pl.ds(128 * t, 128)] = value
                if step < WIDE or not last:
                    state[later, 2 + j, t, pl.ds(8 + 8 * block, 8)] = value

            layer_step(state, now, 1 + j, coefs, sign, put)
    if not last:
        ahead[0] = out[WIDE - 1]
        ahead[1] = out[WIDE - 2]
        coefs = [own_coefs(odd, force, vel, upt, c) for c in (DEPTH - 2, DEPTH - 3)]
        put_stairs(state, coefs, sign, ahead, (WIDE, WIDE - 1))
    if last:
        put_tiles(summed, 0, (out[0] + out[1]) + (out[2] + out[3]))
        near_coarse = restrict_summed(summed)
        chip_coarse = coarse_chip[...]
        coarse[0] = jnp.where(odd == 1, chip_coarse, near_coarse)
        coarse[1] = jnp.where(odd == 1, near_coarse, chip_coarse)
        kept = jnp.where(where[1] == 1, 0.0, 1.0)
        part = coarse[...] - kept * stepped[pl.ds(2 * slab, 2)]
        for copy in range(begun.shape[0]):
            begun[copy] = part


def wedge(last, where, force, vel, upt, edge, halo, near, near_rest, more=(), copies=0):
    _, rows, cols = force.shape
    outs = (f32(WIDE, rows, cols),)
    if not last:
        outs += (f32(STAIRS, rows, cols),)
    scratch = [pltpu.VMEM((2, WIDE + 2, cols // 128, rows + 16, 128), jnp.float32)]
    if last:
        outs += (f32(copies, 2, rows // 4, cols // 4), f32(2, rows // 4, cols // 4))
        scratch.append(pltpu.VMEM((cols // 128, rows, 128), jnp.float32))
    return call(
        functools.partial(wedge_kernel, last),
        "wedge_last" if last else "wedge_first",
        outs,
        [SMEM] + [VMEM] * (7 + len(more)),
        (where, force, vel, upt, edge, halo, near, near_rest) + more,
        scratch,
    )


NEIGHBOURS = ((0, 0, 0), (1, 0, 0), (-1, 0, 0), (0, 1, 0), (0, -1, 0), (0, 0, 1), (0, 0, -1))
STENCIL = sorted({tuple(a + b for a, b in zip(p, q)) for p in NEIGHBOURS for q in NEIGHBOURS})


def shifted(field, offset):
    dz, dy, dx = offset
    if dz:
        field = jnp.concatenate([field[dz:], field[:dz]], axis=0)
    for axis, by in ((1, dy), (2, dx)):
        if by:
            size = field.shape[axis]
            field = pltpu.roll(field, (size - by) % size, axis)
    return field


def coarse_step(field, coef):
    depth = len(field)
    rows, cols = field[0].shape
    moved = {0: field}
    for dy in (-2, -1, 1, 2):
        moved[dy] = [pltpu.roll(c, (rows - dy) % rows, 0) for c in field]

    def part(dx, z):
        total = None
        for k, offset in enumerate(STENCIL):
            if offset[2] != dx or not 0 <= z + offset[0] < depth:
                continue
            term = coef[k, z] * moved[offset[1]][z + offset[0]]
            total = term if total is None else total + term
        return total

    sides = []
    for z in range(depth):
        sides.append([pltpu.roll(part(dx, z), (cols - dx) % cols, 1) for dx in (-2, 2, -1, 1)])
    return [part(0, z) + ((s[0] + s[1]) + (s[2] + s[3])) for z, s in enumerate(sides)]


def prepare_kernel(where, own, one, pair, coef, stepped, whole):
    slab = where[0]
    size = own.shape[0]
    depth = size // 5
    parts = (own, one, pair.at[pl.ds(0, size)], pair.at[pl.ds(size, size)])
    for flip, ref in enumerate(parts):
        first = lax.bitwise_xor(slab, flip) * depth
        for part in range(5):
            whole[part, pl.ds(first, depth)] = ref[pl.ds(part * depth, depth)]
    full = whole.shape[1:]
    half = {NEIGHBOURS[0]: (1.0 - 6.0 * DIFFUSION_COARSE) - 4.0 * whole[4]}
    for dim in range(3):
        v = whole[1 + dim]
        half[NEIGHBOURS[0]] -= jnp.abs(v)
        at = lax.broadcasted_iota(jnp.int32, full, dim)
        plus = DIFFUSION_COARSE + jnp.maximum(v, 0.0)
        minus = DIFFUSION_COARSE - jnp.minimum(v, 0.0)
        half[NEIGHBOURS[1 + 2 * dim]] = jnp.where(at == full[dim] - 1, 0.0, plus)
        half[NEIGHBOURS[2 + 2 * dim]] = jnp.where(at == 0, 0.0, minus)
    both = {}
    for p in NEIGHBOURS:
        for q in NEIGHBOURS:
            offset = tuple(a + b for a, b in zip(p, q))
            term = half[p] * shifted(half[q], p)
            both[offset] = both[offset] + term if offset in both else term
    for k, offset in enumerate(STENCIL):
        coef[k] = shifted(both[offset], (0, 0, -offset[2]))
    field = coarse_step([whole[0, z] for z in range(full[0])], coef)
    for z in range(full[0]):
        stepped[z] = field[z]


def prepare(where, parts):
    depth5, rows, cols = parts[0].shape
    full = (4 * depth5 // 5, rows, cols)
    return call(
        prepare_kernel,
        "prepare",
        (f32(len(STENCIL), *full), f32(*full)),
        [SMEM] + [VMEM] * 3,
        (where, *parts),
        [pltpu.VMEM((5,) + full, jnp.float32)],
    )


def outer_kernel(where, coef, own, other, out, whole, ends):
    slab, group, place = where[0], where[2], where[3]
    core = lax.rem(slab, 2)
    targets, half = out.shape[:2]
    count, depth = whole.shape[:2]
    chips = own.shape[0] // count
    part = own.shape[1]
    for g in range(count):
        for chip in range(chips):
            here = 2 * chip + core
            there = 2 * chip + 1 - core
            whole[g, pl.ds(here * part, part)] = own[g * chips + chip]
            whole[g, pl.ds(there * part, part)] = other[g * chips + chip]

    def keep(which, layers):
        for z in range(depth):
            ends[which, z] = layers[z]

    def body(i, layers):
        keep(1, layers)
        layers = list(layers)
        for _ in range(targets):
            layers = coarse_step(layers, coef)
        return tuple(layers[z] + whole[count - 2 - i, z] for z in range(depth))

    ends[1] = jnp.zeros(ends.shape[1:], jnp.float32)
    field = tuple(whole[count - 1, z] for z in range(depth))
    keep(0, lax.fori_loop(0, count - 1 - group, body, field))
    for target in range(targets):
        out[target] = ends[jnp.where(place >= target, 0, 1), pl.ds(core * half, half)]


def outer(targets, where, coef, own, other):
    full = coef.shape[1:]
    depth, rows, cols = full
    count = own.shape[0] * own.shape[1] * 2 // depth
    return call(
        outer_kernel,
        "outer",
        f32(targets, depth // 2, rows, cols),
        [SMEM] + [VMEM] * 3,
        (where, coef, own, other),
        [pltpu.VMEM((count,) + full, jnp.float32), pltpu.VMEM((2,) + full, jnp.float32)],
    )


def finish_kernel(where, coef, own, other, coarse, chip_part, near_part, *refs):
    corrected, coarse_new, whole, down = refs
    slab, place = where[0], where[3]
    odd = lax.rem(slab, 2)
    count, depth = whole.shape[:2]
    half = depth // 2
    for t in range(count):
        whole[t, pl.ds(odd * half, half)] = own[t]
        whole[t, pl.ds((1 - odd) * half, half)] = other[t]

    def term(j):
        return whole.at[lax.rem(place + j, count)]

    def body(i, layers):
        stepped = coarse_step(list(layers), coef)
        added = term(count - 2 - i)
        return tuple(stepped[z] + added[z] for z in range(depth))

    first = term(count - 1)
    field = tuple(first[z] for z in range(depth))
    for i in range(count - 1):
        field = body(i, field)
    for z in range(depth):
        coarse_new[z] = field[z]
    rows, cols = chip_part.shape[1:]
    part = (coarse_new[pl.ds(2 * slab, 2)] - coarse[...]).reshape(rows // 2, cols // 4)
    for row in range(rows // 2):
        down[pl.ds(4 * row, 4)] = jnp.broadcast_to(part[row : row + 1], (4, cols // 4))
    fine = jnp.dot(down[...], groups_of_four(cols // 4, cols, 1.0), precision=HIGH)
    lower, upper = fine[:rows], fine[rows:]
    chip_fine = jnp.where(odd == 1, lower, upper)
    near_fine = jnp.where(odd == 1, upper, lower)
    for c in range(DEPTH):
        z = jnp.where(odd == 1, c, DEPTH - 1 - c)
        corrected[z] = chip_part[c] + chip_fine if c < WIDE else near_part[c - WIDE] + near_fine


def finish(where, *args):
    _, rows, cols = args[-1].shape
    full = args[0].shape[1:]
    return call(
        finish_kernel,
        "finish",
        (f32(DEPTH, rows, cols), f32(*full)),
        [SMEM] + [VMEM] * len(args),
        (where, *args),
        [
            pltpu.VMEM(args[1].shape[:1] + full, jnp.float32),
            pltpu.VMEM((2 * rows, cols // 4), jnp.float32),
        ],
    )


def per_device(adjoint_end, forcing, velocity, uptake):
    adj, force = adjoint_end[0], forcing[0]
    groups, places, chips, cores = (lax.axis_size(axis) for axis in AXES)
    group, place, chip_no, core = (lax.axis_index(axis) for axis in AXES)
    times, slabs = groups * places, chips * cores
    slab = chip_no * cores + core
    last_slice = jnp.logical_and(group == groups - 1, place == places - 1)
    where = jnp.stack([slab, last_slice.astype(slab.dtype), group, place]).astype(jnp.int32)

    def send(array, pairs):
        route = [(t0 * slabs + s0, t1 * slabs + s1) for (t0, s0), (t1, s1) in pairs]
        return lax.ppermute(array, AXES, route)

    def flipped(array, flip):
        return send(array, [((t, s ^ flip), (t, s)) for t in range(times) for s in range(slabs)])

    def to_next_chip(array, shift=0):
        pairs = [(1, 2), (2, 1)]
        return send(
            array, [((t, a), ((t + shift) % times, b)) for t in range(times) for a, b in pairs]
        )

    own = (force, velocity, uptake)
    near_pack, rest_pack = pack(False, where, adj, *own)
    near = to_next_chip(near_pack)
    near_rest = to_next_chip(rest_pack, times // 2)
    restricted = restrict_inputs(adj, velocity, uptake)
    chip = [flipped(array, 1) for array in pack(True, where, adj, *own)]
    restricted_one = flipped(restricted, 1)
    pair = flipped(jnp.concatenate([restricted, restricted_one]), 2)
    edge, chip_part, ahead = inner(False, where, *own, (adj,), chip[0], chip)
    chip_halo = flipped(ahead, 1)
    near, near_rest, pair, edge = lax.optimization_barrier((near, near_rest, pair, edge))
    near_part, ahead = wedge(False, where, *own, edge, near, near, near_rest)
    near_halo = to_next_chip(ahead)
    edge, chip_part, coarse_chip = inner(True, where, *own, (chip_part, near_part), chip_halo, chip)
    coef, stepped = prepare(where, (restricted, restricted_one, pair))
    near_halo, edge, coef, stepped = lax.optimization_barrier((near_halo, edge, coef, stepped))
    near_part, begun, coarse = wedge(
        True, where, *own, edge, near_halo, near, near_rest, (coarse_chip, stepped), groups * chips
    )

    begun = lax.all_to_all(begun, ("group", "chip"), 0, 0)
    terms = outer(places, where, coef, begun, flipped(begun, 1))
    terms = lax.all_to_all(terms, "place", 0, 0)
    corrected, coarse_new = finish(
        where, coef, terms, flipped(terms, 1), coarse, chip_part, near_part
    )
    return corrected[None], coarse_new[None]


def solution(mesh):
    times, slabs = mesh.devices.shape
    places = 8 if times >= 16 else 2
    shape = (times // places, places, slabs // 2, 2)
    time, slab = AXES[:2], AXES[2:]
    return jax.shard_map(
        per_device,
        mesh=Mesh(mesh.devices.reshape(shape), AXES),
        in_specs=(P(time, slab), P(time, slab), P(None, slab), P(slab)),
        out_specs=(P(time, slab), P(time)),
        check_vma=False,
    )
```
